32 devices in a mesh: ctx: 8 (over z, core), ch: 4 (over y, x).
Axes of the slice: x: 2, y: 2, z: 4, core: 2. Of those that a mesh axis runs over, the one named last changes fastest.
Arguments:
- query_in: bfloat16 [2048, 4096], P('ctx', 'ch'), may hold values from -63 to 63
- key_in: bfloat16 [2048, 4096], P('ctx', 'ch'), may hold values from -4 to 4
- value_in: bfloat16 [2048, 4096], P('ctx', 'ch'), may hold values from -4 to 4
- short_taps: float32 [7, 3, 4096], P(None, None, 'ch'), may hold values from -2 to 2
- residues: float32 [4096, 16], P('ch'), may hold values from -1.5 to 1.5
- decays: float32 [4096, 16], P('ch'), may hold values from 2.4414063e-05 to 0.02
- out_weight: bfloat16 [4096, 4096], P('ch'), may hold values from -0.125 to 0.125
- out_grad: bfloat16 [2048, 4096], P('ctx', 'ch'), may hold values from -6 to 6
Outputs:
- projected: bfloat16 [2048, 4096], P('ctx', 'ch')
- grad_query: bfloat16 [2048, 4096], P('ctx', 'ch')
- grad_key: bfloat16 [2048, 4096], P('ctx', 'ch')
- grad_value: bfloat16 [2048, 4096], P('ctx', 'ch')
The draws below stay inside these ranges and needn't reach their ends.
All inputs are finite; a program needn't handle non-finite values.
Results may differ from the reference program's by a relative error of at most 0.0058.
Values may be sent and summed in bfloat16 or wider, within the bound.
No kernel may reach another device: no remote copies, remote signals or barrier semaphores. Data moves between devices by JAX's collectives and lax.ppermute only.
A program may use at most 128 MiB of HBM per device.

```python
import math
import jax
import jax.numpy as jnp
import numpy as np
from jax import lax

D = 4096
MODES = 16
KERNEL = 7
SEQ = 2048


def offset_field(key, salt):
    base_key = jax.random.fold_in(key, salt)
    values = jnp.clip(jax.random.normal(base_key, (SEQ, D), jnp.float32), -4.0, 4.0)
    return values.astype(jnp.bfloat16)


def draw_query_in(key, part):
    streams = jax.random.split(jax.random.fold_in(key, 11), 3)
    base_vals = jnp.clip(jax.random.normal(streams[0], (SEQ, D), jnp.float32), -4.0, 4.0)
    trend_span = 3.0
    position = jnp.arange(D, dtype=jnp.float32) / D - 0.5
    column_scale = jnp.exp(jax.random.uniform(streams[1], (D,), jnp.float32, math.log(0.3), math.log(3.0)))
    column_scale = column_scale * jnp.exp(math.log(trend_span) * position)
    row_scale = jnp.exp(jax.random.uniform(streams[2], (SEQ, 1), jnp.float32, math.log(0.3), math.log(3.0)))
    return (base_vals * column_scale * row_scale).astype(jnp.bfloat16)


def draw_key_in(key, part):
    return offset_field(key, 23)


def draw_value_in(key, part):
    return offset_field(key, 37)


def with_spikes(entries, own_key, source, target, blocks, factor):
    owner, partner = [(jnp.arange(entries.shape[dim]) // (entries.shape[dim] // blocks)).reshape([-1 if axis == dim else 1 for axis in range(entries.ndim)]) for dim in (source, target)]
    chosen = jax.random.permutation(own_key, blocks)[partner]
    strong = (owner == chosen) | (owner == (partner + blocks // 2) % blocks)
    return jnp.where(strong, factor * entries, entries)


def level_of(rng, extent, cuts, smallest, top_value):
    loudness = 1.0
    for dim, parts in cuts:
        draws = jax.random.uniform(jax.random.fold_in(jax.random.fold_in(rng, 6), dim), (parts,), jnp.float32, smallest / len(cuts), top_value / len(cuts))
        loudness = loudness * jnp.repeat(jnp.exp(draws), extent[dim] // parts).reshape((-1,) + (1,) * (len(extent) - 1 - dim))
    return loudness


def normal_values(own_key, extent, deviation, limit, cuts=(), kind=jnp.bfloat16):
    array = deviation * jax.random.normal(own_key, extent, jnp.float32)
    if cuts:
        array = array * level_of(own_key, extent, cuts, -0.22, 0.18)
    return jnp.clip(array, -limit, limit).astype(kind)


def gaussian_with(key, dims, width, most, cuts, heavy, kind=jnp.bfloat16):
    entries = width * jax.random.normal(key, dims, jnp.float32)
    if cuts:
        entries = entries * level_of(key, dims, cuts, -0.22, 0.18)
    return jnp.clip(with_spikes(entries, jax.random.fold_in(key, 3), *heavy), -most, most).astype(kind)


def setup_inputs(seed: int = 0) -> dict:
    keys = jax.random.split(jax.random.key(seed), 9)
    query_in = draw_query_in(jax.random.fold_in(keys[8], 71), 0)
    key_in = draw_key_in(jax.random.fold_in(keys[8], 71), 0)
    value_in = draw_value_in(jax.random.fold_in(keys[8], 71), 0)
    short_taps = normal_values(keys[3], (KERNEL, 3, D), KERNEL ** -0.5, 2.0, ((2, 4),), jnp.float32)
    residues = normal_values(keys[4], (D, MODES), MODES ** -0.5, 1.5, ((0, 4),), jnp.float32)
    decays = jnp.clip(jnp.exp(math.log(0.02) - 6.7083282 * jax.random.uniform(keys[5], (D, MODES), jnp.float32) ** level_of(keys[5], (D, MODES), ((0, 4),), -0.2, 0.2)), 2.441406286379788e-05, 0.02)
    out_weight = gaussian_with(keys[6], (D, D), D ** -0.5, 0.125, ((0, 4),), (0, 1, 4, 2.0))
    out_grad = normal_values(keys[7], (SEQ, D), 1.0, 6.0, ((0, 8), (1, 4)))
    return {"query_in": query_in, "key_in": key_in, "value_in": value_in, "short_taps": short_taps, "residues": residues, "decays": decays, "out_weight": out_weight, "out_grad": out_grad}


block_len = 64
exact_precision = lax.Precision.HIGHEST

def featurize(signal, taps):
    kernel_len = taps.shape[0]
    length = signal.shape[0]
    padded = jnp.pad(signal, ((kernel_len - 1, 0), (0, 0)))
    final_output = jnp.zeros_like(signal)
    for tap_index in range(kernel_len):
        begin = kernel_len - 1 - tap_index
        final_output = final_output + taps[tap_index] * padded[begin:begin + length]
    return final_output

def featurize_back(grads_in, taps):
    kernel_len = taps.shape[0]
    length = grads_in.shape[0]
    padded = jnp.pad(grads_in, ((0, kernel_len - 1), (0, 0)))
    final_output = jnp.zeros_like(grads_in)
    for tap_index in range(kernel_len):
        final_output = final_output + taps[tap_index] * padded[tap_index:tap_index + length]
    return final_output

def modal_conv(signal, residues, decays):
    channels, length = signal.shape
    pieces = length // block_len
    offsets = jnp.arange(block_len, dtype=jnp.float32)
    scaled = residues * jnp.sqrt(decays)
    filter_head = jnp.einsum('cn,cnd->cd', scaled, jnp.exp(-decays[:, :, None] * offsets), precision=exact_precision)
    indices = np.arange(block_len)
    distance = indices[:, None] - indices[None, :]
    toeplitz = jnp.where(jnp.asarray(distance >= 0)[None], filter_head[:, np.maximum(distance, 0)], 0.0)
    decay_in = jnp.exp(-decays[:, :, None] * (block_len - 1.0 - offsets))
    decay_out = scaled[:, :, None] * jnp.exp(-decays[:, :, None] * (offsets + 1.0))
    step_decay = jnp.exp(-decays * block_len)
    block_list = jnp.transpose(signal.reshape(channels, pieces, block_len), (1, 0, 2))

    def advance(carried_state, segment):
        produced = jnp.einsum('cij,cj->ci', toeplitz, segment, precision=exact_precision)
        produced = produced + jnp.einsum('cn,cni->ci', carried_state, decay_out, precision=exact_precision)
        carried_state = carried_state * step_decay + jnp.einsum('cj,cnj->cn', segment, decay_in, precision=exact_precision)
        return (carried_state, produced)
    _, outputs = lax.scan(advance, jnp.zeros(decays.shape, jnp.float32), block_list)
    return jnp.transpose(outputs, (1, 0, 2)).reshape(channels, length)

def reference(query_in, key_in, value_in, short_taps, residues, decays, out_weight, out_grad):
    query_feat = featurize(query_in.astype(jnp.float32), short_taps[:, 0])
    key_feat = featurize(key_in.astype(jnp.float32), short_taps[:, 1])
    value_feat = featurize(value_in.astype(jnp.float32), short_taps[:, 2])
    mixed_values = (key_feat * value_feat).astype(jnp.bfloat16)
    mixed_wide = lax.optimization_barrier(mixed_values).astype(jnp.float32)
    conv_out = modal_conv(mixed_wide.T, residues, decays).T
    gated = (query_feat * conv_out).astype(jnp.bfloat16)
    projected = jnp.dot(gated, out_weight, preferred_element_type=jnp.float32).astype(jnp.bfloat16)
    grad_gated = jnp.dot(out_grad, out_weight.T, preferred_element_type=jnp.float32)
    grad_query_feat = (grad_gated * conv_out).astype(jnp.bfloat16)
    grad_mixed = (grad_gated * query_feat).astype(jnp.bfloat16)
    grad_wide = lax.optimization_barrier(grad_mixed).astype(jnp.float32)
    grad_conv = jnp.flip(modal_conv(jnp.flip(grad_wide.T, 1), residues, decays), 1).T
    grad_key_feat = (grad_conv * value_feat).astype(jnp.bfloat16)
    grad_value_feat = (grad_conv * key_feat).astype(jnp.bfloat16)
    grad_query = featurize_back(grad_query_feat.astype(jnp.float32), short_taps[:, 0]).astype(jnp.bfloat16)
    grad_key = featurize_back(grad_key_feat.astype(jnp.float32), short_taps[:, 1]).astype(jnp.bfloat16)
    grad_value = featurize_back(grad_value_feat.astype(jnp.float32), short_taps[:, 2]).astype(jnp.bfloat16)
    return (projected, grad_query, grad_key, grad_value)
```

```python
import functools

import jax
import jax.numpy as jnp
from jax import lax
from jax.experimental import pallas as pl
from jax.experimental.pallas import tpu as pltpu
from jax.sharding import PartitionSpec as P

SUB = 8
LANES = 128
STEP = 8
F32 = jnp.float32
BF16 = jnp.bfloat16
VMEM_LIMIT = 48 * 1024 * 1024


def as_tiles(rows):
    return rows.reshape(rows.shape[0] // SUB, SUB, LANES)


def as_rows(tiles):
    return tiles.reshape(tiles.shape[0] * SUB, LANES)


def tile(ref, token):
    return ref[pl.ds(pl.multiple_of(token * SUB, SUB), SUB), :]


def tree_sum(terms):
    while len(terms) > 1:
        terms = [
            terms[i] + terms[i + 1] if i + 1 < len(terms) else terms[i]
            for i in range(0, len(terms), 2)
        ]
    return terms[0]


def round16(value):
    return value.astype(BF16).astype(F32)


def scatter_tokens(ref, value, first_token):
    tokens, channels = value.shape
    for group in range(channels // LANES):
        ref[pl.ds(first_token * SUB + group, tokens, stride=SUB), :] = value[
            :, group * LANES : (group + 1) * LANES
        ]


def gather_tokens(ref, out_ref):
    tokens, channels = out_ref.shape
    for group in range(channels // LANES):
        out_ref[:, group * LANES : (group + 1) * LANES] = ref[
            pl.ds(group, tokens, stride=SUB), :
        ].astype(out_ref.dtype)


def end_state(signal_ref, decay_ref, state_ref, reverse):
    modes = decay_ref.shape[0]
    tokens = signal_ref.shape[0] // SUB
    factors = [jnp.exp(-decay_ref[n]) for n in range(modes)]

    def body(step, states):
        for inner in range(STEP):
            token = step * STEP + inner
            u = tile(signal_ref, tokens - 1 - token if reverse else token)
            states = [factors[n] * states[n] + u for n in range(modes)]
        return states

    zeros = [jnp.zeros((SUB, LANES), F32) for _ in range(modes)]
    states = lax.fori_loop(0, tokens // STEP, body, zeros)
    for n in range(modes):
        state_ref[n] = states[n]


def featurize_kernel(
    q_ref, k_ref, v_ref, halo_ref, taps_ref, decay_ref,
    qf_ref, kf_ref, vf_ref, mixed_ref, state_ref, wide_ref,
):
    tokens = q_ref.shape[0]
    taps = taps_ref.shape[0]
    rim = taps - 1
    halo = halo_ref[...].astype(F32)
    for stream, source in enumerate((q_ref, k_ref, v_ref)):
        wide = wide_ref.at[stream]
        scatter_tokens(wide, halo[stream * rim : (stream + 1) * rim], 0)
        scatter_tokens(wide, source[...].astype(F32), rim)

    def body(step, carry):
        first = pl.multiple_of(step * STEP * SUB, SUB)
        feats = []
        for stream, feat_ref in enumerate((qf_ref, kf_ref, vf_ref)):
            window = as_tiles(wide_ref[stream, pl.ds(first, (STEP + rim) * SUB), :])
            total = taps_ref[0, stream] * window[rim : rim + STEP]
            for tap in range(1, taps):
                total = total + taps_ref[tap, stream] * window[rim - tap : rim - tap + STEP]
            feat_ref[pl.ds(first, STEP * SUB), :] = as_rows(total)
            feats.append(total)
        mixed_ref[pl.ds(first, STEP * SUB), :] = as_rows(round16(feats[1] * feats[2]))
        return carry

    lax.fori_loop(0, tokens // STEP, body, 0)
    end_state(mixed_ref, decay_ref, state_ref, False)


def local_conv_kernel(signal_ref, decay_ref, scale_ref, out_ref, *, reverse):
    modes = decay_ref.shape[0]
    tokens = signal_ref.shape[0] // SUB
    factors = [jnp.exp(-decay_ref[n]) for n in range(modes)]
    scales = [scale_ref[n] for n in range(modes)]

    def body(step, states):
        for inner in range(STEP):
            token = step * STEP + inner
            token = tokens - 1 - token if reverse else token
            u = tile(signal_ref, token)
            states = [factors[n] * states[n] + u for n in range(modes)]
            out_ref[pl.ds(pl.multiple_of(token * SUB, SUB), SUB), :] = tree_sum(
                [scales[n] * states[n] for n in range(modes)]
            )
        return states

    zeros = [jnp.zeros((SUB, LANES), F32) for _ in range(modes)]
    lax.fori_loop(0, tokens // STEP, body, zeros)


def carried_states(message_refs, decay_ref, powers):
    states = []
    for n in range(decay_ref.shape[0]):
        terms = [
            ref[n] if power == 0 else ref[n] * jnp.exp(-decay_ref[n] * float(power))
            for ref, power in zip(message_refs, powers)
        ]
        states.append(tree_sum(terms))
    return states


def add_carried(local_ref, out_ref, states, decay_ref, scale_ref, reverse):
    modes = decay_ref.shape[0]
    tokens = local_ref.shape[0] // SUB
    factors = [jnp.exp(-decay_ref[n]) for n in range(modes)]
    scaled = [scale_ref[n] * states[n] for n in range(modes)]

    def body(step, scaled):
        for inner in range(STEP):
            token = step * STEP + inner
            token = tokens - 1 - token if reverse else token
            scaled = [factors[n] * scaled[n] for n in range(modes)]
            rows = pl.ds(pl.multiple_of(token * SUB, SUB), SUB)
            out_ref[rows, :] = local_ref[rows, :] + tree_sum(list(scaled))
        return scaled

    lax.fori_loop(0, tokens // STEP, body, scaled)


def project_kernel(*refs, powers, order):
    count = len(powers)
    messages = refs[:count]
    (
        local_ref, decay_ref, scale_ref, qf_ref, weight_ref,
        conv_ref, out_ref, rows_ref, gated_ref, held_ref, sems,
    ) = refs[count:]
    parts, _, width = out_ref.shape
    copies = [
        pltpu.make_async_copy(
            weight_ref.at[:, pl.ds(part * width, width)], held_ref.at[part], sems.at[part]
        )
        for part in range(parts)
    ]
    for part in order:
        copies[part].start()
    states = carried_states(messages, decay_ref, powers)
    add_carried(local_ref, conv_ref, states, decay_ref, scale_ref, False)
    rows_ref[...] = qf_ref[...] * conv_ref[...]
    gather_tokens(rows_ref, gated_ref)
    block = min(width, 256)
    for part in order:
        copies[part].wait()

        def body(step, carry):
            columns = pl.ds(pl.multiple_of(step * block, block), block)
            out_ref[part, :, columns] = jnp.dot(
                gated_ref[...], held_ref[part, :, columns], preferred_element_type=F32
            ).astype(out_ref.dtype)
            return carry

        lax.fori_loop(0, width // block, body, 0)


def back_products(index_ref, piece_refs, weight_ref, held_ref, sems, total_ref, base_ref):
    channels = total_ref.shape[1]
    copies, parts = [], []
    for ref in piece_refs:
        for inner in range(ref.shape[0]):
            parts.append((ref, inner))
    width = piece_refs[0].shape[2]
    for number in range(len(parts)):
        first = pl.multiple_of(index_ref[number] * width, width)
        copies.append(
            pltpu.make_async_copy(
                weight_ref.at[:, pl.ds(first, width)], held_ref.at[number], sems.at[number]
            )
        )
    for copy in copies:
        copy.start()
    block = min(channels, 256)
    for number, (ref, inner) in enumerate(parts):
        copies[number].wait()

        def body(step, carry):
            columns = pl.ds(pl.multiple_of(step * block, block), block)
            product = lax.dot_general(
                ref[inner], held_ref[number, columns, :],
                (((1,), (1,)), ((), ())), preferred_element_type=F32,
            )
            before = base_ref if number == 0 else total_ref
            total_ref[:, columns] = product if before is None else before[:, columns] + product
            return carry

        lax.fori_loop(0, channels // block, body, 0)


def back_part_kernel(*refs):
    index_ref, *pieces, weight_ref, total_ref, held_ref, sems = refs
    back_products(index_ref, pieces, weight_ref, held_ref, sems, total_ref, None)


def back_last_kernel(*refs, has_base):
    index_ref, *rest = refs
    (
        weight_ref, qf_ref, decay_ref,
        grad_ref, mixed_ref, state_ref, total_ref, held_ref, sems,
    ) = rest[-9:]
    pieces = rest[:-9]
    base_ref = None
    if has_base:
        base_ref, *pieces = pieces
    back_products(index_ref, pieces, weight_ref, held_ref, sems, total_ref, base_ref)
    scatter_tokens(grad_ref, total_ref[...], 0)
    mixed_ref[...] = round16(grad_ref[...] * qf_ref[...])
    end_state(mixed_ref, decay_ref, state_ref, True)


def finish_kernel(*refs, powers):
    count = len(powers)
    messages = refs[:count]
    (
        local_ref, decay_ref, scale_ref, kf_ref, vf_ref, grad_ref, conv_ref, halo_ref, taps_ref,
        gq_ref, gk_ref, gv_ref, total_ref, wide_ref, rows_ref,
    ) = refs[count:]
    modes = decay_ref.shape[0]
    taps = taps_ref.shape[0]
    rim = taps - 1
    tokens = gq_ref.shape[0]
    states = carried_states(messages, decay_ref, powers)
    add_carried(local_ref, total_ref, states, decay_ref, scale_ref, True)

    def body(step, carry):
        rows = pl.ds(pl.multiple_of(step * STEP * SUB, SUB), STEP * SUB)
        wide_ref[0, rows, :] = round16(grad_ref[rows, :] * conv_ref[rows, :])
        wide_ref[1, rows, :] = round16(total_ref[rows, :] * vf_ref[rows, :])
        wide_ref[2, rows, :] = round16(total_ref[rows, :] * kf_ref[rows, :])
        return carry

    lax.fori_loop(0, tokens // STEP, body, 0)
    growth = [jnp.exp(decay_ref[n]) for n in range(modes)]
    for ahead in range(rim):
        rows = pl.ds((tokens + ahead) * SUB, SUB)
        grad_conv = tree_sum([scale_ref[n] * states[n] for n in range(modes)])
        wide_ref[0, rows, :] = halo_ref[0, pl.ds(ahead * SUB, SUB), :]
        wide_ref[1, rows, :] = round16(grad_conv * halo_ref[3, pl.ds(ahead * SUB, SUB), :])
        wide_ref[2, rows, :] = round16(grad_conv * halo_ref[2, pl.ds(ahead * SUB, SUB), :])
        arrived = halo_ref[1, pl.ds(ahead * SUB, SUB), :]
        states = [(states[n] - arrived) * growth[n] for n in range(modes)]

    def spread(step, carry):
        first = pl.multiple_of(step * STEP * SUB, SUB)
        for stream in range(3):
            window = as_tiles(wide_ref[stream, pl.ds(first, (STEP + rim) * SUB), :])
            total = taps_ref[0, stream] * window[:STEP]
            for tap in range(1, taps):
                total = total + taps_ref[tap, stream] * window[tap : tap + STEP]
            rows_ref[stream, pl.ds(first, STEP * SUB), :] = as_rows(total)
        return carry

    lax.fori_loop(0, tokens // STEP, spread, 0)
    for stream, out_ref in enumerate((gq_ref, gk_ref, gv_ref)):
        gather_tokens(rows_ref.at[stream], out_ref)


IN_VMEM = pl.BlockSpec(memory_space=pltpu.VMEM)
IN_SMEM = pl.BlockSpec(memory_space=pltpu.SMEM)
ANYWHERE = pl.BlockSpec(memory_space=pl.ANY)


def call(kernel, outs, args, specs, scratch, name, flops, moved):
    return pl.pallas_call(
        kernel,
        out_shape=[jax.ShapeDtypeStruct(shape, kind) for shape, kind in outs],
        in_specs=specs,
        out_specs=[IN_VMEM] * len(outs),
        scratch_shapes=scratch,
        compiler_params=pltpu.CompilerParams(vmem_limit_bytes=VMEM_LIMIT),
        cost_estimate=pl.CostEstimate(flops=flops, bytes_accessed=moved, transcendentals=0),
        name=name,
    )(*args)


def shift(value, axis, steps):
    count = lax.axis_size(axis)
    pairs = [(s, s + steps) for s in range(count) if 0 <= s + steps < count]
    return lax.ppermute(value, axis, pairs)


def exchange(value, axis, mask):
    count = lax.axis_size(axis)
    return lax.ppermute(value, axis, [(s, s ^ mask) for s in range(count)])


def windowed(state, decays, tokens, direction, radix):
    count = lax.axis_size("ctx")
    window = 1
    while window * radix < count - 1 and window < radix:
        terms = [state]
        for step in range(1, radix):
            faded = jnp.exp(-decays * float(tokens * window * step))
            terms.append(faded * shift(state, "ctx", direction * window * step))
        state = tree_sum(terms)
        window *= radix
    messages, powers = [], []
    offset = 0
    while 1 + offset < count:
        messages.append(shift(state, "ctx", direction * (1 + offset)))
        powers.append(offset * tokens)
        offset += window
    return messages, powers


def gathered_state(state, decays, tokens, direction):
    count = lax.axis_size("ctx")
    everyone = lax.all_gather(state, "ctx", axis=0, tiled=False)
    gap = direction * (lax.axis_index("ctx") - jnp.arange(count)) - 1
    gap = gap[:, None, None, None]
    faded = jnp.exp(-decays[None] * (jnp.maximum(gap, 0) * tokens).astype(F32))
    return [jnp.sum(jnp.where(gap >= 0, faded * everyone, 0.0), axis=0)], [0]


def tiled_channels(value):
    groups = value.shape[-1] // LANES
    value = value.reshape(value.shape[:-1] + (groups, LANES))
    return jnp.pad(value, [(0, 0)] * (value.ndim - 2) + [(0, SUB - groups), (0, 0)])


def shards(query_in, key_in, value_in, short_taps, residues, decays, out_weight, out_grad):
    tokens, channels = query_in.shape
    taps = short_taps.shape[0]
    rim = taps - 1
    modes = decays.shape[1]
    fans = lax.axis_size("ch")
    mine = lax.axis_index("ch")
    rows = tokens * SUB
    size = rows * LANES * 4
    matmul = 2 * tokens * channels * channels
    tile_shape = (rows, LANES)
    state_shape = (modes, SUB, LANES)

    halo = jnp.concatenate([x[tokens - rim :] for x in (query_in, key_in, value_in)], axis=0)
    halo = shift(halo, "ctx", 1)
    tap_tiles = tiled_channels(short_taps)
    scale_tiles = tiled_channels((residues * jnp.sqrt(decays)).T)
    decay_tiles = tiled_channels(decays.T)

    query_feat, key_feat, value_feat, mixed, state = call(
        featurize_kernel,
        [(tile_shape, F32)] * 4 + [(state_shape, F32)],
        (query_in, key_in, value_in, halo, tap_tiles, decay_tiles),
        [IN_VMEM] * 6,
        [pltpu.VMEM((3, (tokens + rim) * SUB, LANES), F32)],
        "featurize", 20 * size, 5 * size,
    )
    messages, powers = windowed(state, decay_tiles, tokens, 1, 3)
    (local,) = call(
        functools.partial(local_conv_kernel, reverse=False),
        [(tile_shape, F32)], (mixed, decay_tiles, scale_tiles), [IN_VMEM] * 3, [],
        "local_conv", 16 * size, 2 * size,
    )
    conv_out, partial_sums = call(
        functools.partial(project_kernel, powers=tuple(powers), order=tuple(range(fans))),
        [(tile_shape, F32), ((fans, tokens, channels), BF16)],
        (*messages, local, decay_tiles, scale_tiles, query_feat, out_weight),
        [IN_VMEM] * (len(messages) + 4) + [ANYWHERE],
        [
            pltpu.VMEM(tile_shape, F32),
            pltpu.VMEM((tokens, channels), BF16),
            pltpu.VMEM((fans, channels, channels), BF16),
            pltpu.SemaphoreType.DMA((fans,)),
        ],
        "project", fans * matmul, fans * channels * channels * 2,
    )
    arrived = lax.all_to_all(partial_sums, "ch", split_axis=0, concat_axis=0, tiled=True)
    projected = jnp.sum(arrived.astype(F32), axis=0).astype(BF16)

    def scratch_for(count):
        return [
            pltpu.VMEM((count, channels, channels), BF16),
            pltpu.SemaphoreType.DMA((count,)),
        ]

    own = out_grad[None]
    if fans == 4:
        near = exchange(own, "ch", 1)
        far = exchange(own, "ch", 2)
        half = tokens // 2
        top = exchange(far[:, :half], "ch", 1)
        bottom = exchange(near[:, half:], "ch", 2)
        across = jnp.concatenate([top, bottom], axis=1)
        first_index = jnp.stack([mine, mine ^ 1, mine ^ 2]).astype(jnp.int32)
        (base,) = call(
            back_part_kernel,
            [((tokens, channels), F32)],
            (first_index, own, near, far, out_weight),
            [IN_SMEM] + [IN_VMEM] * 3 + [ANYWHERE],
            scratch_for(3), "back_part", 3 * matmul, 3 * channels * channels * 2,
        )
        pieces, bases, count = [across], [base], 1
        last_index = (mine ^ 3)[None].astype(jnp.int32)
    else:
        pieces, bases, count = [lax.all_gather(out_grad, "ch", axis=0, tiled=False)], [], fans
        last_index = jnp.arange(fans, dtype=jnp.int32)
    grad_gated, grad_mixed, back_state = call(
        functools.partial(back_last_kernel, has_base=bool(bases)),
        [(tile_shape, F32), (tile_shape, F32), (state_shape, F32)],
        (last_index, *bases, *pieces, out_weight, query_feat, decay_tiles),
        [IN_SMEM] + [IN_VMEM] * (len(bases) + len(pieces)) + [ANYWHERE] + [IN_VMEM] * 2,
        [pltpu.VMEM((tokens, channels), F32)] + scratch_for(count),
        "back_last", count * matmul, 4 * size,
    )
    back_messages, back_powers = gathered_state(back_state, decay_tiles, tokens, -1)
    (back_local,) = call(
        functools.partial(local_conv_kernel, reverse=True),
        [(tile_shape, F32)], (grad_mixed, decay_tiles, scale_tiles), [IN_VMEM] * 3, [],
        "back_local_conv", 16 * size, 2 * size,
    )
    head = slice(0, rim * SUB)
    grad_query_head = (grad_gated[head] * conv_out[head]).astype(BF16).astype(F32)
    ahead = shift(
        jnp.stack([grad_query_head, grad_mixed[head], key_feat[head], value_feat[head]]), "ctx", -1
    )
    grad_query, grad_key, grad_value = call(
        functools.partial(finish_kernel, powers=tuple(back_powers)),
        [((tokens, channels), BF16)] * 3,
        (
            *back_messages, back_local, decay_tiles, scale_tiles, key_feat, value_feat,
            grad_gated, conv_out, ahead, tap_tiles,
        ),
        [IN_VMEM] * (len(back_messages) + 9),
        [
            pltpu.VMEM(tile_shape, F32),
            pltpu.VMEM((3, (tokens + rim) * SUB, LANES), F32),
            pltpu.VMEM((3,) + tile_shape, F32),
        ],
        "finish", 20 * size, 8 * size,
    )
    return (projected, grad_query, grad_key, grad_value)


def solution(mesh):
    in_specs = (
        P("ctx", "ch"),
        P("ctx", "ch"),
        P("ctx", "ch"),
        P(None, None, "ch"),
        P("ch", None),
        P("ch", None),
        P("ch", None),
        P("ctx", "ch"),
    )
    out_specs = (P("ctx", "ch"), P("ctx", "ch"), P("ctx", "ch"), P("ctx", "ch"))
    return jax.shard_map(shards, mesh=mesh, in_specs=in_specs, out_specs=out_specs, check_vma=False)
```

```python
import functools

import jax
import jax.numpy as jnp
from jax import lax
from jax.experimental import pallas as pl
from jax.experimental.pallas import tpu as pltpu
from jax.sharding import PartitionSpec as P

SUB = 8
LANES = 128
STEP = 8
F32 = jnp.float32
BF16 = jnp.bfloat16
VMEM_LIMIT = 48 * 1024 * 1024


def as_tiles(rows):
    return rows.reshape(rows.shape[0] // SUB, SUB, LANES)


def as_rows(tiles):
    return tiles.reshape(tiles.shape[0] * SUB, LANES)


def tile(ref, token):
    return ref[pl.ds(pl.multiple_of(token * SUB, SUB), SUB), :]


def tree_sum(terms):
    while len(terms) > 1:
        terms = [
            terms[i] + terms[i + 1] if i + 1 < len(terms) else terms[i]
            for i in range(0, len(terms), 2)
        ]
    return terms[0]


def round16(value):
    return value.astype(BF16).astype(F32)


def scatter_tokens(ref, value, first_token):
    tokens, channels = value.shape
    for group in range(channels // LANES):
        ref[pl.ds(first_token * SUB + group, tokens, stride=SUB), :] = value[
            :, group * LANES : (group + 1) * LANES
        ]


def gather_tokens(ref, out_ref):
    tokens, channels = out_ref.shape
    for group in range(channels // LANES):
        out_ref[:, group * LANES : (group + 1) * LANES] = ref[
            pl.ds(group, tokens, stride=SUB), :
        ].astype(out_ref.dtype)


def advance_states(signal_ref, factors, states, first, count, reverse):
    last = signal_ref.shape[0] // SUB - 1

    def body(step, states):
        for inner in range(STEP):
            token = first + step * STEP + inner
            u = tile(signal_ref, last - token if reverse else token)
            states = [factor * state + u for factor, state in zip(factors, states)]
        return states

    return lax.fori_loop(0, count // STEP, body, states)


def zero_states(modes):
    return [jnp.zeros((SUB, LANES), F32) for _ in range(modes)]


def mode_rows(n):
    return slice(n * SUB, (n + 1) * SUB)


def fades(decay_ref, tokens):
    return [
        jnp.exp(-decay_ref[mode_rows(n), :] * tokens) for n in range(decay_ref.shape[0] // SUB)
    ]


def write_messages(out_ref, states, decay_ref, position_ref, tokens, direction):
    for other in range(out_ref.shape[0]):
        gap = direction * (other - position_ref[0]) - 1
        span = (jnp.maximum(gap, 0) * tokens).astype(F32)
        factor = jnp.where(gap >= 0, 1.0, 0.0).astype(F32)
        rows = [
            state * (fade * factor) for state, fade in zip(states, fades(decay_ref, span))
        ]
        out_ref[other] = jnp.concatenate(rows, axis=0).astype(out_ref.dtype)


def read_messages(in_ref):
    total = in_ref[0].astype(F32)
    for other in range(1, in_ref.shape[0]):
        total = total + in_ref[other].astype(F32)
    return [total[mode_rows(n)] for n in range(total.shape[0] // SUB)]


def rim_kernel(q_ref, k_ref, v_ref, out_ref):
    rows = q_ref.shape[0]
    for stream, source in enumerate((q_ref, k_ref, v_ref)):
        out_ref[stream * rows : (stream + 1) * rows, :] = source[...]


def filtered(window, taps_ref, stream, taps, steps, forward):
    total = None
    for tap in range(taps):
        first = taps - 1 - tap if forward else tap
        term = taps_ref[pl.ds((tap * 3 + stream) * SUB, SUB), :] * window[first : first + steps]
        total = term if total is None else total + term
    return total


def featurize_kernel(
    q_ref, k_ref, v_ref, taps_in_ref, residue_in_ref, decay_in_ref,
    qf_ref, kf_ref, vf_ref, mixed_ref, state_ref, taps_ref, scale_ref, decay_ref,
    narrow_ref, wide_ref, sems,
):
    tokens = q_ref.shape[0]
    taps = taps_in_ref.shape[0]
    modes = decay_in_ref.shape[1]
    sources = (q_ref, k_ref, v_ref)
    copies = [
        pltpu.make_async_copy(source, narrow_ref.at[stream], sems.at[stream])
        for stream, source in enumerate(sources)
    ]
    for copy in copies:
        copy.start()
    decays = decay_in_ref[...]
    scatter_tokens(decay_ref, decays.T, 0)
    scatter_tokens(scale_ref, (residue_in_ref[...] * jnp.sqrt(decays)).T, 0)
    for tap in range(taps):
        scatter_tokens(taps_ref, taps_in_ref[tap], tap * 3)
    for stream in range(3):
        copies[stream].wait()
        scatter_tokens(wide_ref.at[stream], narrow_ref[stream].astype(F32), 0)

    def body(step, carry):
        begin = pl.multiple_of((step + 1) * STEP * SUB, SUB)
        before = pl.multiple_of(begin - (taps - 1) * SUB, SUB)
        rows = pl.ds(begin, STEP * SUB)
        feats = []
        for stream, feat_ref in enumerate((qf_ref, kf_ref, vf_ref)):
            window = as_tiles(wide_ref[stream, pl.ds(before, (STEP + taps - 1) * SUB), :])
            feats.append(filtered(window, taps_ref, stream, taps, STEP, True))
            feat_ref[rows, :] = as_rows(feats[-1])
        mixed_ref[rows, :] = as_rows(round16(feats[1] * feats[2]))
        return carry

    lax.fori_loop(0, tokens // STEP - 1, body, 0)
    states = advance_states(
        mixed_ref, fades(decay_ref, 1.0), zero_states(modes), STEP, tokens - STEP, False
    )
    for n in range(modes):
        state_ref[mode_rows(n), :] = states[n]


def first_tokens_kernel(
    position_ref, q_ref, k_ref, v_ref, halo_ref, taps_ref, decay_ref, state_ref,
    qf_in, kf_in, vf_in, mixed_in, qf_ref, kf_ref, vf_ref, mixed_ref, message_ref,
    wide_ref, head_ref, sems, *, tokens, taps,
):
    rim = taps - 1
    modes = decay_ref.shape[0] // SUB
    block = q_ref.shape[0]
    copies = []
    feats = []
    for stream, source in enumerate((q_ref, k_ref, v_ref)):
        behind = halo_ref[stream * block : (stream + 1) * block, :].astype(F32)
        scatter_tokens(wide_ref, behind[block - rim :], 0)
        scatter_tokens(wide_ref, source[...].astype(F32)[:STEP], rim)
        window = as_tiles(wide_ref[...])
        feats.append(filtered(window, taps_ref, stream, taps, STEP, True))
        head_ref[stream] = as_rows(feats[-1])
    head_ref[3] = as_rows(round16(feats[1] * feats[2]))
    for stream, target in enumerate((qf_ref, kf_ref, vf_ref, mixed_ref)):
        copies.append(
            pltpu.make_async_copy(
                head_ref.at[stream], target.at[pl.ds(0, STEP * SUB), :], sems.at[stream]
            )
        )
        copies[-1].start()
    states = advance_states(
        head_ref.at[3], fades(decay_ref, 1.0), zero_states(modes), 0, STEP, False
    )
    later = fades(decay_ref, float(tokens - STEP))
    states = [
        state * fade + state_ref[mode_rows(n), :]
        for n, (state, fade) in enumerate(zip(states, later))
    ]
    write_messages(message_ref, states, decay_ref, position_ref, tokens, 1)
    for copy in copies:
        copy.wait()


def scales_of(scale_ref):
    return [scale_ref[mode_rows(n), :] for n in range(scale_ref.shape[0] // SUB)]


def local_conv_kernel(signal_ref, decay_ref, scale_ref, out_ref, *, reverse):
    tokens = signal_ref.shape[0] // SUB
    factors = fades(decay_ref, 1.0)
    scales = scales_of(scale_ref)

    def body(step, states):
        for inner in range(STEP):
            token = step * STEP + inner
            token = tokens - 1 - token if reverse else token
            u = tile(signal_ref, token)
            states = [factor * state + u for factor, state in zip(factors, states)]
            out_ref[pl.ds(pl.multiple_of(token * SUB, SUB), SUB), :] = tree_sum(
                [scale * state for scale, state in zip(scales, states)]
            )
        return states

    lax.fori_loop(0, tokens // STEP, body, zero_states(len(factors)))


def add_carried(local_ref, out_ref, states, decay_ref, scale_ref, reverse):
    tokens = local_ref.shape[0] // SUB
    factors = fades(decay_ref, 1.0)
    scaled = [scale * state for scale, state in zip(scales_of(scale_ref), states)]

    def body(step, scaled):
        for inner in range(STEP):
            token = step * STEP + inner
            token = tokens - 1 - token if reverse else token
            scaled = [factor * state for factor, state in zip(factors, scaled)]
            rows = pl.ds(pl.multiple_of(token * SUB, SUB), SUB)
            out_ref[rows, :] = local_ref[rows, :] + tree_sum(list(scaled))
        return scaled

    lax.fori_loop(0, tokens // STEP, body, scaled)


def project_kernel(
    message_ref, local_ref, decay_ref, scale_ref, qf_ref, weight_ref,
    conv_ref, out_ref, rows_ref, gated_ref, held_ref, sems,
):
    parts, _, width = out_ref.shape
    copies = [
        pltpu.make_async_copy(
            weight_ref.at[:, pl.ds(part * width, width)], held_ref.at[part], sems.at[part]
        )
        for part in range(parts)
    ]
    for copy in copies:
        copy.start()
    add_carried(local_ref, conv_ref, read_messages(message_ref), decay_ref, scale_ref, False)
    rows_ref[...] = qf_ref[...] * conv_ref[...]
    gather_tokens(rows_ref, gated_ref)
    block = min(width, 256)
    for part in range(parts):
        copies[part].wait()

        def body(step, carry):
            columns = pl.ds(pl.multiple_of(step * block, block), block)
            out_ref[part, :, columns] = jnp.dot(
                gated_ref[...], held_ref[part, :, columns], preferred_element_type=F32
            ).astype(out_ref.dtype)
            return carry

        lax.fori_loop(0, width // block, body, 0)


def add_parts_kernel(parts_ref, out_ref):
    out_ref[...] = tree_sum([parts_ref[n].astype(F32) for n in range(parts_ref.shape[0])]).astype(
        out_ref.dtype
    )


def back_products(index_ref, piece_refs, weight_ref, held_ref, sems, total_ref, base_ref):
    channels = total_ref.shape[0]
    parts = [(ref, inner) for ref in piece_refs for inner in range(ref.shape[0])]
    width = piece_refs[0].shape[2]
    copies = []
    for number in range(len(parts)):
        first = pl.multiple_of(index_ref[number] * width, width)
        copies.append(
            pltpu.make_async_copy(
                weight_ref.at[:, pl.ds(first, width)], held_ref.at[number], sems.at[number]
            )
        )
        copies[-1].start()
    block = min(channels, 256)
    for number, (ref, inner) in enumerate(parts):
        copies[number].wait()

        def body(step, carry):
            rows = pl.ds(pl.multiple_of(step * block, block), block)
            product = lax.dot_general(
                held_ref[number, rows, :], ref[inner],
                (((1,), (1,)), ((), ())), preferred_element_type=F32,
            )
            before = base_ref if number == 0 else total_ref
            total_ref[rows, :] = product if before is None else before[rows, :] + product
            return carry

        lax.fori_loop(0, channels // block, body, 0)


def back_part_kernel(*refs):
    index_ref, *pieces, weight_ref, total_ref, held_ref, sems = refs
    back_products(index_ref, pieces, weight_ref, held_ref, sems, total_ref, None)


def back_last_kernel(*refs, has_base):
    index_ref, *rest = refs
    (
        position_ref, weight_ref, qf_ref, decay_ref,
        grad_ref, mixed_ref, message_ref, total_ref, held_ref, sems,
    ) = rest[-10:]
    pieces = rest[:-10]
    base_ref = None
    if has_base:
        base_ref, *pieces = pieces
    back_products(index_ref, pieces, weight_ref, held_ref, sems, total_ref, base_ref)
    tokens = total_ref.shape[1]
    scatter_tokens(grad_ref, total_ref[...].T, 0)
    mixed_ref[...] = round16(grad_ref[...] * qf_ref[...])
    modes = decay_ref.shape[0] // SUB
    states = advance_states(
        mixed_ref, fades(decay_ref, 1.0), zero_states(modes), 0, tokens, True
    )
    write_messages(message_ref, states, decay_ref, position_ref, tokens, -1)


def finish_kernel(
    message_ref, local_ref, decay_ref, scale_ref, kf_ref, vf_ref, grad_ref, conv_ref, halo_ref,
    taps_ref, gq_ref, gk_ref, gv_ref, total_ref, wide_ref, rows_ref, *, taps,
):
    rim = taps - 1
    tokens = gq_ref.shape[0]
    states = read_messages(message_ref)
    add_carried(local_ref, total_ref, states, decay_ref, scale_ref, True)

    def body(step, carry):
        rows = pl.ds(pl.multiple_of(step * STEP * SUB, SUB), STEP * SUB)
        wide_ref[0, rows, :] = round16(grad_ref[rows, :] * conv_ref[rows, :])
        wide_ref[1, rows, :] = round16(total_ref[rows, :] * vf_ref[rows, :])
        wide_ref[2, rows, :] = round16(total_ref[rows, :] * kf_ref[rows, :])
        return carry

    lax.fori_loop(0, tokens // STEP, body, 0)
    growth = fades(decay_ref, -1.0)
    scales = scales_of(scale_ref)
    for ahead in range(rim):
        rows = pl.ds((tokens + ahead) * SUB, SUB)
        theirs = pl.ds(ahead * SUB, SUB)
        grad_conv = tree_sum([scale * state for scale, state in zip(scales, states)])
        wide_ref[0, rows, :] = halo_ref[0, theirs, :]
        wide_ref[1, rows, :] = round16(grad_conv * halo_ref[3, theirs, :])
        wide_ref[2, rows, :] = round16(grad_conv * halo_ref[2, theirs, :])
        arrived = halo_ref[1, theirs, :]
        states = [(state - arrived) * grow for state, grow in zip(states, growth)]

    def spread(step, carry):
        first = pl.multiple_of(step * STEP * SUB, SUB)
        for stream in range(3):
            window = as_tiles(wide_ref[stream, pl.ds(first, (STEP + rim) * SUB), :])
            rows_ref[stream, pl.ds(first, STEP * SUB), :] = as_rows(
                filtered(window, taps_ref, stream, taps, STEP, False)
            )
        return carry

    lax.fori_loop(0, tokens // STEP, spread, 0)
    for stream, out_ref in enumerate((gq_ref, gk_ref, gv_ref)):
        gather_tokens(rows_ref.at[stream], out_ref)


IN_VMEM = pl.BlockSpec(memory_space=pltpu.VMEM)
IN_SMEM = pl.BlockSpec(memory_space=pltpu.SMEM)
ANYWHERE = pl.BlockSpec(memory_space=pl.ANY)
HBM_RATE = 3.5e6


def call(kernel, outs, args, specs, scratch, name, micros, out_specs=None, **options):
    return pl.pallas_call(
        kernel,
        out_shape=[jax.ShapeDtypeStruct(shape, kind) for shape, kind in outs],
        in_specs=specs,
        out_specs=out_specs or [IN_VMEM] * len(outs),
        scratch_shapes=scratch,
        compiler_params=pltpu.CompilerParams(vmem_limit_bytes=VMEM_LIMIT),
        cost_estimate=pl.CostEstimate(
            flops=0, bytes_accessed=int(micros * HBM_RATE), transcendentals=0
        ),
        name=name,
        **options,
    )(*args)


def shift(value, axis, steps):
    count = lax.axis_size(axis)
    pairs = [(s, s + steps) for s in range(count) if 0 <= s + steps < count]
    return lax.ppermute(value, axis, pairs)


def exchange(value, axis, mask):
    count = lax.axis_size(axis)
    return lax.ppermute(value, axis, [(s, s ^ mask) for s in range(count)])


def shards(query_in, key_in, value_in, short_taps, residues, decays, out_weight, out_grad):
    tokens, channels = query_in.shape
    taps = short_taps.shape[0]
    rim = taps - 1
    modes = decays.shape[1]
    blocks = lax.axis_size("ctx")
    fans = lax.axis_size("ch")
    mine = lax.axis_index("ch")
    position = lax.axis_index("ctx")[None].astype(jnp.int32)
    tile_shape = (tokens * SUB, LANES)
    mode_shape = (modes * SUB, LANES)
    message_shape = (blocks,) + mode_shape
    streams = (query_in, key_in, value_in)
    rim_rows = 16

    def edge(index):
        return pl.BlockSpec((rim_rows, channels), lambda i: (index, 0))

    (halo,) = call(
        rim_kernel, [((3 * rim_rows, channels), BF16)], streams,
        [edge(tokens // rim_rows - 1)] * 3, [], "rim", 1.0,
        out_specs=[pl.BlockSpec((3 * rim_rows, channels), lambda i: (0, 0))], grid=(1,),
    )
    halo = shift(halo, "ctx", 1)

    query_feat, key_feat, value_feat, mixed, state, tap_tiles, scale_tiles, decay_tiles = call(
        featurize_kernel,
        [(tile_shape, F32)] * 4
        + [(mode_shape, F32), ((taps * 3 * SUB, LANES), F32), (mode_shape, F32), (mode_shape, F32)],
        streams + (short_taps, residues, decays),
        [ANYWHERE] * 3 + [IN_VMEM] * 3,
        [
            pltpu.VMEM((3, tokens, channels), BF16),
            pltpu.VMEM((3,) + tile_shape, F32),
            pltpu.SemaphoreType.DMA((3,)),
        ],
        "featurize", 4.0,
    )
    whole = lambda shape: pl.BlockSpec(shape, lambda i: (0,) * len(shape))
    query_feat, key_feat, value_feat, mixed, messages = call(
        functools.partial(first_tokens_kernel, tokens=tokens, taps=taps),
        [(tile_shape, F32)] * 4 + [(message_shape, BF16)],
        (position,) + streams
        + (halo, tap_tiles, decay_tiles, state, query_feat, key_feat, value_feat, mixed),
        [IN_SMEM] + [edge(0)] * 3
        + [whole(halo.shape), whole(tap_tiles.shape), whole(mode_shape), whole(mode_shape)]
        + [ANYWHERE] * 4,
        [
            pltpu.VMEM(((STEP + rim) * SUB, LANES), F32),
            pltpu.VMEM((4, STEP * SUB, LANES), F32),
            pltpu.SemaphoreType.DMA((4,)),
        ],
        "first_tokens", 1.0,
        out_specs=[ANYWHERE] * 4 + [whole(message_shape)], grid=(1,),
        input_output_aliases={8: 0, 9: 1, 10: 2, 11: 3},
    )
    arrived = lax.all_to_all(messages, "ctx", split_axis=0, concat_axis=0, tiled=True)
    (local,) = call(
        functools.partial(local_conv_kernel, reverse=False),
        [(tile_shape, F32)], (mixed, decay_tiles, scale_tiles), [IN_VMEM] * 3, [],
        "local_conv", 2.3,
    )
    conv_out, partial_sums = call(
        project_kernel,
        [(tile_shape, F32), ((fans, tokens, channels), BF16)],
        (arrived, local, decay_tiles, scale_tiles, query_feat, out_weight),
        [IN_VMEM] * 5 + [ANYWHERE],
        [
            pltpu.VMEM(tile_shape, F32),
            pltpu.VMEM((tokens, channels), BF16),
            pltpu.VMEM((fans, channels, channels), BF16),
            pltpu.SemaphoreType.DMA((fans,)),
        ],
        "project", 8.0,
    )
    parts = lax.all_to_all(partial_sums, "ch", split_axis=0, concat_axis=0, tiled=True)
    step_rows = tokens // 4
    (projected,) = call(
        add_parts_kernel, [((tokens, channels), BF16)], (parts,),
        [pl.BlockSpec((fans, step_rows, channels), lambda i: (0, i, 0))], [], "add_parts", 1.5,
        out_specs=[pl.BlockSpec((step_rows, channels), lambda i: (i, 0))],
        grid=(tokens // step_rows,),
    )

    def scratch_for(count):
        return [
            pltpu.VMEM((count, channels, channels), BF16),
            pltpu.SemaphoreType.DMA((count,)),
        ]

    own = out_grad[None]
    if fans == 4:
        near = exchange(own, "ch", 1)
        far = exchange(own, "ch", 2)
        half = tokens // 2
        top = exchange(far[:, :half], "ch", 1)
        bottom = exchange(near[:, half:], "ch", 2)
        across = jnp.concatenate([top, bottom], axis=1)
        first_index = jnp.stack([mine, mine ^ 1, mine ^ 2]).astype(jnp.int32)
        (base,) = call(
            back_part_kernel,
            [((channels, tokens), F32)],
            (first_index, own, near, far, out_weight),
            [IN_SMEM] + [IN_VMEM] * 3 + [ANYWHERE],
            scratch_for(3), "back_part", 5.0,
        )
        pieces, bases, count = [across], [base], 1
        last_index = (mine ^ 3)[None].astype(jnp.int32)
    else:
        pieces, bases, count = [lax.all_gather(out_grad, "ch", axis=0, tiled=False)], [], fans
        last_index = jnp.arange(fans, dtype=jnp.int32)
    grad_gated, grad_mixed, back_messages = call(
        functools.partial(back_last_kernel, has_base=bool(bases)),
        [(tile_shape, F32), (tile_shape, F32), (message_shape, BF16)],
        (last_index, *bases, *pieces, position, out_weight, query_feat, decay_tiles),
        [IN_SMEM] + [IN_VMEM] * (len(bases) + len(pieces)) + [IN_SMEM, ANYWHERE] + [IN_VMEM] * 2,
        [pltpu.VMEM((channels, tokens), F32)] + scratch_for(count),
        "back_last", 4.5,
    )
    back_arrived = lax.all_to_all(back_messages, "ctx", split_axis=0, concat_axis=0, tiled=True)
    (back_local,) = call(
        functools.partial(local_conv_kernel, reverse=True),
        [(tile_shape, F32)], (grad_mixed, decay_tiles, scale_tiles), [IN_VMEM] * 3, [],
        "back_local_conv", 2.3,
    )
    head = slice(0, rim * SUB)
    grad_query_head = (grad_gated[head] * conv_out[head]).astype(BF16).astype(F32)
    ahead = shift(
        jnp.stack([grad_query_head, grad_mixed[head], key_feat[head], value_feat[head]]), "ctx", -1
    )
    grad_query, grad_key, grad_value = call(
        functools.partial(finish_kernel, taps=taps),
        [((tokens, channels), BF16)] * 3,
        (
            back_arrived, back_local, decay_tiles, scale_tiles, key_feat, value_feat,
            grad_gated, conv_out, ahead, tap_tiles,
        ),
        [IN_VMEM] * 10,
        [
            pltpu.VMEM(tile_shape, F32),
            pltpu.VMEM((3, (tokens + rim) * SUB, LANES), F32),
            pltpu.VMEM((3,) + tile_shape, F32),
        ],
        "finish", 5.0,
    )
    return (projected, grad_query, grad_key, grad_value)


def solution(mesh):
    in_specs = (
        P("ctx", "ch"),
        P("ctx", "ch"),
        P("ctx", "ch"),
        P(None, None, "ch"),
        P("ch", None),
        P("ch", None),
        P("ch", None),
        P("ctx", "ch"),
    )
    out_specs = (P("ctx", "ch"), P("ctx", "ch"), P("ctx", "ch"), P("ctx", "ch"))
    return jax.shard_map(shards, mesh=mesh, in_specs=in_specs, out_specs=out_specs, check_vma=False)
```

```python
import functools

import jax
import jax.numpy as jnp
from jax import lax
from jax.experimental import pallas as pl
from jax.experimental.pallas import tpu as pltpu
from jax.sharding import PartitionSpec as P

SUB = 8
LANES = 128
STEP = 8
F32 = jnp.float32
BF16 = jnp.bfloat16


def as_tiles(rows):
    return rows.reshape(rows.shape[0] // SUB, SUB, LANES)


def as_rows(tiles):
    return tiles.reshape(tiles.shape[0] * SUB, LANES)


def tile(ref, token):
    return ref[pl.ds(pl.multiple_of(token * SUB, SUB), SUB), :]


def tree_sum(terms):
    while len(terms) > 1:
        terms = [
            terms[i] + terms[i + 1] if i + 1 < len(terms) else terms[i]
            for i in range(0, len(terms), 2)
        ]
    return terms[0]


def round16(value):
    return value.astype(BF16).astype(F32)


def scatter_tokens(ref, value, first_token):
    tokens, channels = value.shape
    for group in range(channels // LANES):
        ref[pl.ds(first_token * SUB + group, tokens, stride=SUB), :] = value[
            :, group * LANES : (group + 1) * LANES
        ]


def gather_tokens(ref, out_ref):
    tokens, channels = out_ref.shape
    for group in range(channels // LANES):
        out_ref[:, group * LANES : (group + 1) * LANES] = ref[
            pl.ds(group, tokens, stride=SUB), :
        ].astype(out_ref.dtype)


def advance_states(signal_ref, factors, states, first, count, reverse):
    last = signal_ref.shape[0] // SUB - 1

    def body(step, states):
        for inner in range(STEP):
            token = first + step * STEP + inner
            u = tile(signal_ref, last - token if reverse else token)
            states = [factor * state + u for factor, state in zip(factors, states)]
        return states

    return lax.fori_loop(0, count // STEP, body, states)


def zero_states(modes):
    return [jnp.zeros((SUB, LANES), F32) for _ in range(modes)]


def mode_rows(n):
    return slice(n * SUB, (n + 1) * SUB)


def fades(decay_ref, tokens):
    return [
        jnp.exp(-decay_ref[mode_rows(n), :] * tokens) for n in range(decay_ref.shape[0] // SUB)
    ]


def write_messages(out_ref, states, decay_ref, position_ref, tokens, direction):
    for other in range(out_ref.shape[0]):
        gap = direction * (other - position_ref[0]) - 1
        span = (jnp.maximum(gap, 0) * tokens).astype(F32)
        factor = jnp.where(gap >= 0, 1.0, 0.0).astype(F32)
        rows = [
            state * (fade * factor) for state, fade in zip(states, fades(decay_ref, span))
        ]
        out_ref[other] = jnp.concatenate(rows, axis=0).astype(out_ref.dtype)


def read_messages(in_ref):
    total = in_ref[0].astype(F32)
    for other in range(1, in_ref.shape[0]):
        total = total + in_ref[other].astype(F32)
    return [total[mode_rows(n)] for n in range(total.shape[0] // SUB)]


def rim_kernel(q_ref, k_ref, v_ref, out_ref, sems):
    rows = out_ref.shape[0] // 3
    copies = [
        pltpu.make_async_copy(
            source.at[pl.ds(source.shape[0] - rows, rows), :],
            out_ref.at[pl.ds(stream * rows, rows), :],
            sems.at[stream],
        )
        for stream, source in enumerate((q_ref, k_ref, v_ref))
    ]
    for copy in copies:
        copy.start()
    for copy in copies:
        copy.wait()


def filtered(window, taps_ref, stream, taps, steps, forward):
    total = None
    for tap in range(taps):
        first = taps - 1 - tap if forward else tap
        term = taps_ref[pl.ds((stream * taps + tap) * SUB, SUB), :] * window[first : first + steps]
        total = term if total is None else total + term
    return total


def featurize_kernel(
    position_ref, q_ref, k_ref, v_ref, taps_in_ref, residue_in_ref, decay_in_ref, halo_ref,
    qf_ref, kf_ref, vf_ref, mixed_ref, message_ref, taps_ref, scale_ref, decay_ref,
    narrow_ref, wide_ref, taps_vmem, residue_vmem, decay_vmem, sems,
):
    tokens = q_ref.shape[0]
    _, taps, _ = taps_in_ref.shape
    rim = taps - 1
    modes = decay_in_ref.shape[0]
    copies = [
        pltpu.make_async_copy(source, target, sems.at[number])
        for number, (source, target) in enumerate(
            (
                (decay_in_ref, decay_vmem),
                (residue_in_ref, residue_vmem),
                (taps_in_ref, taps_vmem),
                (q_ref, narrow_ref.at[0]),
                (k_ref, narrow_ref.at[1]),
                (v_ref, narrow_ref.at[2]),
            )
        )
    ]
    for copy in copies:
        copy.start()
    held = halo_ref.shape[0] // 3
    for stream in range(3):
        behind = halo_ref[stream * held : (stream + 1) * held, :].astype(F32)
        scatter_tokens(wide_ref.at[stream], behind[held - rim :], 0)
    for copy in copies[:3]:
        copy.wait()
    decays = decay_vmem[...]
    scatter_tokens(decay_ref, decays, 0)
    scatter_tokens(scale_ref, residue_vmem[...] * jnp.sqrt(decays), 0)
    for stream in range(3):
        scatter_tokens(taps_ref, taps_vmem[stream], stream * taps)
    for stream in range(3):
        copies[3 + stream].wait()
        scatter_tokens(wide_ref.at[stream], narrow_ref[stream].astype(F32), rim)

    def body(step, carry):
        begin = pl.multiple_of(step * STEP * SUB, SUB)
        rows = pl.ds(begin, STEP * SUB)
        feats = []
        for stream, feat_ref in enumerate((qf_ref, kf_ref, vf_ref)):
            window = as_tiles(wide_ref[stream, pl.ds(begin, (STEP + rim) * SUB), :])
            feats.append(filtered(window, taps_ref, stream, taps, STEP, True))
            feat_ref[rows, :] = as_rows(feats[-1])
        mixed_ref[rows, :] = as_rows(round16(feats[1] * feats[2]))
        return carry

    lax.fori_loop(0, tokens // STEP, body, 0)
    states = advance_states(
        mixed_ref, fades(decay_ref, 1.0), zero_states(modes), 0, tokens, False
    )
    write_messages(message_ref, states, decay_ref, position_ref, tokens, 1)


def scales_of(scale_ref):
    return [scale_ref[mode_rows(n), :] for n in range(scale_ref.shape[0] // SUB)]


def local_conv_kernel(signal_ref, decay_ref, scale_ref, out_ref, *, reverse):
    tokens = signal_ref.shape[0] // SUB
    factors = fades(decay_ref, 1.0)
    scales = scales_of(scale_ref)

    def body(step, states):
        for inner in range(STEP):
            token = step * STEP + inner
            token = tokens - 1 - token if reverse else token
            u = tile(signal_ref, token)
            states = [factor * state + u for factor, state in zip(factors, states)]
            out_ref[pl.ds(pl.multiple_of(token * SUB, SUB), SUB), :] = tree_sum(
                [scale * state for scale, state in zip(scales, states)]
            )
        return states

    lax.fori_loop(0, tokens // STEP, body, zero_states(len(factors)))


def add_carried(local_ref, out_ref, states, decay_ref, scale_ref, reverse):
    tokens = local_ref.shape[0] // SUB
    factors = fades(decay_ref, 1.0)
    scaled = [scale * state for scale, state in zip(scales_of(scale_ref), states)]

    def body(step, scaled):
        for inner in range(STEP):
            token = step * STEP + inner
            token = tokens - 1 - token if reverse else token
            scaled = [factor * state for factor, state in zip(factors, scaled)]
            rows = pl.ds(pl.multiple_of(token * SUB, SUB), SUB)
            out_ref[rows, :] = local_ref[rows, :] + tree_sum(list(scaled))
        return scaled

    lax.fori_loop(0, tokens // STEP, body, scaled)


def project_kernel(
    index_ref, message_ref, local_ref, decay_ref, scale_ref, qf_ref, weight_ref, conv_ref, *refs
):
    *out_refs, rows_ref, gated_ref, held_ref, sems = refs
    width = out_refs[0].shape[1]
    copies = []
    for number in reversed(range(len(out_refs))):
        first = pl.multiple_of(index_ref[number] * width, width)
        copies.append(
            pltpu.make_async_copy(
                weight_ref.at[:, pl.ds(first, width)], held_ref.at[number], sems.at[number]
            )
        )
        copies[-1].start()
    add_carried(local_ref, conv_ref, read_messages(message_ref), decay_ref, scale_ref, False)
    rows_ref[...] = qf_ref[...] * conv_ref[...]
    gather_tokens(rows_ref, gated_ref)
    block = min(width, 256)
    for copy, number in zip(copies, reversed(range(len(out_refs)))):
        out_ref = out_refs[number]
        copy.wait()

        def body(step, carry):
            columns = pl.ds(pl.multiple_of(step * block, block), block)
            out_ref[:, columns] = jnp.dot(
                gated_ref[...], held_ref[number, :, columns], preferred_element_type=F32
            ).astype(out_ref.dtype)
            return carry

        lax.fori_loop(0, width // block, body, 0)


def add_parts_kernel(*refs):
    *part_refs, out_ref = refs
    out_ref[...] = tree_sum([ref[...].astype(F32) for ref in part_refs]).astype(out_ref.dtype)


def back_kernel(
    index_ref, position_ref, weight_ref, qf_ref, kf_ref, vf_ref, conv_ref, decay_ref, *refs, rim
):
    *piece_refs, grad_ref, mixed_ref, message_ref, ahead_ref, turned_ref, total_ref, held_ref, sems = refs
    channels, tokens = total_ref.shape
    width = piece_refs[0].shape[1]

    def fetch(number):
        first = pl.multiple_of(index_ref[number] * width, width)
        return pltpu.make_async_copy(
            weight_ref.at[:, pl.ds(first, width)], held_ref.at[number], sems.at[number]
        )

    for number in range(len(piece_refs)):
        fetch(number).start()
    for number, ref in enumerate(piece_refs):
        turned_ref[number] = ref[...].T
    total_ref[...] = jnp.zeros_like(total_ref)

    def body(number, carry):
        fetch(number).wait()
        total_ref[...] += jnp.dot(
            held_ref[number], turned_ref[number], preferred_element_type=F32
        )
        return carry

    lax.fori_loop(0, len(piece_refs), body, 0)
    scatter_tokens(grad_ref, total_ref[...].T, 0)
    mixed_ref[...] = round16(grad_ref[...] * qf_ref[...])
    head = slice(0, rim * SUB)
    ahead_ref[0] = round16(grad_ref[head, :] * conv_ref[head, :])
    ahead_ref[1] = mixed_ref[head, :]
    ahead_ref[2] = kf_ref[head, :]
    ahead_ref[3] = vf_ref[head, :]
    modes = decay_ref.shape[0] // SUB
    states = advance_states(
        mixed_ref, fades(decay_ref, 1.0), zero_states(modes), 0, tokens, True
    )
    write_messages(message_ref, states, decay_ref, position_ref, tokens, -1)


def finish_kernel(
    message_ref, local_ref, decay_ref, scale_ref, kf_ref, vf_ref, grad_ref, conv_ref, halo_ref,
    taps_ref, gq_ref, gk_ref, gv_ref, total_ref, wide_ref, rows_ref, *, taps,
):
    rim = taps - 1
    tokens = gq_ref.shape[0]
    states = read_messages(message_ref)
    add_carried(local_ref, total_ref, states, decay_ref, scale_ref, True)

    def body(step, carry):
        rows = pl.ds(pl.multiple_of(step * STEP * SUB, SUB), STEP * SUB)
        wide_ref[0, rows, :] = round16(grad_ref[rows, :] * conv_ref[rows, :])
        wide_ref[1, rows, :] = round16(total_ref[rows, :] * vf_ref[rows, :])
        wide_ref[2, rows, :] = round16(total_ref[rows, :] * kf_ref[rows, :])
        return carry

    lax.fori_loop(0, tokens // STEP, body, 0)
    growth = fades(decay_ref, -1.0)
    scales = scales_of(scale_ref)
    for ahead in range(rim):
        rows = pl.ds((tokens + ahead) * SUB, SUB)
        theirs = pl.ds(ahead * SUB, SUB)
        grad_conv = tree_sum([scale * state for scale, state in zip(scales, states)])
        wide_ref[0, rows, :] = halo_ref[0, theirs, :]
        wide_ref[1, rows, :] = round16(grad_conv * halo_ref[3, theirs, :])
        wide_ref[2, rows, :] = round16(grad_conv * halo_ref[2, theirs, :])
        arrived = halo_ref[1, theirs, :]
        states = [(state - arrived) * grow for state, grow in zip(states, growth)]

    def spread(step, carry):
        first = pl.multiple_of(step * STEP * SUB, SUB)
        for stream in range(3):
            window = as_tiles(wide_ref[stream, pl.ds(first, (STEP + rim) * SUB), :])
            rows_ref[stream, pl.ds(first, STEP * SUB), :] = as_rows(
                filtered(window, taps_ref, stream, taps, STEP, False)
            )
        return carry

    lax.fori_loop(0, tokens // STEP, spread, 0)
    for stream, out_ref in enumerate((gq_ref, gk_ref, gv_ref)):
        gather_tokens(rows_ref.at[stream], out_ref)


IN_VMEM = pl.BlockSpec(memory_space=pltpu.VMEM)
IN_SMEM = pl.BlockSpec(memory_space=pltpu.SMEM)
IN_HBM = pl.BlockSpec(memory_space=pltpu.HBM)
HBM_RATE = 3.5e6


def call(kernel, outs, args, specs, scratch, name, micros, mebibytes, out_specs=None, **options):
    args = [
        pltpu.with_memory_space_constraint(arg, pltpu.HBM) if spec is IN_HBM else arg
        for arg, spec in zip(args, specs)
    ]
    return pl.pallas_call(
        kernel,
        out_shape=[jax.ShapeDtypeStruct(shape, kind) for shape, kind in outs],
        in_specs=specs,
        out_specs=out_specs or [IN_VMEM] * len(outs),
        scratch_shapes=scratch,
        compiler_params=pltpu.CompilerParams(vmem_limit_bytes=mebibytes * 1024 * 1024),
        cost_estimate=pl.CostEstimate(
            flops=0, bytes_accessed=int(micros * HBM_RATE), transcendentals=0
        ),
        name=name,
        **options,
    )(*args)


def shift(value, axis, steps):
    count = lax.axis_size(axis)
    pairs = [(s, s + steps) for s in range(count) if 0 <= s + steps < count]
    return lax.ppermute(value, axis, pairs)


def exchange(value, axis, mask):
    count = lax.axis_size(axis)
    return lax.ppermute(value, axis, [(s, s ^ mask) for s in range(count)])


def shards(query_in, key_in, value_in, short_taps, residues, decays, out_weight, out_grad):
    tokens, channels = query_in.shape
    taps = short_taps.shape[0]
    rim = taps - 1
    modes = decays.shape[1]
    blocks = lax.axis_size("ctx")
    fans = lax.axis_size("ch")
    position = lax.axis_index("ctx")[None].astype(jnp.int32)
    tile_shape = (tokens * SUB, LANES)
    mode_shape = (modes * SUB, LANES)
    message_shape = (blocks,) + mode_shape
    streams = (query_in, key_in, value_in)
    rim_rows = 16

    (halo,) = call(
        rim_kernel, [((3 * rim_rows, channels), BF16)], streams, [IN_HBM] * 3,
        [pltpu.SemaphoreType.DMA((3,))], "rim", 1.0, 2,
    )
    halo, out_grad = lax.optimization_barrier((halo, out_grad))
    halo = shift(halo, "ctx", 1)
    if fans == 4:
        order = lax.axis_index("ch") ^ jnp.arange(fans, dtype=jnp.int32)
        pieces = [out_grad] + [exchange(out_grad, "ch", mask) for mask in range(1, fans)]
    else:
        order = jnp.arange(fans, dtype=jnp.int32)
        everyone = lax.all_gather(out_grad, "ch", axis=0, tiled=False)
        pieces = [everyone[number] for number in range(fans)]

    (
        query_feat, key_feat, value_feat, mixed, messages, tap_tiles, scale_tiles, decay_tiles,
    ) = call(
        featurize_kernel,
        [(tile_shape, F32)] * 4
        + [(message_shape, BF16), ((taps * 3 * SUB, LANES), F32), (mode_shape, F32), (mode_shape, F32)],
        (position,) + streams
        + (jnp.transpose(short_taps, (1, 0, 2)), residues.T, decays.T, halo),
        [IN_SMEM] + [IN_HBM] * 6 + [IN_VMEM],
        [
            pltpu.VMEM((3, tokens, channels), BF16),
            pltpu.VMEM((3, (tokens + rim) * SUB, LANES), F32),
            pltpu.VMEM((3, taps, channels), F32),
            pltpu.VMEM((modes, channels), F32),
            pltpu.VMEM((modes, channels), F32),
            pltpu.SemaphoreType.DMA((6,)),
        ],
        "featurize", 4.5, 8,
    )
    arrived = lax.all_to_all(messages, "ctx", split_axis=0, concat_axis=0, tiled=True)
    (local,) = call(
        functools.partial(local_conv_kernel, reverse=False),
        [(tile_shape, F32)], (mixed, decay_tiles, scale_tiles), [IN_VMEM] * 3, [],
        "local_conv", 2.3, 2,
    )
    conv_out, *partial_sums = call(
        project_kernel,
        [(tile_shape, F32)] + [((tokens, channels), BF16)] * fans,
        (order, arrived, local, decay_tiles, scale_tiles, query_feat, out_weight),
        [IN_SMEM] + [IN_VMEM] * 5 + [IN_HBM],
        [
            pltpu.VMEM(tile_shape, F32),
            pltpu.VMEM((tokens, channels), BF16),
            pltpu.VMEM((fans, channels, channels), BF16),
            pltpu.SemaphoreType.DMA((fans,)),
        ],
        "project", 7.0, 14,
    )
    if fans == 4:
        parts = [
            exchange(part, "ch", mask) if mask else part for mask, part in enumerate(partial_sums)
        ]
    else:
        parts = lax.all_to_all(
            jnp.stack(partial_sums), "ch", split_axis=0, concat_axis=0, tiled=True
        )
        parts = [parts[number] for number in range(fans)]
    (projected,) = call(
        add_parts_kernel, [((tokens, channels), BF16)], tuple(parts), [IN_VMEM] * fans, [],
        "add_parts", 1.5, 4,
    )

    grad_gated, grad_mixed, back_messages, ahead = call(
        functools.partial(back_kernel, rim=rim),
        [(tile_shape, F32)] * 2 + [(message_shape, BF16), ((4, rim * SUB, LANES), F32)],
        (
            order, position, out_weight, query_feat, key_feat, value_feat, conv_out, decay_tiles,
            *pieces,
        ),
        [IN_SMEM] * 2 + [IN_HBM] + [IN_VMEM] * (5 + fans),
        [
            pltpu.VMEM((fans, channels, tokens), BF16),
            pltpu.VMEM((channels, tokens), F32),
            pltpu.VMEM((fans, channels, channels), BF16),
            pltpu.SemaphoreType.DMA((fans,)),
        ],
        "back", 8.0, 18,
    )
    back_arrived = lax.all_to_all(back_messages, "ctx", split_axis=0, concat_axis=0, tiled=True)
    ahead = shift(ahead, "ctx", -1)
    (back_local,) = call(
        functools.partial(local_conv_kernel, reverse=True),
        [(tile_shape, F32)], (grad_mixed, decay_tiles, scale_tiles), [IN_VMEM] * 3, [],
        "back_local_conv", 2.3, 2,
    )
    grad_query, grad_key, grad_value = call(
        functools.partial(finish_kernel, taps=taps),
        [((tokens, channels), BF16)] * 3,
        (
            back_arrived, back_local, decay_tiles, scale_tiles, key_feat, value_feat,
            grad_gated, conv_out, ahead, tap_tiles,
        ),
        [IN_VMEM] * 10,
        [
            pltpu.VMEM(tile_shape, F32),
            pltpu.VMEM((3, (tokens + rim) * SUB, LANES), F32),
            pltpu.VMEM((3,) + tile_shape, F32),
        ],
        "finish", 5.0, 10,
    )
    return (projected, grad_query, grad_key, grad_value)


def solution(mesh):
    in_specs = (
        P("ctx", "ch"),
        P("ctx", "ch"),
        P("ctx", "ch"),
        P(None, None, "ch"),
        P("ch", None),
        P("ch", None),
        P("ch", None),
        P("ctx", "ch"),
    )
    out_specs = (P("ctx", "ch"), P("ctx", "ch"), P("ctx", "ch"), P("ctx", "ch"))
    return jax.shard_map(shards, mesh=mesh, in_specs=in_specs, out_specs=out_specs, check_vma=False)
```

```python
import functools

import jax
import jax.numpy as jnp
from jax import lax
from jax.experimental import pallas as pl
from jax.experimental.pallas import tpu as pltpu
from jax.sharding import PartitionSpec as P

SUB = 8
LANES = 128
STEP = 8
F32 = jnp.float32
BF16 = jnp.bfloat16


def as_tiles(rows):
    return rows.reshape(rows.shape[0] // SUB, SUB, LANES)


def as_rows(tiles):
    return tiles.reshape(tiles.shape[0] * SUB, LANES)


def tile(ref, token):
    return ref[pl.ds(pl.multiple_of(token * SUB, SUB), SUB), :]


def tree_sum(terms):
    while len(terms) > 1:
        terms = [
            terms[i] + terms[i + 1] if i + 1 < len(terms) else terms[i]
            for i in range(0, len(terms), 2)
        ]
    return terms[0]


def round16(value):
    return value.astype(BF16).astype(F32)


def scatter_tokens(ref, value, first_token):
    tokens, channels = value.shape
    for group in range(channels // LANES):
        ref[pl.ds(first_token * SUB + group, tokens, stride=SUB), :] = value[
            :, group * LANES : (group + 1) * LANES
        ]


def gather_tokens(rows, out_ref):
    for group in range(out_ref.shape[1] // LANES):
        out_ref[:, group * LANES : (group + 1) * LANES] = rows(group).astype(out_ref.dtype)


def group_rows(ref, group, tokens):
    return ref[pl.ds(group, tokens, stride=SUB), :]


def start_all(copies):
    for copy in copies:
        copy.start()
    return copies


def wait_all(copies):
    for copy in copies:
        copy.wait()


def advance_states(signal_ref, factors, states, first, count, reverse):
    last = signal_ref.shape[0] // SUB - 1

    def body(step, states):
        for inner in range(STEP):
            token = first + step * STEP + inner
            u = tile(signal_ref, last - token if reverse else token)
            states = [factor * state + u for factor, state in zip(factors, states)]
        return states

    return lax.fori_loop(0, count // STEP, body, states)


def zero_states(modes):
    return [jnp.zeros((SUB, LANES), F32) for _ in range(modes)]


def mode_rows(n):
    return slice(n * SUB, (n + 1) * SUB)


def fades(decay_ref, tokens):
    return [
        jnp.exp(-decay_ref[mode_rows(n), :] * tokens) for n in range(decay_ref.shape[0] // SUB)
    ]


def write_messages(out_ref, states, decay_ref, position_ref, tokens, direction):
    count = out_ref.shape[0]
    out_ref[...] = jnp.zeros_like(out_ref)
    fade = fades(decay_ref, float(tokens))
    for gap in range(count - 1):
        other = position_ref[0] + direction * (gap + 1)
        value = jnp.concatenate(states, axis=0).astype(out_ref.dtype)

        @pl.when((other >= 0) & (other < count))
        def _():
            out_ref[jnp.clip(other, 0, count - 1)] = value

        states = [state * factor for state, factor in zip(states, fade)]


def read_messages(in_ref):
    total = in_ref[0].astype(F32)
    for other in range(1, in_ref.shape[0]):
        total = total + in_ref[other].astype(F32)
    return [total[mode_rows(n)] for n in range(total.shape[0] // SUB)]


def rim_kernel(q_ref, k_ref, v_ref, out_ref, sems):
    rows = out_ref.shape[0] // 3
    copies = [
        pltpu.make_async_copy(
            source.at[pl.ds(source.shape[0] - rows, rows), :],
            out_ref.at[pl.ds(stream * rows, rows), :],
            sems.at[stream],
        )
        for stream, source in enumerate((q_ref, k_ref, v_ref))
    ]
    for copy in copies:
        copy.start()
    for copy in copies:
        copy.wait()


def filtered(window, taps_ref, stream, taps, steps, forward):
    total = None
    for tap in range(taps):
        first = taps - 1 - tap if forward else tap
        term = taps_ref[pl.ds((stream * taps + tap) * SUB, SUB), :] * window[first : first + steps]
        total = term if total is None else total + term
    return total


def featurize_kernel(
    position_ref, q_ref, k_ref, v_ref, taps_in_ref, residue_in_ref, decay_in_ref, halo_ref,
    qf_ref, kf_ref, vf_ref, mixed_ref, message_ref, scale_ref, decay_ref,
    narrow_ref, wide_ref, feat_ref, taps_ref, taps_vmem, residue_vmem, decay_vmem, sems,
):
    tokens = q_ref.shape[0]
    _, taps, _ = taps_in_ref.shape
    rim = taps - 1
    modes = decay_in_ref.shape[0]
    copies = start_all(
        [
            pltpu.make_async_copy(source, target, sems.at[number])
            for number, (source, target) in enumerate(
                (
                    (decay_in_ref, decay_vmem),
                    (residue_in_ref, residue_vmem),
                    (taps_in_ref, taps_vmem),
                    (q_ref, narrow_ref.at[0]),
                    (k_ref, narrow_ref.at[1]),
                    (v_ref, narrow_ref.at[2]),
                )
            )
        ]
    )
    held = halo_ref.shape[0] // 3
    for stream in range(3):
        behind = halo_ref[stream * held : (stream + 1) * held, :].astype(F32)
        scatter_tokens(wide_ref.at[stream], behind[held - rim :], 0)
    wait_all(copies[:3])
    decays = decay_vmem[...]
    scatter_tokens(decay_ref, decays, 0)
    scatter_tokens(scale_ref, residue_vmem[...] * jnp.sqrt(decays), 0)
    for stream in range(3):
        scatter_tokens(taps_ref, taps_vmem[stream], stream * taps)
    for stream in range(3):
        copies[3 + stream].wait()
        scatter_tokens(wide_ref.at[stream], narrow_ref[stream].astype(F32), rim)

    def body(step, carry):
        begin = pl.multiple_of(step * STEP * SUB, SUB)
        rows = pl.ds(begin, STEP * SUB)
        feats = []
        for stream in range(3):
            window = as_tiles(wide_ref[stream, pl.ds(begin, (STEP + rim) * SUB), :])
            feats.append(filtered(window, taps_ref, stream, taps, STEP, True))
            feat_ref[stream, rows, :] = as_rows(feats[-1])
        mixed_ref[rows, :] = as_rows(round16(feats[1] * feats[2]))
        return carry

    lax.fori_loop(0, tokens // STEP, body, 0)
    copies = start_all(
        [
            pltpu.make_async_copy(feat_ref.at[stream], target, sems.at[stream])
            for stream, target in enumerate((qf_ref, kf_ref, vf_ref))
        ]
    )
    states = advance_states(
        mixed_ref, fades(decay_ref, 1.0), zero_states(modes), 0, tokens, False
    )
    write_messages(message_ref, states, decay_ref, position_ref, tokens, 1)
    wait_all(copies)


def scales_of(scale_ref):
    return [scale_ref[mode_rows(n), :] for n in range(scale_ref.shape[0] // SUB)]


def local_conv_kernel(signal_ref, decay_ref, scale_ref, out_ref, *, reverse):
    tokens = signal_ref.shape[0] // SUB
    factors = fades(decay_ref, 1.0)
    scales = scales_of(scale_ref)

    def body(step, states):
        for inner in range(STEP):
            token = step * STEP + inner
            token = tokens - 1 - token if reverse else token
            u = tile(signal_ref, token)
            states = [factor * state + u for factor, state in zip(factors, states)]
            out_ref[pl.ds(pl.multiple_of(token * SUB, SUB), SUB), :] = tree_sum(
                [scale * state for scale, state in zip(scales, states)]
            )
        return states

    lax.fori_loop(0, tokens // STEP, body, zero_states(len(factors)))


def add_carried(local_ref, out_ref, states, decay_ref, scale_ref, reverse):
    tokens = local_ref.shape[0] // SUB
    factors = fades(decay_ref, 1.0)
    scaled = [scale * state for scale, state in zip(scales_of(scale_ref), states)]

    def body(step, scaled):
        for inner in range(STEP):
            token = step * STEP + inner
            token = tokens - 1 - token if reverse else token
            scaled = [factor * state for factor, state in zip(factors, scaled)]
            rows = pl.ds(pl.multiple_of(token * SUB, SUB), SUB)
            out_ref[rows, :] = local_ref[rows, :] + tree_sum(list(scaled))
        return scaled

    lax.fori_loop(0, tokens // STEP, body, scaled)


def project_kernel(
    index_ref, message_ref, local_ref, decay_ref, scale_ref, _, qf_ref, weight_ref, conv_ref, *refs
):
    *out_refs, rows_ref, feat_ref, gated_ref, held_ref, sems = refs
    parts = len(out_refs)
    tokens, width = out_refs[0].shape
    copies = []
    for number in reversed(range(parts)):
        first = pl.multiple_of(index_ref[number] * width, width)
        copies.append(
            pltpu.make_async_copy(
                weight_ref.at[:, pl.ds(first, width)], held_ref.at[number], sems.at[number]
            )
        )
    feat_copy = pltpu.make_async_copy(qf_ref, feat_ref, sems.at[parts])
    feat_copy.start()
    start_all(copies)
    add_carried(local_ref, rows_ref, read_messages(message_ref), decay_ref, scale_ref, False)
    conv_copy = pltpu.make_async_copy(rows_ref, conv_ref, sems.at[parts + 1])
    conv_copy.start()
    feat_copy.wait()
    gather_tokens(
        lambda group: group_rows(rows_ref, group, tokens) * group_rows(feat_ref, group, tokens),
        gated_ref,
    )
    block = min(width, 256)
    for copy, number in zip(copies, reversed(range(parts))):
        out_ref = out_refs[number]
        copy.wait()

        def body(step, carry):
            columns = pl.ds(pl.multiple_of(step * block, block), block)
            out_ref[:, columns] = jnp.dot(
                gated_ref[...], held_ref[number, :, columns], preferred_element_type=F32
            ).astype(out_ref.dtype)
            return carry

        lax.fori_loop(0, width // block, body, 0)
    conv_copy.wait()


def add_parts_kernel(*refs):
    *part_refs, _, out_ref, held_ref, total_ref, sems, out_sems = refs
    chunks = out_sems.shape[0]
    rows = out_ref.shape[0] // chunks

    def fetch(chunk, number):
        return pltpu.make_async_copy(
            part_refs[number].at[pl.ds(chunk * rows, rows), :],
            held_ref.at[number, pl.ds(chunk * rows, rows), :],
            sems.at[chunk, number],
        )

    numbers = range(len(part_refs))
    fetches = [start_all([fetch(chunk, number) for number in numbers]) for chunk in range(chunks)]
    outs = []
    for chunk in range(chunks):
        wait_all(fetches[chunk])
        here = pl.ds(chunk * rows, rows)
        total_ref[here, :] = tree_sum(
            [held_ref[number, here, :].astype(F32) for number in numbers]
        ).astype(total_ref.dtype)
        outs.append(
            pltpu.make_async_copy(total_ref.at[here, :], out_ref.at[here, :], out_sems.at[chunk])
        )
        outs[-1].start()
    wait_all(outs)


def back_products(index_ref, piece_refs, weight_ref, turned_ref, held_ref, sems, total_ref):
    width = piece_refs[0].shape[1]
    count = len(piece_refs)

    def fetch(number):
        first = pl.multiple_of(index_ref[number] * width, width)
        return pltpu.make_async_copy(
            weight_ref.at[:, pl.ds(first, width)], held_ref.at[number], sems.at[number]
        )

    start_all([fetch(number) for number in range(count)])
    for number, ref in enumerate(piece_refs):
        turned_ref[number] = ref[...].T

    def body(number, carry):
        fetch(number).wait()
        total_ref[...] += jnp.dot(
            held_ref[number], turned_ref[number], preferred_element_type=F32
        )
        return carry

    lax.fori_loop(0, count, body, 0)


def back_part_kernel(index_ref, weight_ref, *refs):
    *piece_refs, total_ref, turned_ref, held_ref, sems = refs
    total_ref[...] = jnp.zeros_like(total_ref)
    back_products(index_ref, piece_refs, weight_ref, turned_ref, held_ref, sems, total_ref)


def back_last_kernel(
    index_ref, position_ref, weight_ref, qf_ref, kf_ref, vf_ref, conv_ref, decay_ref, *refs, rim
):
    (
        *piece_refs, base_ref, grad_ref, mixed_ref, message_ref, ahead_ref,
        turned_ref, total_ref, rows_ref, feat_ref, conv_head_ref, held_ref, sems, own_sems,
    ) = refs
    channels, tokens = total_ref.shape
    head = slice(0, rim * SUB)
    heads = pl.ds(0, rim * SUB)
    copies = start_all(
        [
            pltpu.make_async_copy(qf_ref, feat_ref, own_sems.at[0]),
            pltpu.make_async_copy(conv_ref.at[heads, :], conv_head_ref, own_sems.at[1]),
            pltpu.make_async_copy(kf_ref.at[heads, :], ahead_ref.at[2], own_sems.at[2]),
            pltpu.make_async_copy(vf_ref.at[heads, :], ahead_ref.at[3], own_sems.at[3]),
        ]
    )
    total_ref[...] = base_ref[...]
    back_products(index_ref, piece_refs, weight_ref, turned_ref, held_ref, sems, total_ref)
    scatter_tokens(rows_ref, total_ref[...].T, 0)
    grad_copy = pltpu.make_async_copy(rows_ref, grad_ref, own_sems.at[4])
    grad_copy.start()
    wait_all(copies)
    mixed_ref[...] = round16(rows_ref[...] * feat_ref[...])
    ahead_ref[0] = round16(rows_ref[head, :] * conv_head_ref[...])
    ahead_ref[1] = mixed_ref[head, :]
    modes = decay_ref.shape[0] // SUB
    states = advance_states(
        mixed_ref, fades(decay_ref, 1.0), zero_states(modes), 0, tokens, True
    )
    write_messages(message_ref, states, decay_ref, position_ref, tokens, -1)
    grad_copy.wait()


def spread_back(wide_ref, taps_ref, stream, taps, rows_ref, out_ref):
    tokens = out_ref.shape[0]

    def body(step, carry):
        first = pl.multiple_of(step * STEP * SUB, SUB)
        window = as_tiles(wide_ref[pl.ds(first, (STEP + taps - 1) * SUB), :])
        rows_ref[pl.ds(first, STEP * SUB), :] = as_rows(
            filtered(window, taps_ref, stream, taps, STEP, False)
        )
        return carry

    lax.fori_loop(0, tokens // STEP, body, 0)
    gather_tokens(lambda group: group_rows(rows_ref, group, tokens), out_ref)


def finish_query_kernel(
    grad_ref, conv_ref, ahead_ref, taps_in_ref, gq_ref,
    grad_vmem, conv_vmem, wide_ref, rows_ref, out_vmem, taps_vmem, taps_ref, sems,
):
    taps = taps_in_ref.shape[1]
    tokens = gq_ref.shape[0]
    rim = taps - 1
    copies = start_all(
        [
            pltpu.make_async_copy(taps_in_ref.at[0], taps_vmem, sems.at[0]),
            pltpu.make_async_copy(
                ahead_ref.at[0], wide_ref.at[pl.ds(tokens * SUB, rim * SUB), :], sems.at[1]
            ),
            pltpu.make_async_copy(grad_ref, grad_vmem, sems.at[2]),
            pltpu.make_async_copy(conv_ref, conv_vmem, sems.at[3]),
        ]
    )
    copies[0].wait()
    scatter_tokens(taps_ref, taps_vmem[...], 0)
    wait_all(copies[1:])
    wide_ref[pl.ds(0, tokens * SUB), :] = round16(grad_vmem[...] * conv_vmem[...])
    spread_back(wide_ref, taps_ref, 0, taps, rows_ref, out_vmem)
    out = pltpu.make_async_copy(out_vmem, gq_ref, sems.at[0])
    out.start()
    out.wait()


def finish_kernel(
    message_ref, local_ref, decay_ref, scale_ref, kf_ref, vf_ref, ahead_ref, taps_in_ref,
    gk_ref, gv_ref, total_ref, feat_ref, halo_ref, wide_ref, rows_ref, out_vmem, taps_vmem,
    taps_ref, sems,
):
    taps = taps_in_ref.shape[1]
    tokens = gk_ref.shape[0]
    rim = taps - 1
    copies = start_all(
        [
            pltpu.make_async_copy(ahead_ref, halo_ref, sems.at[0]),
            pltpu.make_async_copy(taps_in_ref, taps_vmem, sems.at[1]),
            pltpu.make_async_copy(vf_ref, feat_ref.at[0], sems.at[2]),
            pltpu.make_async_copy(kf_ref, feat_ref.at[1], sems.at[3]),
        ]
    )
    states = read_messages(message_ref)
    add_carried(local_ref, total_ref, states, decay_ref, scale_ref, True)
    wait_all(copies[:2])
    for stream in (1, 2):
        scatter_tokens(taps_ref, taps_vmem[stream], stream * taps)
    growth = fades(decay_ref, -1.0)
    scales = scales_of(scale_ref)
    for ahead in range(rim):
        rows = pl.ds((tokens + ahead) * SUB, SUB)
        theirs = pl.ds(ahead * SUB, SUB)
        grad_conv = tree_sum([scale * state for scale, state in zip(scales, states)])
        wide_ref[0, rows, :] = round16(grad_conv * halo_ref[3, theirs, :])
        wide_ref[1, rows, :] = round16(grad_conv * halo_ref[2, theirs, :])
        arrived = halo_ref[1, theirs, :]
        states = [(state - arrived) * grow for state, grow in zip(states, growth)]
    outs = []
    for number, out_ref in enumerate((gk_ref, gv_ref)):
        copies[2 + number].wait()
        wide_ref[number, pl.ds(0, tokens * SUB), :] = round16(total_ref[...] * feat_ref[number])
        spread_back(
            wide_ref.at[number], taps_ref, 1 + number, taps, rows_ref, out_vmem.at[number]
        )
        outs.append(pltpu.make_async_copy(out_vmem.at[number], out_ref, sems.at[number]))
        outs[-1].start()
    wait_all(outs)


IN_VMEM = pl.BlockSpec(memory_space=pltpu.VMEM)
IN_SMEM = pl.BlockSpec(memory_space=pltpu.SMEM)
IN_HBM = pl.BlockSpec(memory_space=pltpu.HBM)
HBM_RATE = 3.5e6


def in_hbm(shape, kind):
    return pltpu.HBM(shape, kind)


def call(kernel, outs, args, specs, scratch, name, micros, mebibytes):
    args = [
        pltpu.with_memory_space_constraint(arg, pltpu.HBM) if spec is IN_HBM else arg
        for arg, spec in zip(args, specs)
    ]
    held = [isinstance(out, tuple) for out in outs]
    return pl.pallas_call(
        kernel,
        out_shape=[jax.ShapeDtypeStruct(*out) if own else out for own, out in zip(held, outs)],
        in_specs=specs,
        out_specs=[IN_VMEM if own else IN_HBM for own in held],
        scratch_shapes=scratch,
        compiler_params=pltpu.CompilerParams(vmem_limit_bytes=mebibytes * 1024 * 1024),
        cost_estimate=pl.CostEstimate(
            flops=0, bytes_accessed=int(micros * HBM_RATE), transcendentals=0
        ),
        name=name,
    )(*args)


def shift(value, axis, steps):
    count = lax.axis_size(axis)
    pairs = [(s, s + steps) for s in range(count) if 0 <= s + steps < count]
    return lax.ppermute(value, axis, pairs)


def exchange(value, axis, mask):
    count = lax.axis_size(axis)
    return lax.ppermute(value, axis, [(s, s ^ mask) for s in range(count)])


def shards(query_in, key_in, value_in, short_taps, residues, decays, out_weight, out_grad):
    tokens, channels = query_in.shape
    taps = short_taps.shape[0]
    rim = taps - 1
    modes = decays.shape[1]
    blocks = lax.axis_size("ctx")
    fans = lax.axis_size("ch")
    position = lax.axis_index("ctx")[None].astype(jnp.int32)
    tile_shape = (tokens * SUB, LANES)
    mode_shape = (modes * SUB, LANES)
    message_shape = (blocks,) + mode_shape
    streams = (query_in, key_in, value_in)
    rim_rows = 16

    (halo,) = call(
        rim_kernel, [((3 * rim_rows, channels), BF16)], streams, [IN_HBM] * 3,
        [pltpu.SemaphoreType.DMA((3,))], "rim", 1.0, 2,
    )
    halo, out_grad = lax.optimization_barrier((halo, out_grad))
    halo = shift(halo, "ctx", 1)
    if fans == 4:
        order = lax.axis_index("ch") ^ jnp.arange(fans, dtype=jnp.int32)
        pieces = [out_grad] + [exchange(out_grad, "ch", mask) for mask in range(1, fans)]
    else:
        order = jnp.arange(fans, dtype=jnp.int32)
        everyone = lax.all_gather(out_grad, "ch", axis=0, tiled=False)
        pieces = [everyone[number] for number in range(fans)]
    tap_rows = jnp.transpose(short_taps, (1, 0, 2))
    tap_tiles = pltpu.VMEM((3 * taps * SUB, LANES), F32)
    tile = pltpu.VMEM(tile_shape, F32)
    wide_rows = (tokens + rim) * SUB

    query_feat, key_feat, value_feat, mixed, messages, scale_tiles, decay_tiles = call(
        featurize_kernel,
        [in_hbm(tile_shape, F32)] * 3
        + [(tile_shape, F32), (message_shape, BF16), (mode_shape, F32), (mode_shape, F32)],
        (position,) + streams + (tap_rows, residues.T, decays.T, halo),
        [IN_SMEM] + [IN_HBM] * 6 + [IN_VMEM],
        [
            pltpu.VMEM((3, tokens, channels), BF16),
            pltpu.VMEM((3, wide_rows, LANES), F32),
            pltpu.VMEM((3,) + tile_shape, F32),
            tap_tiles,
            pltpu.VMEM((3, taps, channels), F32),
            pltpu.VMEM((modes, channels), F32),
            pltpu.VMEM((modes, channels), F32),
            pltpu.SemaphoreType.DMA((6,)),
        ],
        "featurize", 5.0, 10,
    )
    arrived = lax.all_to_all(messages, "ctx", split_axis=0, concat_axis=0, tiled=True)
    (local,) = call(
        functools.partial(local_conv_kernel, reverse=False),
        [(tile_shape, F32)], (mixed, decay_tiles, scale_tiles), [IN_VMEM] * 3, [],
        "local_conv", 2.3, 2,
    )

    def back_scratch(count):
        return [
            pltpu.VMEM((count, channels, tokens), BF16),
            pltpu.VMEM((channels, tokens), F32),
            tile,
            tile,
            pltpu.VMEM((rim * SUB, LANES), F32),
            pltpu.VMEM((count, channels, channels), BF16),
            pltpu.SemaphoreType.DMA((count,)),
            pltpu.SemaphoreType.DMA((5,)),
        ]

    early = fans - 1
    (base,) = call(
        back_part_kernel,
        [((channels, tokens), F32)],
        (order[:early], out_weight, *pieces[:early]),
        [IN_SMEM, IN_HBM] + [IN_VMEM] * early,
        [
            pltpu.VMEM((early, channels, tokens), BF16),
            pltpu.VMEM((early, channels, channels), BF16),
            pltpu.SemaphoreType.DMA((early,)),
        ],
        "back_part", 6.0, 10,
    )
    conv_out, *partial_sums = call(
        project_kernel,
        [in_hbm(tile_shape, F32)] + [((tokens, channels), BF16)] * fans,
        (order, arrived, local, decay_tiles, scale_tiles, base, query_feat, out_weight),
        [IN_SMEM] + [IN_VMEM] * 5 + [IN_HBM] * 2,
        [
            tile,
            tile,
            pltpu.VMEM((tokens, channels), BF16),
            pltpu.VMEM((fans, channels, channels), BF16),
            pltpu.SemaphoreType.DMA((fans + 2,)),
        ],
        "project", 7.0, 16,
    )
    if fans == 4:
        parts = [
            exchange(part, "ch", mask) if mask else part for mask, part in enumerate(partial_sums)
        ]
    else:
        parts = lax.all_to_all(
            jnp.stack(partial_sums), "ch", split_axis=0, concat_axis=0, tiled=True
        )
        parts = [parts[number] for number in range(fans)]
    grad_gated, grad_mixed, back_messages, ahead = call(
        functools.partial(back_last_kernel, rim=rim),
        [in_hbm(tile_shape, F32), (tile_shape, F32), (message_shape, BF16)]
        + [((4, rim * SUB, LANES), F32)],
        (
            order[early:], position, out_weight, query_feat, key_feat, value_feat, conv_out,
            decay_tiles, *pieces[early:], base,
        ),
        [IN_SMEM] * 2 + [IN_HBM] * 5 + [IN_VMEM] * 3,
        back_scratch(fans - early),
        "back_last", 5.0, 8,
    )
    back_arrived = lax.all_to_all(back_messages, "ctx", split_axis=0, concat_axis=0, tiled=True)
    ahead = shift(ahead, "ctx", -1)
    (back_local,) = call(
        functools.partial(local_conv_kernel, reverse=True),
        [(tile_shape, F32)], (grad_mixed, decay_tiles, scale_tiles), [IN_VMEM] * 3, [],
        "back_local_conv", 2.3, 2,
    )
    (grad_query,) = call(
        finish_query_kernel,
        [in_hbm((tokens, channels), BF16)],
        (grad_gated, conv_out, ahead, tap_rows),
        [IN_HBM] * 4,
        [
            tile,
            tile,
            pltpu.VMEM((wide_rows, LANES), F32),
            tile,
            pltpu.VMEM((tokens, channels), BF16),
            pltpu.VMEM((taps, channels), F32),
            tap_tiles,
            pltpu.SemaphoreType.DMA((4,)),
        ],
        "finish_query", 2.5, 7,
    )
    grad_key, grad_value = call(
        finish_kernel,
        [in_hbm((tokens, channels), BF16)] * 2,
        (
            back_arrived, back_local, decay_tiles, scale_tiles, key_feat, value_feat, ahead,
            tap_rows,
        ),
        [IN_VMEM] * 4 + [IN_HBM] * 4,
        [
            tile,
            pltpu.VMEM((2,) + tile_shape, F32),
            pltpu.VMEM((4, rim * SUB, LANES), F32),
            pltpu.VMEM((2, wide_rows, LANES), F32),
            tile,
            pltpu.VMEM((2, tokens, channels), BF16),
            pltpu.VMEM((3, taps, channels), F32),
            tap_tiles,
            pltpu.SemaphoreType.DMA((4,)),
        ],
        "finish", 4.0, 10,
    )
    (projected,) = call(
        add_parts_kernel, [in_hbm((tokens, channels), BF16)], (*parts, grad_key),
        [IN_HBM] * (fans + 1),
        [
            pltpu.VMEM((fans, tokens, channels), BF16),
            pltpu.VMEM((tokens, channels), BF16),
            pltpu.SemaphoreType.DMA((4, fans)),
            pltpu.SemaphoreType.DMA((4,)),
        ],
        "add_parts", 1.5, 4,
    )
    return (projected, grad_query, grad_key, grad_value)


def solution(mesh):
    in_specs = (
        P("ctx", "ch"),
        P("ctx", "ch"),
        P("ctx", "ch"),
        P(None, None, "ch"),
        P("ch", None),
        P("ch", None),
        P("ch", None),
        P("ctx", "ch"),
    )
    out_specs = (P("ctx", "ch"), P("ctx", "ch"), P("ctx", "ch"), P("ctx", "ch"))
    return jax.shard_map(shards, mesh=mesh, in_specs=in_specs, out_specs=out_specs, check_vma=False)
```

```python
import functools

import jax
import jax.numpy as jnp
from jax import lax
from jax.experimental import pallas as pl
from jax.experimental.pallas import tpu as pltpu
from jax.sharding import PartitionSpec as P

SUB = 8
LANES = 128
STEP = 8
F32 = jnp.float32
BF16 = jnp.bfloat16


def as_tiles(rows):
    return rows.reshape(rows.shape[0] // SUB, SUB, LANES)


def as_rows(tiles):
    return tiles.reshape(tiles.shape[0] * SUB, LANES)


def tile(ref, token):
    return ref[pl.ds(pl.multiple_of(token * SUB, SUB), SUB), :]


def tree_sum(terms):
    while len(terms) > 1:
        terms = [
            terms[i] + terms[i + 1] if i + 1 < len(terms) else terms[i]
            for i in range(0, len(terms), 2)
        ]
    return terms[0]


def round16(value):
    return value.astype(BF16).astype(F32)


def scatter_tokens(ref, value, first_token):
    tokens, channels = value.shape
    for group in range(channels // LANES):
        ref[pl.ds(first_token * SUB + group, tokens, stride=SUB), :] = value[
            :, group * LANES : (group + 1) * LANES
        ]


def gather_tokens(rows, out_ref):
    for group in range(out_ref.shape[1] // LANES):
        out_ref[:, group * LANES : (group + 1) * LANES] = rows(group).astype(out_ref.dtype)


def group_rows(ref, group, tokens):
    return ref[pl.ds(group, tokens, stride=SUB), :]


def start_all(copies):
    for copy in copies:
        copy.start()
    return copies


def wait_all(copies):
    for copy in copies:
        copy.wait()


def advance_states(signal_ref, factors, states, first, count, reverse):
    last = signal_ref.shape[0] // SUB - 1

    def body(step, states):
        for inner in range(STEP):
            token = first + step * STEP + inner
            u = tile(signal_ref, last - token if reverse else token)
            states = [factor * state + u for factor, state in zip(factors, states)]
        return states

    return lax.fori_loop(0, count // STEP, body, states)


def zero_states(modes):
    return [jnp.zeros((SUB, LANES), F32) for _ in range(modes)]


def mode_rows(n):
    return slice(n * SUB, (n + 1) * SUB)


def fades(decay_ref, tokens):
    return [
        jnp.exp(-decay_ref[mode_rows(n), :] * tokens) for n in range(decay_ref.shape[0] // SUB)
    ]


def write_messages(out_ref, states, decay_ref, position_ref, tokens, direction):
    count = out_ref.shape[0]
    out_ref[...] = jnp.zeros_like(out_ref)
    fade = fades(decay_ref, float(tokens))
    for gap in range(count - 1):
        other = position_ref[0] + direction * (gap + 1)
        value = jnp.concatenate(states, axis=0).astype(out_ref.dtype)

        @pl.when((other >= 0) & (other < count))
        def _():
            out_ref[jnp.clip(other, 0, count - 1)] = value

        states = [state * factor for state, factor in zip(states, fade)]


def read_messages(in_ref):
    total = in_ref[0].astype(F32)
    for other in range(1, in_ref.shape[0]):
        total = total + in_ref[other].astype(F32)
    return [total[mode_rows(n)] for n in range(total.shape[0] // SUB)]


def rim_kernel(q_ref, k_ref, v_ref, out_ref, sems):
    rows = out_ref.shape[0] // 3
    copies = [
        pltpu.make_async_copy(
            source.at[pl.ds(source.shape[0] - rows, rows), :],
            out_ref.at[pl.ds(stream * rows, rows), :],
            sems.at[stream],
        )
        for stream, source in enumerate((q_ref, k_ref, v_ref))
    ]
    for copy in copies:
        copy.start()
    for copy in copies:
        copy.wait()


def filtered(window, taps_ref, stream, taps, steps, forward):
    total = None
    for tap in range(taps):
        first = taps - 1 - tap if forward else tap
        term = taps_ref[pl.ds((stream * taps + tap) * SUB, SUB), :] * window[first : first + steps]
        total = term if total is None else total + term
    return total


def featurize_kernel(
    position_ref, q_ref, k_ref, v_ref, taps_in_ref, residue_in_ref, decay_in_ref, halo_ref,
    qf_ref, kf_ref, vf_ref, mixed_ref, message_ref, scale_ref, decay_ref,
    narrow_ref, wide_ref, feat_ref, taps_ref, taps_vmem, residue_vmem, decay_vmem, sems,
):
    tokens = q_ref.shape[0]
    _, taps, _ = taps_in_ref.shape
    rim = taps - 1
    modes = decay_in_ref.shape[0]
    copies = start_all(
        [
            pltpu.make_async_copy(source, target, sems.at[number])
            for number, (source, target) in enumerate(
                (
                    (decay_in_ref, decay_vmem),
                    (residue_in_ref, residue_vmem),
                    (taps_in_ref, taps_vmem),
                    (q_ref, narrow_ref.at[0]),
                    (k_ref, narrow_ref.at[1]),
                    (v_ref, narrow_ref.at[2]),
                )
            )
        ]
    )
    held = halo_ref.shape[0] // 3
    for stream in range(3):
        behind = halo_ref[stream * held : (stream + 1) * held, :].astype(F32)
        scatter_tokens(wide_ref.at[stream], behind[held - rim :], 0)
    wait_all(copies[:3])
    decays = decay_vmem[...]
    scatter_tokens(decay_ref, decays, 0)
    scatter_tokens(scale_ref, residue_vmem[...] * jnp.sqrt(decays), 0)
    for stream in range(3):
        scatter_tokens(taps_ref, taps_vmem[stream], stream * taps)
    for stream in range(3):
        copies[3 + stream].wait()
        scatter_tokens(wide_ref.at[stream], narrow_ref[stream].astype(F32), rim)

    def body(step, carry):
        begin = pl.multiple_of(step * STEP * SUB, SUB)
        rows = pl.ds(begin, STEP * SUB)
        feats = []
        for stream in range(3):
            window = as_tiles(wide_ref[stream, pl.ds(begin, (STEP + rim) * SUB), :])
            feats.append(filtered(window, taps_ref, stream, taps, STEP, True))
            feat_ref[stream, rows, :] = as_rows(feats[-1])
        mixed_ref[rows, :] = as_rows(round16(feats[1] * feats[2]))
        return carry

    lax.fori_loop(0, tokens // STEP, body, 0)
    copies = start_all(
        [
            pltpu.make_async_copy(feat_ref.at[stream], target, sems.at[stream])
            for stream, target in enumerate((qf_ref, kf_ref, vf_ref))
        ]
    )
    states = advance_states(
        mixed_ref, fades(decay_ref, 1.0), zero_states(modes), 0, tokens, False
    )
    write_messages(message_ref, states, decay_ref, position_ref, tokens, 1)
    wait_all(copies)


def scales_of(scale_ref):
    return [scale_ref[mode_rows(n), :] for n in range(scale_ref.shape[0] // SUB)]


def local_conv(signal_ref, decay_ref, scale_ref, out_ref, reverse):
    tokens = signal_ref.shape[0] // SUB
    factors = fades(decay_ref, 1.0)
    scales = scales_of(scale_ref)

    def body(step, states):
        for inner in range(STEP):
            token = step * STEP + inner
            token = tokens - 1 - token if reverse else token
            u = tile(signal_ref, token)
            states = [factor * state + u for factor, state in zip(factors, states)]
            out_ref[pl.ds(pl.multiple_of(token * SUB, SUB), SUB), :] = tree_sum(
                [scale * state for scale, state in zip(scales, states)]
            )
        return states

    lax.fori_loop(0, tokens // STEP, body, zero_states(len(factors)))


def back_local_kernel(signal_ref, decay_ref, scale_ref, out_ref):
    local_conv(signal_ref, decay_ref, scale_ref, out_ref, True)


def add_carried(local_ref, out_ref, states, decay_ref, scale_ref, reverse):
    tokens = local_ref.shape[0] // SUB
    factors = fades(decay_ref, 1.0)
    scaled = [scale * state for scale, state in zip(scales_of(scale_ref), states)]

    def body(step, scaled):
        for inner in range(STEP):
            token = step * STEP + inner
            token = tokens - 1 - token if reverse else token
            scaled = [factor * state for factor, state in zip(factors, scaled)]
            rows = pl.ds(pl.multiple_of(token * SUB, SUB), SUB)
            out_ref[rows, :] = local_ref[rows, :] + tree_sum(list(scaled))
        return scaled

    lax.fori_loop(0, tokens // STEP, body, scaled)


def project_kernel(
    message_ref, local_ref, decay_ref, scale_ref, qf_ref, weight_ref, *refs
):
    conv_ref, out_ref, rows_ref, feat_ref, gated_ref, held_ref, sent_ref, sems, out_sems = refs[-9:]
    parts, tokens, width = sent_ref.shape
    copies = [
        pltpu.make_async_copy(
            weight_ref.at[:, pl.ds(part * width, width)], held_ref.at[part], sems.at[part]
        )
        for part in range(parts)
    ]
    outs = [
        pltpu.make_async_copy(
            sent_ref.at[part], out_ref.at[:, pl.ds(part * width, width)], out_sems.at[part]
        )
        for part in range(parts)
    ]
    feat_copy = pltpu.make_async_copy(qf_ref, feat_ref, sems.at[parts])
    feat_copy.start()
    start_all(copies)
    add_carried(local_ref, rows_ref, read_messages(message_ref), decay_ref, scale_ref, False)
    conv_copy = pltpu.make_async_copy(rows_ref, conv_ref, sems.at[parts + 1])
    conv_copy.start()
    feat_copy.wait()
    gather_tokens(
        lambda group: group_rows(rows_ref, group, tokens) * group_rows(feat_ref, group, tokens),
        gated_ref,
    )
    block = min(width, 256)
    for part in range(parts):
        copies[part].wait()

        def body(step, carry):
            columns = pl.ds(pl.multiple_of(step * block, block), block)
            sent_ref[part, :, columns] = jnp.dot(
                gated_ref[...], held_ref[part, :, columns], preferred_element_type=F32
            ).astype(sent_ref.dtype)
            return carry

        lax.fori_loop(0, width // block, body, 0)
        outs[part].start()
    conv_copy.wait()
    wait_all(outs)


def start_back(index_ref, piece_refs, weight_ref, piece_vmem, held_ref, sems):
    count = len(piece_refs)
    width = held_ref.shape[2]
    pieces = start_all(
        [
            pltpu.make_async_copy(ref, piece_vmem.at[number], sems.at[count + number])
            for number, ref in enumerate(piece_refs)
        ]
    )
    weights = [
        pltpu.make_async_copy(
            weight_ref.at[:, pl.ds(pl.multiple_of(index_ref[number] * width, width), width)],
            held_ref.at[number],
            sems.at[number],
        )
        for number in range(count)
    ]
    return pieces, start_all(weights)


def back_products(copies, piece_vmem, turned_ref, held_ref, total_ref, before_ref):
    pieces, weights = copies
    for number in range(len(pieces)):
        pieces[number].wait()
        turned_ref[number] = piece_vmem[number].T
    for number in range(len(pieces)):
        weights[number].wait()
        product = jnp.dot(held_ref[number], turned_ref[number], preferred_element_type=F32)
        earlier = before_ref if number == 0 else total_ref
        total_ref[...] = product if earlier is None else earlier[...] + product


def middle_kernel(index_ref, signal_ref, decay_ref, scale_ref, weight_ref, *refs):
    *piece_refs, local_ref, total_ref, piece_vmem, turned_ref, held_ref, sems = refs
    copies = start_back(index_ref, piece_refs, weight_ref, piece_vmem, held_ref, sems)
    local_conv(signal_ref, decay_ref, scale_ref, local_ref, False)
    back_products(copies, piece_vmem, turned_ref, held_ref, total_ref, None)


def back_last_kernel(
    index_ref, position_ref, base_ref, decay_ref, weight_ref, qf_ref, kf_ref, vf_ref, conv_ref,
    *refs, rim,
):
    (
        *piece_refs, back_query_ref, mixed_ref, message_ref, ahead_ref,
        piece_vmem, turned_ref, total_ref, rows_ref, feat_ref, conv_vmem, held_ref, sems, own_sems,
    ) = refs
    tokens = total_ref.shape[1]
    heads = pl.ds(0, rim * SUB)
    products = start_back(index_ref, piece_refs, weight_ref, piece_vmem, held_ref, sems)
    copies = start_all(
        [
            pltpu.make_async_copy(qf_ref, feat_ref, own_sems.at[0]),
            pltpu.make_async_copy(conv_ref, conv_vmem, own_sems.at[1]),
            pltpu.make_async_copy(kf_ref.at[heads, :], ahead_ref.at[2], own_sems.at[2]),
            pltpu.make_async_copy(vf_ref.at[heads, :], ahead_ref.at[3], own_sems.at[3]),
        ]
    )
    back_products(products, piece_vmem, turned_ref, held_ref, total_ref, base_ref)
    scatter_tokens(rows_ref, total_ref[...].T, 0)
    wait_all(copies)
    mixed_ref[...] = round16(rows_ref[...] * feat_ref[...])
    rows_ref[...] = round16(rows_ref[...] * conv_vmem[...])
    out = pltpu.make_async_copy(rows_ref, back_query_ref, own_sems.at[4])
    out.start()
    ahead_ref[0] = rows_ref[: rim * SUB, :]
    ahead_ref[1] = mixed_ref[: rim * SUB, :]
    modes = decay_ref.shape[0] // SUB
    states = advance_states(
        mixed_ref, fades(decay_ref, 1.0), zero_states(modes), 0, tokens, True
    )
    write_messages(message_ref, states, decay_ref, position_ref, tokens, -1)
    out.wait()


def spread_back(wide_ref, taps_ref, stream, taps, rows_ref, out_ref):
    tokens = out_ref.shape[0]

    def body(step, carry):
        first = pl.multiple_of(step * STEP * SUB, SUB)
        window = as_tiles(wide_ref[pl.ds(first, (STEP + taps - 1) * SUB), :])
        rows_ref[pl.ds(first, STEP * SUB), :] = as_rows(
            filtered(window, taps_ref, stream, taps, STEP, False)
        )
        return carry

    lax.fori_loop(0, tokens // STEP, body, 0)
    gather_tokens(lambda group: group_rows(rows_ref, group, tokens), out_ref)


def finish_query_kernel(
    back_query_ref, ahead_ref, taps_in_ref, gq_ref,
    wide_ref, rows_ref, out_vmem, taps_vmem, taps_ref, sems,
):
    taps = taps_in_ref.shape[1]
    tokens = gq_ref.shape[0]
    rim = taps - 1
    copies = start_all(
        [
            pltpu.make_async_copy(taps_in_ref.at[0], taps_vmem, sems.at[0]),
            pltpu.make_async_copy(
                ahead_ref.at[0], wide_ref.at[pl.ds(tokens * SUB, rim * SUB), :], sems.at[1]
            ),
            pltpu.make_async_copy(
                back_query_ref, wide_ref.at[pl.ds(0, tokens * SUB), :], sems.at[2]
            ),
        ]
    )
    copies[0].wait()
    scatter_tokens(taps_ref, taps_vmem[...], 0)
    wait_all(copies[1:])
    spread_back(wide_ref, taps_ref, 0, taps, rows_ref, out_vmem)
    out = pltpu.make_async_copy(out_vmem, gq_ref, sems.at[0])
    out.start()
    out.wait()


def finish_kernel(
    message_ref, local_ref, decay_ref, scale_ref, kf_ref, vf_ref, ahead_ref, taps_in_ref,
    gk_ref, gv_ref, total_ref, feat_ref, halo_ref, wide_ref, rows_ref, out_vmem, taps_vmem,
    taps_ref, sems,
):
    taps = taps_in_ref.shape[1]
    tokens = gk_ref.shape[0]
    rim = taps - 1
    copies = start_all(
        [
            pltpu.make_async_copy(ahead_ref, halo_ref, sems.at[0]),
            pltpu.make_async_copy(taps_in_ref, taps_vmem, sems.at[1]),
            pltpu.make_async_copy(vf_ref, feat_ref.at[0], sems.at[2]),
            pltpu.make_async_copy(kf_ref, feat_ref.at[1], sems.at[3]),
        ]
    )
    states = read_messages(message_ref)
    add_carried(local_ref, total_ref, states, decay_ref, scale_ref, True)
    wait_all(copies[:2])
    for stream in (1, 2):
        scatter_tokens(taps_ref, taps_vmem[stream], stream * taps)
    growth = fades(decay_ref, -1.0)
    scales = scales_of(scale_ref)
    for ahead in range(rim):
        rows = pl.ds((tokens + ahead) * SUB, SUB)
        theirs = pl.ds(ahead * SUB, SUB)
        grad_conv = tree_sum([scale * state for scale, state in zip(scales, states)])
        wide_ref[0, rows, :] = round16(grad_conv * halo_ref[3, theirs, :])
        wide_ref[1, rows, :] = round16(grad_conv * halo_ref[2, theirs, :])
        arrived = halo_ref[1, theirs, :]
        states = [(state - arrived) * grow for state, grow in zip(states, growth)]
    outs = []
    for number, out_ref in enumerate((gk_ref, gv_ref)):
        copies[2 + number].wait()
        wide_ref[number, pl.ds(0, tokens * SUB), :] = round16(total_ref[...] * feat_ref[number])
        spread_back(
            wide_ref.at[number], taps_ref, 1 + number, taps, rows_ref, out_vmem.at[number]
        )
        outs.append(pltpu.make_async_copy(out_vmem.at[number], out_ref, sems.at[number]))
        outs[-1].start()
    wait_all(outs)


IN_VMEM = pl.BlockSpec(memory_space=pltpu.VMEM)
IN_SMEM = pl.BlockSpec(memory_space=pltpu.SMEM)
IN_HBM = pl.BlockSpec(memory_space=pltpu.HBM)
HBM_RATE = 3.5e6


def in_hbm(shape, kind):
    return pltpu.HBM(shape, kind)


def call(kernel, outs, args, specs, scratch, name, micros, mebibytes):
    args = [
        pltpu.with_memory_space_constraint(arg, pltpu.HBM) if spec is IN_HBM else arg
        for arg, spec in zip(args, specs)
    ]
    held = [isinstance(out, tuple) for out in outs]
    return pl.pallas_call(
        kernel,
        out_shape=[jax.ShapeDtypeStruct(*out) if own else out for own, out in zip(held, outs)],
        in_specs=specs,
        out_specs=[IN_VMEM if own else IN_HBM for own in held],
        scratch_shapes=scratch,
        compiler_params=pltpu.CompilerParams(vmem_limit_bytes=mebibytes * 1024 * 1024),
        cost_estimate=pl.CostEstimate(
            flops=0, bytes_accessed=int(micros * HBM_RATE), transcendentals=0
        ),
        name=name,
    )(*args)


def shift(value, axis, steps):
    count = lax.axis_size(axis)
    pairs = [(s, s + steps) for s in range(count) if 0 <= s + steps < count]
    return lax.ppermute(value, axis, pairs)


def exchange(value, axis, mask):
    count = lax.axis_size(axis)
    return lax.ppermute(value, axis, [(s, s ^ mask) for s in range(count)])


def shards(query_in, key_in, value_in, short_taps, residues, decays, out_weight, out_grad):
    tokens, channels = query_in.shape
    taps = short_taps.shape[0]
    rim = taps - 1
    modes = decays.shape[1]
    blocks = lax.axis_size("ctx")
    fans = lax.axis_size("ch")
    position = lax.axis_index("ctx")[None].astype(jnp.int32)
    tile_shape = (tokens * SUB, LANES)
    mode_shape = (modes * SUB, LANES)
    message_shape = (blocks,) + mode_shape
    streams = (query_in, key_in, value_in)
    rim_rows = 16

    (halo,) = call(
        rim_kernel, [((3 * rim_rows, channels), BF16)], streams, [IN_HBM] * 3,
        [pltpu.SemaphoreType.DMA((3,))], "rim", 1.0, 2,
    )
    halo, out_grad = lax.optimization_barrier((halo, out_grad))
    halo = shift(halo, "ctx", 1)
    if fans == 4:
        order = lax.axis_index("ch") ^ jnp.arange(fans, dtype=jnp.int32)
        pieces = [out_grad] + [exchange(out_grad, "ch", mask) for mask in range(1, fans)]
    else:
        order = jnp.arange(fans, dtype=jnp.int32)
        everyone = lax.all_gather(out_grad, "ch", axis=0, tiled=False)
        pieces = [everyone[number] for number in range(fans)]
    tap_rows = jnp.transpose(short_taps, (1, 0, 2))
    tap_tiles = pltpu.VMEM((3 * taps * SUB, LANES), F32)
    tile = pltpu.VMEM(tile_shape, F32)
    wide_rows = (tokens + rim) * SUB

    query_feat, key_feat, value_feat, mixed, messages, scale_tiles, decay_tiles = call(
        featurize_kernel,
        [in_hbm(tile_shape, F32)] * 3
        + [(tile_shape, F32), (message_shape, BF16), (mode_shape, F32), (mode_shape, F32)],
        (position,) + streams + (tap_rows, residues.T, decays.T, halo),
        [IN_SMEM] + [IN_HBM] * 6 + [IN_VMEM],
        [
            pltpu.VMEM((3, tokens, channels), BF16),
            pltpu.VMEM((3, wide_rows, LANES), F32),
            pltpu.VMEM((3,) + tile_shape, F32),
            tap_tiles,
            pltpu.VMEM((3, taps, channels), F32),
            pltpu.VMEM((modes, channels), F32),
            pltpu.VMEM((modes, channels), F32),
            pltpu.SemaphoreType.DMA((6,)),
        ],
        "featurize", 5.0, 10,
    )
    arrived = lax.all_to_all(messages, "ctx", split_axis=0, concat_axis=0, tiled=True)
    early = fans // 2

    def back_scratch(count):
        return [
            pltpu.VMEM((count, tokens, channels), BF16),
            pltpu.VMEM((count, channels, tokens), BF16),
        ]

    def weight_scratch(count):
        return [
            pltpu.VMEM((count, channels, channels), BF16),
            pltpu.SemaphoreType.DMA((2 * count,)),
        ]

    local, base = call(
        middle_kernel,
        [(tile_shape, F32), ((channels, tokens), F32)],
        (order[:early], mixed, decay_tiles, scale_tiles, out_weight, *pieces[:early]),
        [IN_SMEM] + [IN_VMEM] * 3 + [IN_HBM] * (1 + early),
        back_scratch(early) + weight_scratch(early),
        "middle", 6.0, 8,
    )
    conv_out, partial_sums = call(
        project_kernel,
        [in_hbm(tile_shape, F32), in_hbm((tokens, fans * channels), BF16)],
        (arrived, local, decay_tiles, scale_tiles, query_feat, out_weight, *pieces[early:]),
        [IN_VMEM] * 4 + [IN_HBM] * (2 + fans - early),
        [
            tile,
            tile,
            pltpu.VMEM((tokens, channels), BF16),
            pltpu.VMEM((fans, channels, channels), BF16),
            pltpu.VMEM((fans, tokens, channels), BF16),
            pltpu.SemaphoreType.DMA((fans + 2,)),
            pltpu.SemaphoreType.DMA((fans,)),
        ],
        "project", 7.0, 16,
    )
    projected = lax.psum_scatter(partial_sums, "ch", scatter_dimension=1, tiled=True)
    back_query, grad_mixed, back_messages, ahead = call(
        functools.partial(back_last_kernel, rim=rim),
        [in_hbm(tile_shape, F32), (tile_shape, F32), (message_shape, BF16)]
        + [((4, rim * SUB, LANES), F32)],
        (
            order[early:], position, base, decay_tiles, out_weight, query_feat, key_feat,
            value_feat, conv_out, *pieces[early:],
        ),
        [IN_SMEM] * 2 + [IN_VMEM] * 2 + [IN_HBM] * (5 + fans - early),
        back_scratch(fans - early)
        + [pltpu.VMEM((channels, tokens), F32), tile, tile, tile]
        + weight_scratch(fans - early)
        + [pltpu.SemaphoreType.DMA((5,))],
        "back_last", 6.0, 12,
    )
    back_arrived = lax.all_to_all(back_messages, "ctx", split_axis=0, concat_axis=0, tiled=True)
    ahead = shift(ahead, "ctx", -1)
    (back_local,) = call(
        back_local_kernel,
        [(tile_shape, F32)], (grad_mixed, decay_tiles, scale_tiles), [IN_VMEM] * 3, [],
        "back_local", 2.3, 2,
    )
    (grad_query,) = call(
        finish_query_kernel,
        [in_hbm((tokens, channels), BF16)],
        (back_query, ahead, tap_rows),
        [IN_HBM] * 3,
        [
            pltpu.VMEM((wide_rows, LANES), F32),
            tile,
            pltpu.VMEM((tokens, channels), BF16),
            pltpu.VMEM((taps, channels), F32),
            tap_tiles,
            pltpu.SemaphoreType.DMA((3,)),
        ],
        "finish_query", 2.5, 5,
    )
    grad_key, grad_value = call(
        finish_kernel,
        [in_hbm((tokens, channels), BF16)] * 2,
        (
            back_arrived, back_local, decay_tiles, scale_tiles, key_feat, value_feat, ahead,
            tap_rows,
        ),
        [IN_VMEM] * 4 + [IN_HBM] * 4,
        [
            tile,
            pltpu.VMEM((2,) + tile_shape, F32),
            pltpu.VMEM((4, rim * SUB, LANES), F32),
            pltpu.VMEM((2, wide_rows, LANES), F32),
            tile,
            pltpu.VMEM((2, tokens, channels), BF16),
            pltpu.VMEM((3, taps, channels), F32),
            tap_tiles,
            pltpu.SemaphoreType.DMA((4,)),
        ],
        "finish", 4.0, 10,
    )
    return (projected, grad_query, grad_key, grad_value)


def solution(mesh):
    in_specs = (
        P("ctx", "ch"),
        P("ctx", "ch"),
        P("ctx", "ch"),
        P(None, None, "ch"),
        P("ch", None),
        P("ch", None),
        P("ch", None),
        P("ctx", "ch"),
    )
    out_specs = (P("ctx", "ch"), P("ctx", "ch"), P("ctx", "ch"), P("ctx", "ch"))
    return jax.shard_map(shards, mesh=mesh, in_specs=in_specs, out_specs=out_specs, check_vma=False)
```

```python
import functools

import jax
import jax.numpy as jnp
from jax import lax
from jax.experimental import pallas as pl
from jax.experimental.pallas import tpu as pltpu
from jax.sharding import PartitionSpec as P

SUB = 8
LANES = 128
STEP = 8
F32 = jnp.float32
BF16 = jnp.bfloat16


def as_tiles(rows):
    return rows.reshape(rows.shape[0] // SUB, SUB, LANES)


def as_rows(tiles):
    return tiles.reshape(tiles.shape[0] * SUB, LANES)


def tile(ref, token):
    return ref[pl.ds(pl.multiple_of(token * SUB, SUB), SUB), :]


def tree_sum(terms):
    while len(terms) > 1:
        terms = [
            terms[i] + terms[i + 1] if i + 1 < len(terms) else terms[i]
            for i in range(0, len(terms), 2)
        ]
    return terms[0]


def round16(value):
    return value.astype(BF16).astype(F32)


def scatter_tokens(ref, value, first_token):
    tokens, channels = value.shape
    for group in range(channels // LANES):
        ref[pl.ds(first_token * SUB + group, tokens, stride=SUB), :] = value[
            :, group * LANES : (group + 1) * LANES
        ]


def gather_tokens(rows, out_ref):
    for group in range(out_ref.shape[1] // LANES):
        out_ref[:, group * LANES : (group + 1) * LANES] = rows(group).astype(out_ref.dtype)


def group_rows(ref, group, tokens):
    return ref[pl.ds(group, tokens, stride=SUB), :]


def start_all(copies):
    for copy in copies:
        copy.start()
    return copies


def wait_all(copies):
    for copy in copies:
        copy.wait()


def advance_states(signal_ref, factors, states, first, count, reverse):
    last = signal_ref.shape[0] // SUB - 1

    def body(step, states):
        for inner in range(STEP):
            token = first + step * STEP + inner
            u = tile(signal_ref, last - token if reverse else token)
            states = [factor * state + u for factor, state in zip(factors, states)]
        return states

    return lax.fori_loop(0, count // STEP, body, states)


def zero_states(modes):
    return [jnp.zeros((SUB, LANES), F32) for _ in range(modes)]


def mode_rows(n):
    return slice(n * SUB, (n + 1) * SUB)


def fades(decay_ref, tokens):
    return [
        jnp.exp(-decay_ref[mode_rows(n), :] * tokens) for n in range(decay_ref.shape[0] // SUB)
    ]


def write_messages(out_ref, states, decay_ref, position_ref, tokens, direction):
    count = out_ref.shape[0]
    out_ref[...] = jnp.zeros_like(out_ref)
    fade = fades(decay_ref, float(tokens))
    for gap in range(count - 1):
        other = position_ref[0] + direction * (gap + 1)
        value = jnp.concatenate(states, axis=0).astype(out_ref.dtype)

        @pl.when((other >= 0) & (other < count))
        def _():
            out_ref[jnp.clip(other, 0, count - 1)] = value

        states = [state * factor for state, factor in zip(states, fade)]


def read_messages(in_ref):
    total = in_ref[0].astype(F32)
    for other in range(1, in_ref.shape[0]):
        total = total + in_ref[other].astype(F32)
    return [total[mode_rows(n)] for n in range(total.shape[0] // SUB)]


def rim_kernel(
    q_ref, k_ref, v_ref, taps_ref, residue_ref, decay_ref,
    rim_ref, streams_ref, taps_vmem, residue_vmem, decay_vmem, sems,
):
    rows = rim_ref.shape[0] // 3
    streams = (q_ref, k_ref, v_ref)
    rims = [
        pltpu.make_async_copy(
            source.at[pl.ds(source.shape[0] - rows, rows), :],
            rim_ref.at[pl.ds(stream * rows, rows), :],
            sems.at[stream],
        )
        for stream, source in enumerate(streams)
    ]
    pairs = [(source, streams_ref.at[stream]) for stream, source in enumerate(streams)]
    pairs += [(taps_ref, taps_vmem), (residue_ref, residue_vmem), (decay_ref, decay_vmem)]
    others = [
        pltpu.make_async_copy(source, target, sems.at[3 + number])
        for number, (source, target) in enumerate(pairs)
    ]
    wait_all(start_all(rims + others))


def filtered(window, taps_ref, stream, taps, steps, forward):
    total = None
    for tap in range(taps):
        first = taps - 1 - tap if forward else tap
        term = taps_ref[pl.ds((stream * taps + tap) * SUB, SUB), :] * window[first : first + steps]
        total = term if total is None else total + term
    return total


def featurize_kernel(
    position_ref, streams_ref, taps_in_ref, residue_ref, decay_in_ref, halo_ref,
    qf_ref, kf_ref, vf_ref, mixed_ref, message_ref, taps_ref, scale_ref, decay_ref,
    wide_ref, feat_ref, sems,
):
    tokens = streams_ref.shape[1]
    _, taps, _ = taps_in_ref.shape
    rim = taps - 1
    modes = decay_in_ref.shape[0]
    held = halo_ref.shape[0] // 3
    decays = decay_in_ref[...]
    scatter_tokens(decay_ref, decays, 0)
    scatter_tokens(scale_ref, residue_ref[...] * jnp.sqrt(decays), 0)
    for stream in range(3):
        scatter_tokens(taps_ref, taps_in_ref[stream], stream * taps)
        behind = halo_ref[stream * held : (stream + 1) * held, :].astype(F32)
        scatter_tokens(wide_ref.at[stream], behind[held - rim :], 0)
        scatter_tokens(wide_ref.at[stream], streams_ref[stream].astype(F32), rim)

    def body(step, carry):
        begin = pl.multiple_of(step * STEP * SUB, SUB)
        rows = pl.ds(begin, STEP * SUB)
        feats = []
        for stream in range(3):
            window = as_tiles(wide_ref[stream, pl.ds(begin, (STEP + rim) * SUB), :])
            feats.append(filtered(window, taps_ref, stream, taps, STEP, True))
            feat_ref[stream, rows, :] = as_rows(feats[-1])
        mixed_ref[rows, :] = as_rows(round16(feats[1] * feats[2]))
        return carry

    lax.fori_loop(0, tokens // STEP, body, 0)
    copies = start_all(
        [
            pltpu.make_async_copy(feat_ref.at[stream], target, sems.at[stream])
            for stream, target in enumerate((qf_ref, kf_ref, vf_ref))
        ]
    )
    states = advance_states(
        mixed_ref, fades(decay_ref, 1.0), zero_states(modes), 0, tokens, False
    )
    write_messages(message_ref, states, decay_ref, position_ref, tokens, 1)
    wait_all(copies)


def scales_of(scale_ref):
    return [scale_ref[mode_rows(n), :] for n in range(scale_ref.shape[0] // SUB)]


def local_conv(signal_ref, decay_ref, scale_ref, out_ref, reverse):
    tokens = signal_ref.shape[0] // SUB
    factors = fades(decay_ref, 1.0)
    scales = scales_of(scale_ref)

    def body(step, states):
        for inner in range(STEP):
            token = step * STEP + inner
            token = tokens - 1 - token if reverse else token
            u = tile(signal_ref, token)
            states = [factor * state + u for factor, state in zip(factors, states)]
            out_ref[pl.ds(pl.multiple_of(token * SUB, SUB), SUB), :] = tree_sum(
                [scale * state for scale, state in zip(scales, states)]
            )
        return states

    lax.fori_loop(0, tokens // STEP, body, zero_states(len(factors)))


def back_local_kernel(signal_ref, decay_ref, scale_ref, out_ref):
    local_conv(signal_ref, decay_ref, scale_ref, out_ref, True)


def add_carried(local_ref, out_ref, states, decay_ref, scale_ref, reverse):
    tokens = local_ref.shape[0] // SUB
    factors = fades(decay_ref, 1.0)
    scaled = [scale * state for scale, state in zip(scales_of(scale_ref), states)]

    def body(step, scaled):
        for inner in range(STEP):
            token = step * STEP + inner
            token = tokens - 1 - token if reverse else token
            scaled = [factor * state for factor, state in zip(factors, scaled)]
            rows = pl.ds(pl.multiple_of(token * SUB, SUB), SUB)
            out_ref[rows, :] = local_ref[rows, :] + tree_sum(list(scaled))
        return scaled

    lax.fori_loop(0, tokens // STEP, body, scaled)


def project_kernel(
    index_ref, message_ref, local_ref, decay_ref, scale_ref, _, qf_ref, weight_ref, conv_ref, *refs
):
    *out_refs, rows_ref, feat_ref, gated_ref, held_ref, sent_ref, sems, out_sems = refs
    parts, tokens, width = sent_ref.shape
    order = list(reversed(range(parts)))
    copies = [
        pltpu.make_async_copy(
            weight_ref.at[:, pl.ds(pl.multiple_of(index_ref[part] * width, width), width)],
            held_ref.at[part],
            sems.at[part],
        )
        for part in range(parts)
    ]
    outs = [
        pltpu.make_async_copy(sent_ref.at[part], out_refs[part], out_sems.at[part])
        for part in range(parts)
    ]
    feat_copy = pltpu.make_async_copy(qf_ref, feat_ref, sems.at[parts])
    feat_copy.start()
    start_all([copies[part] for part in order])
    add_carried(local_ref, rows_ref, read_messages(message_ref), decay_ref, scale_ref, False)
    conv_copy = pltpu.make_async_copy(rows_ref, conv_ref, sems.at[parts + 1])
    conv_copy.start()
    feat_copy.wait()
    gather_tokens(
        lambda group: group_rows(rows_ref, group, tokens) * group_rows(feat_ref, group, tokens),
        gated_ref,
    )
    for part in order:
        copies[part].wait()
        sent_ref[part] = jnp.dot(
            gated_ref[...], held_ref[part], preferred_element_type=F32
        ).astype(sent_ref.dtype)
        outs[part].start()
    conv_copy.wait()
    wait_all(outs)


def add_parts_kernel(*refs):
    *part_refs, _, out_ref, held_ref, total_ref, sems, out_sems = refs
    chunks = out_sems.shape[0]
    rows = out_ref.shape[0] // chunks
    numbers = range(len(part_refs))
    fetches = [
        start_all(
            [
                pltpu.make_async_copy(
                    part_refs[number].at[pl.ds(chunk * rows, rows), :],
                    held_ref.at[number, pl.ds(chunk * rows, rows), :],
                    sems.at[chunk, number],
                )
                for number in numbers
            ]
        )
        for chunk in range(chunks)
    ]
    outs = []
    for chunk in range(chunks):
        wait_all(fetches[chunk])
        here = pl.ds(chunk * rows, rows)
        total_ref[here, :] = tree_sum(
            [held_ref[number, here, :].astype(F32) for number in numbers]
        ).astype(total_ref.dtype)
        outs.append(
            pltpu.make_async_copy(total_ref.at[here, :], out_ref.at[here, :], out_sems.at[chunk])
        )
        outs[-1].start()
    wait_all(outs)


def start_weights(index_ref, weight_ref, held_ref, sems):
    count, _, width = held_ref.shape
    return start_all(
        [
            pltpu.make_async_copy(
                weight_ref.at[:, pl.ds(pl.multiple_of(index_ref[number] * width, width), width)],
                held_ref.at[number],
                sems.at[number],
            )
            for number in range(count)
        ]
    )


def back_products(weights, piece_refs, turned_ref, held_ref, total_ref, before_ref):
    for number, ref in enumerate(piece_refs):
        turned_ref[number] = ref[...].T
    for number in range(len(piece_refs)):
        weights[number].wait()
        product = jnp.dot(held_ref[number], turned_ref[number], preferred_element_type=F32)
        earlier = before_ref if number == 0 else total_ref
        total_ref[...] = product if earlier is None else earlier[...] + product


def middle_kernel(index_ref, signal_ref, decay_ref, scale_ref, weight_ref, own_ref, *refs):
    *piece_refs, local_ref, total_ref, own_vmem, turned_ref, held_ref, own_sem, sems = refs
    own = pltpu.make_async_copy(own_ref, own_vmem, own_sem)
    own.start()
    weights = start_weights(index_ref, weight_ref, held_ref, sems)
    local_conv(signal_ref, decay_ref, scale_ref, local_ref, False)
    own.wait()
    back_products(weights, [own_vmem, *piece_refs], turned_ref, held_ref, total_ref, None)


def back_last_kernel(
    index_ref, position_ref, base_ref, decay_ref, weight_ref, qf_ref, kf_ref, vf_ref, conv_ref,
    *refs, rim,
):
    (
        *piece_refs, back_query_ref, mixed_ref, message_ref, ahead_ref,
        turned_ref, total_ref, rows_ref, feat_ref, conv_vmem, held_ref, sems, own_sems,
    ) = refs
    tokens = total_ref.shape[1]
    heads = pl.ds(0, rim * SUB)
    weights = start_weights(index_ref, weight_ref, held_ref, sems)
    copies = start_all(
        [
            pltpu.make_async_copy(qf_ref, feat_ref, own_sems.at[0]),
            pltpu.make_async_copy(conv_ref, conv_vmem, own_sems.at[1]),
            pltpu.make_async_copy(kf_ref.at[heads, :], ahead_ref.at[2], own_sems.at[2]),
            pltpu.make_async_copy(vf_ref.at[heads, :], ahead_ref.at[3], own_sems.at[3]),
        ]
    )
    back_products(weights, piece_refs, turned_ref, held_ref, total_ref, base_ref)
    scatter_tokens(rows_ref, total_ref[...].T, 0)
    wait_all(copies)
    mixed_ref[...] = round16(rows_ref[...] * feat_ref[...])
    rows_ref[...] = round16(rows_ref[...] * conv_vmem[...])
    out = pltpu.make_async_copy(rows_ref, back_query_ref, own_sems.at[4])
    out.start()
    ahead_ref[0] = rows_ref[: rim * SUB, :]
    ahead_ref[1] = mixed_ref[: rim * SUB, :]
    modes = decay_ref.shape[0] // SUB
    states = advance_states(
        mixed_ref, fades(decay_ref, 1.0), zero_states(modes), 0, tokens, True
    )
    write_messages(message_ref, states, decay_ref, position_ref, tokens, -1)
    out.wait()


def spread_back(wide_ref, taps_ref, stream, taps, rows_ref, out_ref):
    tokens = out_ref.shape[0]

    def body(step, carry):
        first = pl.multiple_of(step * STEP * SUB, SUB)
        window = as_tiles(wide_ref[pl.ds(first, (STEP + taps - 1) * SUB), :])
        rows_ref[pl.ds(first, STEP * SUB), :] = as_rows(
            filtered(window, taps_ref, stream, taps, STEP, False)
        )
        return carry

    lax.fori_loop(0, tokens // STEP, body, 0)
    gather_tokens(lambda group: group_rows(rows_ref, group, tokens), out_ref)


def finish_kernel(
    message_ref, local_ref, decay_ref, scale_ref, taps_ref, ahead_ref, query_ref, kf_ref, vf_ref,
    gq_ref, gk_ref, gv_ref, total_ref, feat_ref, wide_ref, rows_ref, out_vmem, sems, *, taps,
):
    tokens = gk_ref.shape[0]
    rim = taps - 1
    inside = pl.ds(0, tokens * SUB)
    copies = start_all(
        [
            pltpu.make_async_copy(query_ref, wide_ref.at[0, inside, :], sems.at[0]),
            pltpu.make_async_copy(vf_ref, feat_ref.at[0], sems.at[1]),
            pltpu.make_async_copy(kf_ref, feat_ref.at[1], sems.at[2]),
        ]
    )
    states = read_messages(message_ref)
    add_carried(local_ref, total_ref, states, decay_ref, scale_ref, True)
    growth = fades(decay_ref, -1.0)
    scales = scales_of(scale_ref)
    for ahead in range(rim):
        rows = pl.ds((tokens + ahead) * SUB, SUB)
        theirs = pl.ds(ahead * SUB, SUB)
        grad_conv = tree_sum([scale * state for scale, state in zip(scales, states)])
        wide_ref[0, rows, :] = ahead_ref[0, theirs, :]
        wide_ref[1, rows, :] = round16(grad_conv * ahead_ref[3, theirs, :])
        wide_ref[2, rows, :] = round16(grad_conv * ahead_ref[2, theirs, :])
        arrived = ahead_ref[1, theirs, :]
        states = [(state - arrived) * grow for state, grow in zip(states, growth)]
    outs = []
    for stream, out_ref in enumerate((gq_ref, gk_ref, gv_ref)):
        copies[stream].wait()
        if stream:
            wide_ref[stream, inside, :] = round16(total_ref[...] * feat_ref[stream - 1])
        spread_back(
            wide_ref.at[stream], taps_ref, stream, taps, rows_ref, out_vmem.at[stream]
        )
        outs.append(pltpu.make_async_copy(out_vmem.at[stream], out_ref, sems.at[stream]))
        outs[-1].start()
    wait_all(outs)


IN_VMEM = pl.BlockSpec(memory_space=pltpu.VMEM)
IN_SMEM = pl.BlockSpec(memory_space=pltpu.SMEM)
IN_HBM = pl.BlockSpec(memory_space=pltpu.HBM)
HBM_RATE = 3.5e6


def in_hbm(shape, kind):
    return pltpu.HBM(shape, kind)


def call(kernel, outs, args, specs, scratch, name, micros, mebibytes):
    args = [
        pltpu.with_memory_space_constraint(arg, pltpu.HBM) if spec is IN_HBM else arg
        for arg, spec in zip(args, specs)
    ]
    held = [isinstance(out, tuple) for out in outs]
    return pl.pallas_call(
        kernel,
        out_shape=[jax.ShapeDtypeStruct(*out) if own else out for own, out in zip(held, outs)],
        in_specs=specs,
        out_specs=[IN_VMEM if own else IN_HBM for own in held],
        scratch_shapes=scratch,
        compiler_params=pltpu.CompilerParams(vmem_limit_bytes=mebibytes * 1024 * 1024),
        cost_estimate=pl.CostEstimate(
            flops=0, bytes_accessed=int(micros * HBM_RATE), transcendentals=0
        ),
        name=name,
    )(*args)


def shift(value, axis, steps):
    count = lax.axis_size(axis)
    pairs = [(s, s + steps) for s in range(count) if 0 <= s + steps < count]
    return lax.ppermute(value, axis, pairs)


def exchange(value, axis, mask):
    count = lax.axis_size(axis)
    return lax.ppermute(value, axis, [(s, s ^ mask) for s in range(count)])


def shards(query_in, key_in, value_in, short_taps, residues, decays, out_weight, out_grad):
    tokens, channels = query_in.shape
    taps = short_taps.shape[0]
    rim = taps - 1
    modes = decays.shape[1]
    blocks = lax.axis_size("ctx")
    fans = lax.axis_size("ch")
    position = lax.axis_index("ctx")[None].astype(jnp.int32)
    tile_shape = (tokens * SUB, LANES)
    mode_shape = (modes * SUB, LANES)
    message_shape = (blocks,) + mode_shape
    streams = (query_in, key_in, value_in)
    rim_rows = 16

    tap_rows = jnp.transpose(short_taps, (1, 0, 2))
    halo, narrow, taps_vmem, residues_vmem, decays_vmem = call(
        rim_kernel,
        [
            ((3 * rim_rows, channels), BF16),
            ((3, tokens, channels), BF16),
            ((3, taps, channels), F32),
            ((modes, channels), F32),
            ((modes, channels), F32),
        ],
        streams + (tap_rows, residues.T, decays.T), [IN_HBM] * 6,
        [pltpu.SemaphoreType.DMA((9,))], "rim", 1.2, 2,
    )
    halo, out_grad = lax.optimization_barrier((halo, out_grad))
    halo = shift(halo, "ctx", 1)
    if fans == 4:
        order = lax.axis_index("ch") ^ jnp.arange(fans, dtype=jnp.int32)
        near, far = exchange(out_grad, "ch", 1), exchange(out_grad, "ch", 2)
        pieces = [out_grad, near, far, exchange(near, "ch", 2)]
    else:
        order = jnp.arange(fans, dtype=jnp.int32)
        everyone = lax.all_gather(out_grad, "ch", axis=0, tiled=False)
        pieces = [everyone[number] for number in range(fans)]
    tile = pltpu.VMEM(tile_shape, F32)
    wide_rows = (tokens + rim) * SUB

    query_feat, key_feat, value_feat, mixed, messages, tap_tiles, scale_tiles, decay_tiles = call(
        featurize_kernel,
        [in_hbm(tile_shape, F32)] * 3
        + [(tile_shape, F32), (message_shape, BF16), ((3 * taps * SUB, LANES), F32)]
        + [(mode_shape, F32)] * 2,
        (position, narrow, taps_vmem, residues_vmem, decays_vmem, halo),
        [IN_SMEM] + [IN_VMEM] * 5,
        [
            pltpu.VMEM((3, wide_rows, LANES), F32),
            pltpu.VMEM((3,) + tile_shape, F32),
            pltpu.SemaphoreType.DMA((3,)),
        ],
        "featurize", 5.0, 8,
    )
    arrived = lax.all_to_all(messages, "ctx", split_axis=0, concat_axis=0, tiled=True)

    def weight_scratch(count):
        return [
            pltpu.VMEM((count, channels, channels), BF16),
            pltpu.SemaphoreType.DMA((count,)),
        ]

    early = fans - 1
    weights = weight_scratch(early)
    local, base = call(
        middle_kernel,
        [(tile_shape, F32), ((channels, tokens), F32)],
        (order[:early], mixed, decay_tiles, scale_tiles, out_weight, *pieces[:early]),
        [IN_SMEM] + [IN_VMEM] * 3 + [IN_HBM] * 2 + [IN_VMEM] * (early - 1),
        [
            pltpu.VMEM((tokens, channels), BF16),
            pltpu.VMEM((early, channels, tokens), BF16),
            weights[0],
            pltpu.SemaphoreType.DMA,
            weights[1],
        ],
        "middle", 6.0, 10,
    )
    conv_out, *partial_sums = call(
        project_kernel,
        [in_hbm(tile_shape, F32)] + [in_hbm((tokens, channels), BF16)] * fans,
        (order, arrived, local, decay_tiles, scale_tiles, base, query_feat, out_weight),
        [IN_SMEM] + [IN_VMEM] * 5 + [IN_HBM] * 2,
        [
            tile,
            tile,
            pltpu.VMEM((tokens, channels), BF16),
            pltpu.VMEM((fans, channels, channels), BF16),
            pltpu.VMEM((fans, tokens, channels), BF16),
            pltpu.SemaphoreType.DMA((fans + 2,)),
            pltpu.SemaphoreType.DMA((fans,)),
        ],
        "project", 7.0, 16,
    )
    if fans == 4:
        parts = [
            exchange(part, "ch", mask) if mask else part for mask, part in enumerate(partial_sums)
        ]
    else:
        parts = lax.all_to_all(
            jnp.stack(partial_sums), "ch", split_axis=0, concat_axis=0, tiled=True
        )
        parts = [parts[number] for number in range(fans)]
    back_query, grad_mixed, back_messages, ahead = call(
        functools.partial(back_last_kernel, rim=rim),
        [in_hbm(tile_shape, F32), (tile_shape, F32), (message_shape, BF16)]
        + [((4, rim * SUB, LANES), F32)],
        (
            order[early:], position, base, decay_tiles, out_weight, query_feat, key_feat,
            value_feat, conv_out, *pieces[early:],
        ),
        [IN_SMEM] * 2 + [IN_VMEM] * 2 + [IN_HBM] * 5 + [IN_VMEM] * (fans - early),
        [
            pltpu.VMEM((fans - early, channels, tokens), BF16),
            pltpu.VMEM((channels, tokens), F32),
            tile,
            tile,
            tile,
        ]
        + weight_scratch(fans - early)
        + [pltpu.SemaphoreType.DMA((5,))],
        "back_last", 6.0, 9,
    )
    back_arrived = lax.all_to_all(back_messages, "ctx", split_axis=0, concat_axis=0, tiled=True)
    ahead = shift(ahead, "ctx", -1)
    (back_local,) = call(
        back_local_kernel,
        [(tile_shape, F32)], (grad_mixed, decay_tiles, scale_tiles), [IN_VMEM] * 3, [],
        "back_local", 2.3, 2,
    )
    grad_query, grad_key, grad_value = call(
        functools.partial(finish_kernel, taps=taps),
        [in_hbm((tokens, channels), BF16)] * 3,
        (
            back_arrived, back_local, decay_tiles, scale_tiles, tap_tiles, ahead, back_query,
            key_feat, value_feat,
        ),
        [IN_VMEM] * 6 + [IN_HBM] * 3,
        [
            tile,
            pltpu.VMEM((2,) + tile_shape, F32),
            pltpu.VMEM((3, wide_rows, LANES), F32),
            tile,
            pltpu.VMEM((3, tokens, channels), BF16),
            pltpu.SemaphoreType.DMA((3,)),
        ],
        "finish", 5.5, 10,
    )
    (projected,) = call(
        add_parts_kernel, [in_hbm((tokens, channels), BF16)], (*parts, grad_key),
        [IN_HBM] * (fans + 1),
        [
            pltpu.VMEM((fans, tokens, channels), BF16),
            pltpu.VMEM((tokens, channels), BF16),
            pltpu.SemaphoreType.DMA((4, fans)),
            pltpu.SemaphoreType.DMA((4,)),
        ],
        "add_parts", 1.5, 4,
    )
    return (projected, grad_query, grad_key, grad_value)


def solution(mesh):
    in_specs = (
        P("ctx", "ch"),
        P("ctx", "ch"),
        P("ctx", "ch"),
        P(None, None, "ch"),
        P("ch", None),
        P("ch", None),
        P("ch", None),
        P("ctx", "ch"),
    )
    out_specs = (P("ctx", "ch"), P("ctx", "ch"), P("ctx", "ch"), P("ctx", "ch"))
    return jax.shard_map(shards, mesh=mesh, in_specs=in_specs, out_specs=out_specs, check_vma=False)
```

```python
import functools

import jax
import jax.numpy as jnp
from jax import lax
from jax.experimental import pallas as pl
from jax.experimental.pallas import tpu as pltpu
from jax.sharding import PartitionSpec as P

SUB = 8
LANES = 128
STEP = 8
F32 = jnp.float32
BF16 = jnp.bfloat16


def as_tiles(rows):
    return rows.reshape(rows.shape[0] // SUB, SUB, LANES)


def as_rows(tiles):
    return tiles.reshape(tiles.shape[0] * SUB, LANES)


def tile(ref, token):
    return ref[pl.ds(pl.multiple_of(token * SUB, SUB), SUB), :]


def tree_sum(terms):
    while len(terms) > 1:
        terms = [
            terms[i] + terms[i + 1] if i + 1 < len(terms) else terms[i]
            for i in range(0, len(terms), 2)
        ]
    return terms[0]


def round16(value):
    return value.astype(BF16).astype(F32)


def scatter_tokens(ref, value, first_token):
    tokens, channels = value.shape
    for group in range(channels // LANES):
        ref[pl.ds(first_token * SUB + group, tokens, stride=SUB), :] = value[
            :, group * LANES : (group + 1) * LANES
        ]


def gather_tokens(rows, out_ref):
    for group in range(out_ref.shape[1] // LANES):
        out_ref[:, group * LANES : (group + 1) * LANES] = rows(group).astype(out_ref.dtype)


def group_rows(ref, group, tokens):
    return ref[pl.ds(group, tokens, stride=SUB), :]


def start_all(copies):
    for copy in copies:
        copy.start()
    return copies


def wait_all(copies):
    for copy in copies:
        copy.wait()


def advance_states(signal_ref, factors, states, first, count, reverse):
    last = signal_ref.shape[0] // SUB - 1

    def body(step, states):
        for inner in range(STEP):
            token = first + step * STEP + inner
            u = tile(signal_ref, last - token if reverse else token)
            states = [factor * state + u for factor, state in zip(factors, states)]
        return states

    return lax.fori_loop(0, count // STEP, body, states)


def zero_states(modes):
    return [jnp.zeros((SUB, LANES), F32) for _ in range(modes)]


def mode_rows(n):
    return slice(n * SUB, (n + 1) * SUB)


def fades(decay_ref, tokens):
    return [
        jnp.exp(-decay_ref[mode_rows(n), :] * tokens) for n in range(decay_ref.shape[0] // SUB)
    ]


def write_messages(out_ref, states, decay_ref, position_ref, tokens, direction):
    count = out_ref.shape[0]
    out_ref[...] = jnp.zeros_like(out_ref)
    fade = fades(decay_ref, float(tokens))
    for gap in range(count - 1):
        other = position_ref[0] + direction * (gap + 1)
        value = jnp.concatenate(states, axis=0).astype(out_ref.dtype)

        @pl.when((other >= 0) & (other < count))
        def _():
            out_ref[jnp.clip(other, 0, count - 1)] = value

        states = [state * factor for state, factor in zip(states, fade)]


def read_messages(in_ref):
    total = in_ref[0].astype(F32)
    for other in range(1, in_ref.shape[0]):
        total = total + in_ref[other].astype(F32)
    return [total[mode_rows(n)] for n in range(total.shape[0] // SUB)]


def rim_kernel(
    q_ref, k_ref, v_ref, taps_ref, residue_ref, decay_ref,
    rim_ref, streams_ref, taps_vmem, residue_vmem, decay_vmem, sems,
):
    rows = rim_ref.shape[0] // 3
    streams = (q_ref, k_ref, v_ref)
    rims = [
        pltpu.make_async_copy(
            source.at[pl.ds(source.shape[0] - rows, rows), :],
            rim_ref.at[pl.ds(stream * rows, rows), :],
            sems.at[stream],
        )
        for stream, source in enumerate(streams)
    ]
    pairs = [(source, streams_ref.at[stream]) for stream, source in enumerate(streams)]
    pairs += [(taps_ref, taps_vmem), (residue_ref, residue_vmem), (decay_ref, decay_vmem)]
    others = [
        pltpu.make_async_copy(source, target, sems.at[3 + number])
        for number, (source, target) in enumerate(pairs)
    ]
    wait_all(start_all(rims + others))


def filtered(window, taps_ref, stream, taps, steps, forward):
    total = None
    for tap in range(taps):
        first = taps - 1 - tap if forward else tap
        term = taps_ref[pl.ds((stream * taps + tap) * SUB, SUB), :] * window[first : first + steps]
        total = term if total is None else total + term
    return total


def featurize_kernel(
    position_ref, streams_ref, taps_in_ref, residue_ref, decay_in_ref, halo_ref, grad_in_ref,
    qf_ref, kf_ref, vf_ref, mixed_ref, grad_copy_ref, message_ref, taps_ref, scale_ref, decay_ref,
    wide_ref, feat_ref, sems,
):
    grad_copy = pltpu.make_async_copy(grad_in_ref, grad_copy_ref, sems.at[4])
    grad_copy.start()
    tokens = streams_ref.shape[1]
    _, taps, _ = taps_in_ref.shape
    rim = taps - 1
    modes = decay_in_ref.shape[0]
    held = halo_ref.shape[0] // 3
    decays = decay_in_ref[...]
    scatter_tokens(decay_ref, decays, 0)
    scatter_tokens(scale_ref, residue_ref[...] * jnp.sqrt(decays), 0)
    for stream in range(3):
        scatter_tokens(taps_ref, taps_in_ref[stream], stream * taps)
        behind = halo_ref[stream * held : (stream + 1) * held, :].astype(F32)
        scatter_tokens(wide_ref.at[stream], behind[held - rim :], 0)
        scatter_tokens(wide_ref.at[stream], streams_ref[stream].astype(F32), rim)

    def body(step, carry):
        begin = pl.multiple_of(step * STEP * SUB, SUB)
        rows = pl.ds(begin, STEP * SUB)
        feats = []
        for stream in range(3):
            window = as_tiles(wide_ref[stream, pl.ds(begin, (STEP + rim) * SUB), :])
            feats.append(filtered(window, taps_ref, stream, taps, STEP, True))
            feat_ref[stream, rows, :] = as_rows(feats[-1])
        feat_ref[3, rows, :] = as_rows(round16(feats[1] * feats[2]))
        return carry

    lax.fori_loop(0, tokens // STEP, body, 0)
    copies = [grad_copy] + start_all(
        [
            pltpu.make_async_copy(feat_ref.at[number], target, sems.at[number])
            for number, target in enumerate((qf_ref, kf_ref, vf_ref, mixed_ref))
        ]
    )
    states = advance_states(
        feat_ref.at[3], fades(decay_ref, 1.0), zero_states(modes), 0, tokens, False
    )
    write_messages(message_ref, states, decay_ref, position_ref, tokens, 1)
    wait_all(copies)


def scales_of(scale_ref):
    return [scale_ref[mode_rows(n), :] for n in range(scale_ref.shape[0] // SUB)]


def local_conv(signal_ref, decay_ref, scale_ref, out_ref, reverse):
    tokens = signal_ref.shape[0] // SUB
    factors = fades(decay_ref, 1.0)
    scales = scales_of(scale_ref)

    def body(step, states):
        for inner in range(STEP):
            token = step * STEP + inner
            token = tokens - 1 - token if reverse else token
            u = tile(signal_ref, token)
            states = [factor * state + u for factor, state in zip(factors, states)]
            out_ref[pl.ds(pl.multiple_of(token * SUB, SUB), SUB), :] = tree_sum(
                [scale * state for scale, state in zip(scales, states)]
            )
        return states

    lax.fori_loop(0, tokens // STEP, body, zero_states(len(factors)))


def back_local_kernel(signal_ref, decay_ref, scale_ref, out_ref):
    local_conv(signal_ref, decay_ref, scale_ref, out_ref, True)


def add_carried(local_ref, out_ref, states, decay_ref, scale_ref, reverse):
    tokens = local_ref.shape[0] // SUB
    factors = fades(decay_ref, 1.0)
    scaled = [scale * state for scale, state in zip(scales_of(scale_ref), states)]

    def body(step, scaled):
        for inner in range(STEP):
            token = step * STEP + inner
            token = tokens - 1 - token if reverse else token
            scaled = [factor * state for factor, state in zip(factors, scaled)]
            rows = pl.ds(pl.multiple_of(token * SUB, SUB), SUB)
            out_ref[rows, :] = local_ref[rows, :] + tree_sum(list(scaled))
        return scaled

    lax.fori_loop(0, tokens // STEP, body, scaled)


def project_kernel(
    index_ref, message_ref, local_ref, decay_ref, scale_ref, _, qf_ref, weight_ref, conv_ref, *refs
):
    *out_refs, rows_ref, feat_ref, gated_ref, held_ref, sent_ref, sems, out_sems = refs
    parts, tokens, width = sent_ref.shape
    order = list(reversed(range(parts)))
    copies = [
        pltpu.make_async_copy(
            weight_ref.at[:, pl.ds(pl.multiple_of(index_ref[part] * width, width), width)],
            held_ref.at[part],
            sems.at[part],
        )
        for part in range(parts)
    ]
    outs = [
        pltpu.make_async_copy(sent_ref.at[part], out_refs[part], out_sems.at[part])
        for part in range(parts)
    ]
    feat_copy = pltpu.make_async_copy(qf_ref, feat_ref, sems.at[parts])
    feat_copy.start()
    start_all([copies[part] for part in order])
    add_carried(local_ref, rows_ref, read_messages(message_ref), decay_ref, scale_ref, False)
    conv_copy = pltpu.make_async_copy(rows_ref, conv_ref, sems.at[parts + 1])
    conv_copy.start()
    feat_copy.wait()
    gather_tokens(
        lambda group: group_rows(rows_ref, group, tokens) * group_rows(feat_ref, group, tokens),
        gated_ref,
    )
    for part in order:
        copies[part].wait()
        sent_ref[part] = jnp.dot(
            gated_ref[...], held_ref[part], preferred_element_type=F32
        ).astype(sent_ref.dtype)
        outs[part].start()
    conv_copy.wait()
    wait_all(outs)


def start_weights(index_ref, first, weight_ref, held_ref, sems):
    count, _, width = held_ref.shape
    return start_all(
        [
            pltpu.make_async_copy(
                weight_ref.at[
                    :, pl.ds(pl.multiple_of(index_ref[first + number] * width, width), width)
                ],
                held_ref.at[number],
                sems.at[number],
            )
            for number in range(count)
        ]
    )


def back_products(weights, piece_refs, turned_ref, held_ref, total_ref, before_ref):
    for number, ref in enumerate(piece_refs):
        turned_ref[number] = ref[...].T
    for number in range(len(piece_refs)):
        weights[number].wait()
        product = jnp.dot(held_ref[number], turned_ref[number], preferred_element_type=F32)
        earlier = before_ref if number == 0 else total_ref
        total_ref[...] = product if earlier is None else earlier[...] + product


def middle_kernel(index_ref, decay_ref, scale_ref, signal_ref, weight_ref, own_ref, *refs):
    *piece_refs, local_ref, total_ref, mixed_vmem, own_vmem, turned_ref, held_ref, own_sems, sems = refs
    mixed = pltpu.make_async_copy(signal_ref, mixed_vmem, own_sems.at[0])
    own = pltpu.make_async_copy(own_ref, own_vmem, own_sems.at[1])
    start_all([mixed, own])
    weights = start_weights(index_ref, 0, weight_ref, held_ref, sems)
    mixed.wait()
    local_conv(mixed_vmem, decay_ref, scale_ref, local_ref, False)
    own.wait()
    back_products(weights, [own_vmem, *piece_refs], turned_ref, held_ref, total_ref, None)


def back_last_kernel(
    index_ref, position_ref, base_ref, decay_ref, weight_ref, qf_ref, kf_ref, vf_ref, conv_ref,
    *refs, rim,
):
    (
        *piece_refs, back_query_ref, mixed_ref, message_ref, ahead_ref,
        turned_ref, total_ref, rows_ref, feat_ref, conv_vmem, held_ref, sems, own_sems,
    ) = refs
    tokens = total_ref.shape[1]
    heads = pl.ds(0, rim * SUB)
    weights = start_weights(
        index_ref, index_ref.shape[0] - len(piece_refs), weight_ref, held_ref, sems
    )
    copies = start_all(
        [
            pltpu.make_async_copy(qf_ref, feat_ref, own_sems.at[0]),
            pltpu.make_async_copy(conv_ref, conv_vmem, own_sems.at[1]),
            pltpu.make_async_copy(kf_ref.at[heads, :], ahead_ref.at[2], own_sems.at[2]),
            pltpu.make_async_copy(vf_ref.at[heads, :], ahead_ref.at[3], own_sems.at[3]),
        ]
    )
    back_products(weights, piece_refs, turned_ref, held_ref, total_ref, base_ref)
    scatter_tokens(rows_ref, total_ref[...].T, 0)
    wait_all(copies)
    mixed_ref[...] = round16(rows_ref[...] * feat_ref[...])
    rows_ref[...] = round16(rows_ref[...] * conv_vmem[...])
    out = pltpu.make_async_copy(rows_ref, back_query_ref, own_sems.at[4])
    out.start()
    ahead_ref[0] = rows_ref[: rim * SUB, :]
    ahead_ref[1] = mixed_ref[: rim * SUB, :]
    modes = decay_ref.shape[0] // SUB
    states = advance_states(
        mixed_ref, fades(decay_ref, 1.0), zero_states(modes), 0, tokens, True
    )
    write_messages(message_ref, states, decay_ref, position_ref, tokens, -1)
    out.wait()


def spread_back(wide_ref, taps_ref, stream, taps, rows_ref, out_ref):
    tokens = out_ref.shape[0]

    def body(step, carry):
        first = pl.multiple_of(step * STEP * SUB, SUB)
        window = as_tiles(wide_ref[pl.ds(first, (STEP + taps - 1) * SUB), :])
        rows_ref[pl.ds(first, STEP * SUB), :] = as_rows(
            filtered(window, taps_ref, stream, taps, STEP, False)
        )
        return carry

    lax.fori_loop(0, tokens // STEP, body, 0)
    gather_tokens(lambda group: group_rows(rows_ref, group, tokens), out_ref)


def finish_kernel(
    message_ref, local_ref, decay_ref, scale_ref, taps_ref, ahead_ref, query_ref, kf_ref, vf_ref,
    *refs, taps,
):
    (
        *part_refs, gq_ref, gk_ref, gv_ref, projected_ref,
        total_ref, feat_ref, wide_ref, rows_ref, out_vmem, parts_vmem, sems, part_sems,
    ) = refs
    tokens = gk_ref.shape[0]
    rim = taps - 1
    inside = pl.ds(0, tokens * SUB)
    copies = start_all(
        [
            pltpu.make_async_copy(query_ref, wide_ref.at[0, inside, :], sems.at[0]),
            pltpu.make_async_copy(vf_ref, feat_ref.at[0], sems.at[1]),
            pltpu.make_async_copy(kf_ref, feat_ref.at[1], sems.at[2]),
        ]
    )
    parts = start_all(
        [
            pltpu.make_async_copy(ref, parts_vmem.at[number], part_sems.at[number])
            for number, ref in enumerate(part_refs)
        ]
    )
    states = read_messages(message_ref)
    add_carried(local_ref, total_ref, states, decay_ref, scale_ref, True)
    growth = fades(decay_ref, -1.0)
    scales = scales_of(scale_ref)
    for ahead in range(rim):
        rows = pl.ds((tokens + ahead) * SUB, SUB)
        theirs = pl.ds(ahead * SUB, SUB)
        grad_conv = tree_sum([scale * state for scale, state in zip(scales, states)])
        wide_ref[0, rows, :] = ahead_ref[0, theirs, :]
        wide_ref[1, rows, :] = round16(grad_conv * ahead_ref[3, theirs, :])
        wide_ref[2, rows, :] = round16(grad_conv * ahead_ref[2, theirs, :])
        arrived = ahead_ref[1, theirs, :]
        states = [(state - arrived) * grow for state, grow in zip(states, growth)]
    outs = []
    for stream, out_ref in enumerate((gq_ref, gk_ref, gv_ref)):
        copies[stream].wait()
        if stream:
            wide_ref[stream, inside, :] = round16(total_ref[...] * feat_ref[stream - 1])
        spread_back(
            wide_ref.at[stream], taps_ref, stream, taps, rows_ref, out_vmem.at[stream]
        )
        outs.append(pltpu.make_async_copy(out_vmem.at[stream], out_ref, sems.at[stream]))
        outs[-1].start()
        if stream == 0:
            wait_all(parts)
            out_vmem[3] = tree_sum(
                [parts_vmem[number].astype(F32) for number in range(len(part_refs))]
            ).astype(out_vmem.dtype)
            outs.append(pltpu.make_async_copy(out_vmem.at[3], projected_ref, sems.at[3]))
            outs[-1].start()
    wait_all(outs)


IN_VMEM = pl.BlockSpec(memory_space=pltpu.VMEM)
IN_SMEM = pl.BlockSpec(memory_space=pltpu.SMEM)
IN_HBM = pl.BlockSpec(memory_space=pltpu.HBM)
HBM_RATE = 3.5e6


def in_hbm(shape, kind):
    return pltpu.HBM(shape, kind)


def call(kernel, outs, args, specs, scratch, name, micros, mebibytes):
    args = [
        pltpu.with_memory_space_constraint(arg, pltpu.HBM) if spec is IN_HBM else arg
        for arg, spec in zip(args, specs)
    ]
    held = [isinstance(out, tuple) for out in outs]
    return pl.pallas_call(
        kernel,
        out_shape=[jax.ShapeDtypeStruct(*out) if own else out for own, out in zip(held, outs)],
        in_specs=specs,
        out_specs=[IN_VMEM if own else IN_HBM for own in held],
        scratch_shapes=scratch,
        compiler_params=pltpu.CompilerParams(vmem_limit_bytes=mebibytes * 1024 * 1024),
        cost_estimate=pl.CostEstimate(
            flops=0, bytes_accessed=int(micros * HBM_RATE), transcendentals=0
        ),
        name=name,
    )(*args)


def shift(value, axis, steps):
    count = lax.axis_size(axis)
    pairs = [(s, s + steps) for s in range(count) if 0 <= s + steps < count]
    return lax.ppermute(value, axis, pairs)


def exchange(value, axis, mask):
    count = lax.axis_size(axis)
    return lax.ppermute(value, axis, [(s, s ^ mask) for s in range(count)])


def shards(query_in, key_in, value_in, short_taps, residues, decays, out_weight, out_grad):
    tokens, channels = query_in.shape
    taps = short_taps.shape[0]
    rim = taps - 1
    modes = decays.shape[1]
    blocks = lax.axis_size("ctx")
    fans = lax.axis_size("ch")
    position = lax.axis_index("ctx")[None].astype(jnp.int32)
    tile_shape = (tokens * SUB, LANES)
    mode_shape = (modes * SUB, LANES)
    message_shape = (blocks,) + mode_shape
    streams = (query_in, key_in, value_in)
    rim_rows = 16

    tap_rows = jnp.transpose(short_taps, (1, 0, 2))
    halo, narrow, taps_vmem, residues_vmem, decays_vmem = call(
        rim_kernel,
        [
            ((3 * rim_rows, channels), BF16),
            ((3, tokens, channels), BF16),
            ((3, taps, channels), F32),
            ((modes, channels), F32),
            ((modes, channels), F32),
        ],
        streams + (tap_rows, residues.T, decays.T), [IN_HBM] * 6,
        [pltpu.SemaphoreType.DMA((9,))], "rim", 1.2, 2,
    )
    halo, out_grad = lax.optimization_barrier((halo, out_grad))
    halo = shift(halo, "ctx", 1)
    if fans == 4:
        order = lax.axis_index("ch") ^ jnp.arange(fans, dtype=jnp.int32)
        pieces = [out_grad] + [exchange(out_grad, "ch", mask) for mask in range(1, fans - 1)]
    else:
        order = jnp.arange(fans, dtype=jnp.int32)
        everyone = lax.all_gather(out_grad, "ch", axis=0, tiled=False)
        pieces = [everyone[number] for number in range(fans)]
    tile = pltpu.VMEM(tile_shape, F32)
    wide_rows = (tokens + rim) * SUB

    (
        query_feat, key_feat, value_feat, mixed, grad_copy, messages,
        tap_tiles, scale_tiles, decay_tiles,
    ) = call(
        featurize_kernel,
        [in_hbm(tile_shape, F32)] * 4
        + [in_hbm((tokens, channels), BF16), (message_shape, BF16)]
        + [((3 * taps * SUB, LANES), F32), (mode_shape, F32), (mode_shape, F32)],
        (position, narrow, taps_vmem, residues_vmem, decays_vmem, halo, out_grad),
        [IN_SMEM] + [IN_VMEM] * 5 + [IN_HBM],
        [
            pltpu.VMEM((3, wide_rows, LANES), F32),
            pltpu.VMEM((4,) + tile_shape, F32),
            pltpu.SemaphoreType.DMA((5,)),
        ],
        "featurize", 5.0, 9,
    )
    if fans == 4:
        pieces.append(exchange(grad_copy, "ch", fans - 1))
    arrived = lax.all_to_all(messages, "ctx", split_axis=0, concat_axis=0, tiled=True)

    def weight_scratch(count):
        return [
            pltpu.VMEM((count, channels, channels), BF16),
            pltpu.SemaphoreType.DMA((count,)),
        ]

    early = fans - 1
    weights = weight_scratch(early)
    local, base = call(
        middle_kernel,
        [(tile_shape, F32), ((channels, tokens), F32)],
        (order, decay_tiles, scale_tiles, mixed, out_weight, *pieces[:early]),
        [IN_SMEM] + [IN_VMEM] * 2 + [IN_HBM] * 3 + [IN_VMEM] * (early - 1),
        [
            tile,
            pltpu.VMEM((tokens, channels), BF16),
            pltpu.VMEM((early, channels, tokens), BF16),
            weights[0],
            pltpu.SemaphoreType.DMA((2,)),
            weights[1],
        ],
        "middle", 7.0, 11,
    )
    conv_out, *partial_sums = call(
        project_kernel,
        [in_hbm(tile_shape, F32)] + [in_hbm((tokens, channels), BF16)] * fans,
        (order, arrived, local, decay_tiles, scale_tiles, base, query_feat, out_weight),
        [IN_SMEM] + [IN_VMEM] * 5 + [IN_HBM] * 2,
        [
            tile,
            tile,
            pltpu.VMEM((tokens, channels), BF16),
            pltpu.VMEM((fans, channels, channels), BF16),
            pltpu.VMEM((fans, tokens, channels), BF16),
            pltpu.SemaphoreType.DMA((fans + 2,)),
            pltpu.SemaphoreType.DMA((fans,)),
        ],
        "project", 7.0, 16,
    )
    if fans == 4:
        parts = [
            exchange(part, "ch", mask) if mask else part for mask, part in enumerate(partial_sums)
        ]
    else:
        parts = lax.all_to_all(
            jnp.stack(partial_sums), "ch", split_axis=0, concat_axis=0, tiled=True
        )
        parts = [parts[number] for number in range(fans)]
    back_query, grad_mixed, back_messages, ahead = call(
        functools.partial(back_last_kernel, rim=rim),
        [in_hbm(tile_shape, F32), (tile_shape, F32), (message_shape, BF16)]
        + [((4, rim * SUB, LANES), F32)],
        (
            order, position, base, decay_tiles, out_weight, query_feat, key_feat,
            value_feat, conv_out, *pieces[early:],
        ),
        [IN_SMEM] * 2 + [IN_VMEM] * 2 + [IN_HBM] * 5 + [IN_VMEM] * (fans - early),
        [
            pltpu.VMEM((fans - early, channels, tokens), BF16),
            pltpu.VMEM((channels, tokens), F32),
            tile,
            tile,
            tile,
        ]
        + weight_scratch(fans - early)
        + [pltpu.SemaphoreType.DMA((5,))],
        "back_last", 6.0, 9,
    )
    back_arrived = lax.all_to_all(back_messages, "ctx", split_axis=0, concat_axis=0, tiled=True)
    ahead = shift(ahead, "ctx", -1)
    (back_local,) = call(
        back_local_kernel,
        [(tile_shape, F32)], (grad_mixed, decay_tiles, scale_tiles), [IN_VMEM] * 3, [],
        "back_local", 2.3, 2,
    )
    grad_query, grad_key, grad_value, projected = call(
        functools.partial(finish_kernel, taps=taps),
        [in_hbm((tokens, channels), BF16)] * 4,
        (
            back_arrived, back_local, decay_tiles, scale_tiles, tap_tiles, ahead, back_query,
            key_feat, value_feat, *parts,
        ),
        [IN_VMEM] * 6 + [IN_HBM] * (3 + fans),
        [
            tile,
            pltpu.VMEM((2,) + tile_shape, F32),
            pltpu.VMEM((3, wide_rows, LANES), F32),
            tile,
            pltpu.VMEM((4, tokens, channels), BF16),
            pltpu.VMEM((fans, tokens, channels), BF16),
            pltpu.SemaphoreType.DMA((4,)),
            pltpu.SemaphoreType.DMA((fans,)),
        ],
        "finish", 6.0, 13,
    )
    return (projected, grad_query, grad_key, grad_value)


def solution(mesh):
    in_specs = (
        P("ctx", "ch"),
        P("ctx", "ch"),
        P("ctx", "ch"),
        P(None, None, "ch"),
        P("ch", None),
        P("ch", None),
        P("ch", None),
        P("ctx", "ch"),
    )
    out_specs = (P("ctx", "ch"), P("ctx", "ch"), P("ctx", "ch"), P("ctx", "ch"))
    return jax.shard_map(shards, mesh=mesh, in_specs=in_specs, out_specs=out_specs, check_vma=False)
```

```python
import functools

import jax
import jax.numpy as jnp
from jax import lax
from jax.experimental import pallas as pl
from jax.experimental.pallas import tpu as pltpu
from jax.sharding import PartitionSpec as P

SUB = 8
LANES = 128
STEP = 8
F32 = jnp.float32
BF16 = jnp.bfloat16


def as_tiles(rows):
    return rows.reshape(rows.shape[0] // SUB, SUB, LANES)


def as_rows(tiles):
    return tiles.reshape(tiles.shape[0] * SUB, LANES)


def tile(ref, token):
    return ref[pl.ds(pl.multiple_of(token * SUB, SUB), SUB), :]


def tree_sum(terms):
    while len(terms) > 1:
        terms = [
            terms[i] + terms[i + 1] if i + 1 < len(terms) else terms[i]
            for i in range(0, len(terms), 2)
        ]
    return terms[0]


def round16(value):
    return value.astype(BF16).astype(F32)


def scatter_tokens(ref, value, first_token):
    tokens, channels = value.shape
    for group in range(channels // LANES):
        ref[pl.ds(first_token * SUB + group, tokens, stride=SUB), :] = value[
            :, group * LANES : (group + 1) * LANES
        ]


def gather_tokens(rows, out_ref):
    for group in range(out_ref.shape[1] // LANES):
        out_ref[:, group * LANES : (group + 1) * LANES] = rows(group).astype(out_ref.dtype)


def group_rows(ref, group, tokens):
    return ref[pl.ds(group, tokens, stride=SUB), :]


def start_all(copies):
    for copy in copies:
        copy.start()
    return copies


def wait_all(copies):
    for copy in copies:
        copy.wait()


def advance_states(signal_ref, factors, states, first, count, reverse):
    last = signal_ref.shape[0] // SUB - 1

    def body(step, states):
        for inner in range(STEP):
            token = first + step * STEP + inner
            u = tile(signal_ref, last - token if reverse else token)
            states = [factor * state + u for factor, state in zip(factors, states)]
        return states

    return lax.fori_loop(0, count // STEP, body, states)


def zero_states(modes):
    return [jnp.zeros((SUB, LANES), F32) for _ in range(modes)]


def mode_rows(n):
    return slice(n * SUB, (n + 1) * SUB)


def fades(decay_ref, tokens):
    return [
        jnp.exp(-decay_ref[mode_rows(n), :] * tokens) for n in range(decay_ref.shape[0] // SUB)
    ]


def write_messages(out_ref, states, decay_ref, position_ref, tokens, direction):
    count = out_ref.shape[0]
    out_ref[...] = jnp.zeros_like(out_ref)
    fade = fades(decay_ref, float(tokens))
    for gap in range(count - 1):
        other = position_ref[0] + direction * (gap + 1)
        value = jnp.concatenate(states, axis=0).astype(out_ref.dtype)

        @pl.when((other >= 0) & (other < count))
        def _():
            out_ref[jnp.clip(other, 0, count - 1)] = value

        states = [state * factor for state, factor in zip(states, fade)]


def read_messages(in_ref):
    total = in_ref[0].astype(F32)
    for other in range(1, in_ref.shape[0]):
        total = total + in_ref[other].astype(F32)
    return [total[mode_rows(n)] for n in range(total.shape[0] // SUB)]


def rim_kernel(
    q_ref, k_ref, v_ref, taps_ref, residue_ref, decay_ref,
    rim_ref, streams_ref, taps_vmem, residue_vmem, decay_vmem, sems,
):
    rows = rim_ref.shape[0] // 3
    streams = (q_ref, k_ref, v_ref)
    rims = [
        pltpu.make_async_copy(
            source.at[pl.ds(source.shape[0] - rows, rows), :],
            rim_ref.at[pl.ds(stream * rows, rows), :],
            sems.at[stream],
        )
        for stream, source in enumerate(streams)
    ]
    pairs = [(source, streams_ref.at[stream]) for stream, source in enumerate(streams)]
    pairs += [(taps_ref, taps_vmem), (residue_ref, residue_vmem), (decay_ref, decay_vmem)]
    others = [
        pltpu.make_async_copy(source, target, sems.at[3 + number])
        for number, (source, target) in enumerate(pairs)
    ]
    wait_all(start_all(rims + others))


def filtered(window, taps_ref, stream, taps, steps, forward):
    total = None
    for tap in range(taps):
        first = taps - 1 - tap if forward else tap
        term = taps_ref[pl.ds((stream * taps + tap) * SUB, SUB), :] * window[first : first + steps]
        total = term if total is None else total + term
    return total


def featurize_kernel(
    position_ref, streams_ref, taps_in_ref, residue_ref, decay_in_ref, halo_ref, grad_in_ref,
    qf_ref, kf_ref, vf_ref, local_ref, grad_copy_ref, message_ref, taps_ref, scale_ref, decay_ref,
    wide_ref, feat_ref, grad_vmem, sems,
):
    grad_in = pltpu.make_async_copy(grad_in_ref, grad_vmem, sems.at[4])
    grad_in.start()
    tokens = streams_ref.shape[1]
    _, taps, _ = taps_in_ref.shape
    rim = taps - 1
    modes = decay_in_ref.shape[0]
    held = halo_ref.shape[0] // 3
    decays = decay_in_ref[...]
    scatter_tokens(decay_ref, decays, 0)
    scatter_tokens(scale_ref, residue_ref[...] * jnp.sqrt(decays), 0)
    for stream in range(3):
        scatter_tokens(taps_ref, taps_in_ref[stream], stream * taps)
        behind = halo_ref[stream * held : (stream + 1) * held, :].astype(F32)
        scatter_tokens(wide_ref.at[stream], behind[held - rim :], 0)
        scatter_tokens(wide_ref.at[stream], streams_ref[stream].astype(F32), rim)

    def body(step, carry):
        begin = pl.multiple_of(step * STEP * SUB, SUB)
        rows = pl.ds(begin, STEP * SUB)
        feats = []
        for stream in range(3):
            window = as_tiles(wide_ref[stream, pl.ds(begin, (STEP + rim) * SUB), :])
            feats.append(filtered(window, taps_ref, stream, taps, STEP, True))
            feat_ref[stream, rows, :] = as_rows(feats[-1])
        feat_ref[3, rows, :] = as_rows(round16(feats[1] * feats[2]))
        return carry

    lax.fori_loop(0, tokens // STEP, body, 0)
    grad_in.wait()
    copies = start_all(
        [
            pltpu.make_async_copy(source, target, sems.at[number])
            for number, (source, target) in enumerate(
                (
                    (feat_ref.at[0], qf_ref),
                    (feat_ref.at[1], kf_ref),
                    (feat_ref.at[2], vf_ref),
                    (grad_vmem, grad_copy_ref),
                )
            )
        ]
    )
    local_vmem = wide_ref.at[0, pl.ds(0, tokens * SUB), :]
    states = local_conv(feat_ref.at[3], decay_ref, scale_ref, local_vmem, False)
    copies += start_all([pltpu.make_async_copy(local_vmem, local_ref, sems.at[4])])
    write_messages(message_ref, states, decay_ref, position_ref, tokens, 1)
    wait_all(copies)


def scales_of(scale_ref):
    return [scale_ref[mode_rows(n), :] for n in range(scale_ref.shape[0] // SUB)]


def local_conv(signal_ref, decay_ref, scale_ref, out_ref, reverse):
    tokens = signal_ref.shape[0] // SUB
    factors = fades(decay_ref, 1.0)
    scales = scales_of(scale_ref)

    def body(step, states):
        for inner in range(STEP):
            token = step * STEP + inner
            token = tokens - 1 - token if reverse else token
            u = tile(signal_ref, token)
            states = [factor * state + u for factor, state in zip(factors, states)]
            out_ref[pl.ds(pl.multiple_of(token * SUB, SUB), SUB), :] = tree_sum(
                [scale * state for scale, state in zip(scales, states)]
            )
        return states

    return lax.fori_loop(0, tokens // STEP, body, zero_states(len(factors)))


def carried(out_ref, states, decay_ref, scale_ref, reverse, local_ref=None):
    tokens = out_ref.shape[0] // SUB
    factors = fades(decay_ref, 1.0)
    scaled = [scale * state for scale, state in zip(scales_of(scale_ref), states)]

    def body(step, scaled):
        for inner in range(STEP):
            token = step * STEP + inner
            token = tokens - 1 - token if reverse else token
            scaled = [factor * state for factor, state in zip(factors, scaled)]
            rows = pl.ds(pl.multiple_of(token * SUB, SUB), SUB)
            total = tree_sum(list(scaled))
            out_ref[rows, :] = total if local_ref is None else local_ref[rows, :] + total
        return scaled

    lax.fori_loop(0, tokens // STEP, body, scaled)


def project_kernel(
    index_ref, message_ref, decay_ref, scale_ref, _, qf_ref, local_ref, weight_ref, *refs
):
    rows_ref, feat_ref, local_vmem, gated_ref, held_ref, sent_ref, sems, out_sems = refs[-8:]
    conv_ref, *out_refs = refs[-9 - sent_ref.shape[0] : -8]
    parts, tokens, width = sent_ref.shape
    order = list(reversed(range(parts)))
    copies = [
        pltpu.make_async_copy(
            weight_ref.at[:, pl.ds(pl.multiple_of(index_ref[part] * width, width), width)],
            held_ref.at[part],
            sems.at[part],
        )
        for part in range(parts)
    ]
    outs = [
        pltpu.make_async_copy(sent_ref.at[part], out_refs[part], out_sems.at[part])
        for part in range(parts)
    ]
    local_copy = pltpu.make_async_copy(local_ref, local_vmem, sems.at[parts + 1])
    feat_copy = pltpu.make_async_copy(qf_ref, feat_ref, sems.at[parts])
    start_all([local_copy, feat_copy])
    start_all([copies[part] for part in order])
    carried(rows_ref, read_messages(message_ref), decay_ref, scale_ref, False)
    local_copy.wait()
    rows_ref[...] += local_vmem[...]
    conv_copy = pltpu.make_async_copy(rows_ref, conv_ref, sems.at[parts + 1])
    conv_copy.start()
    feat_copy.wait()
    gather_tokens(
        lambda group: group_rows(rows_ref, group, tokens) * group_rows(feat_ref, group, tokens),
        gated_ref,
    )
    for part in order:
        copies[part].wait()
        sent_ref[part] = jnp.dot(
            gated_ref[...], held_ref[part], preferred_element_type=F32
        ).astype(sent_ref.dtype)
        outs[part].start()
    conv_copy.wait()
    wait_all(outs)


def start_weights(index_ref, first, weight_ref, held_ref, sems):
    count, _, width = held_ref.shape
    return start_all(
        [
            pltpu.make_async_copy(
                weight_ref.at[
                    :, pl.ds(pl.multiple_of(index_ref[first + number] * width, width), width)
                ],
                held_ref.at[number],
                sems.at[number],
            )
            for number in range(count)
        ]
    )


def back_products(weights, piece_refs, turned_ref, held_ref, total_ref, before_ref):
    for number, ref in enumerate(piece_refs):
        turned_ref[number] = ref[...].T
    for number in range(len(piece_refs)):
        weights[number].wait()
        product = jnp.dot(held_ref[number], turned_ref[number], preferred_element_type=F32)
        earlier = before_ref if number == 0 else total_ref
        total_ref[...] = product if earlier is None else earlier[...] + product


def middle_kernel(index_ref, weight_ref, *refs):
    *piece_refs, total_ref, piece_vmem, turned_ref, held_ref, sems, piece_sems = refs
    pieces = start_all(
        [
            pltpu.make_async_copy(ref, piece_vmem.at[number], piece_sems.at[number])
            for number, ref in enumerate(piece_refs)
        ]
    )
    weights = start_weights(index_ref, 0, weight_ref, held_ref, sems)
    wait_all(pieces)
    held = [piece_vmem.at[number] for number in range(len(piece_refs))]
    back_products(weights, held, turned_ref, held_ref, total_ref, None)


def back_last_kernel(
    index_ref, position_ref, base_ref, decay_ref, weight_ref, qf_ref, kf_ref, vf_ref, conv_ref,
    *refs, rim,
):
    (
        *piece_refs, back_query_ref, mixed_ref, message_ref, ahead_ref,
        turned_ref, total_ref, rows_ref, feat_ref, conv_vmem, held_ref, sems, own_sems,
    ) = refs
    tokens = total_ref.shape[1]
    heads = pl.ds(0, rim * SUB)
    weights = start_weights(
        index_ref, index_ref.shape[0] - len(piece_refs), weight_ref, held_ref, sems
    )
    copies = start_all(
        [
            pltpu.make_async_copy(qf_ref, feat_ref, own_sems.at[0]),
            pltpu.make_async_copy(conv_ref, conv_vmem, own_sems.at[1]),
            pltpu.make_async_copy(kf_ref.at[heads, :], ahead_ref.at[2], own_sems.at[2]),
            pltpu.make_async_copy(vf_ref.at[heads, :], ahead_ref.at[3], own_sems.at[3]),
        ]
    )
    back_products(weights, piece_refs, turned_ref, held_ref, total_ref, base_ref)
    scatter_tokens(rows_ref, total_ref[...].T, 0)
    wait_all(copies)
    mixed_ref[...] = round16(rows_ref[...] * feat_ref[...])
    rows_ref[...] = round16(rows_ref[...] * conv_vmem[...])
    out = pltpu.make_async_copy(rows_ref, back_query_ref, own_sems.at[4])
    out.start()
    ahead_ref[0] = rows_ref[: rim * SUB, :]
    ahead_ref[1] = mixed_ref[: rim * SUB, :]
    modes = decay_ref.shape[0] // SUB
    states = advance_states(
        mixed_ref, fades(decay_ref, 1.0), zero_states(modes), 0, tokens, True
    )
    write_messages(message_ref, states, decay_ref, position_ref, tokens, -1)
    out.wait()


def spread_back(wide_ref, taps_ref, stream, taps, rows_ref, out_ref):
    tokens = out_ref.shape[0]

    def body(step, carry):
        first = pl.multiple_of(step * STEP * SUB, SUB)
        window = as_tiles(wide_ref[pl.ds(first, (STEP + taps - 1) * SUB), :])
        rows_ref[pl.ds(first, STEP * SUB), :] = as_rows(
            filtered(window, taps_ref, stream, taps, STEP, False)
        )
        return carry

    lax.fori_loop(0, tokens // STEP, body, 0)
    gather_tokens(lambda group: group_rows(rows_ref, group, tokens), out_ref)


def back_local_kernel(
    signal_ref, decay_ref, scale_ref, taps_ref, query_ref, local_ref, gq_ref,
    wide_ref, rows_ref, out_vmem, sem, *, taps,
):
    inside = query_ref.shape[0]
    copy = pltpu.make_async_copy(query_ref, wide_ref.at[pl.ds(0, inside), :], sem)
    copy.start()
    local_conv(signal_ref, decay_ref, scale_ref, local_ref, True)
    copy.wait()
    rest = (taps - 1) * SUB
    wide_ref[pl.ds(inside, rest), :] = jnp.zeros((rest, LANES), F32)
    spread_back(wide_ref, taps_ref, 0, taps, rows_ref, out_vmem)
    out = pltpu.make_async_copy(out_vmem, gq_ref, sem)
    out.start()
    out.wait()


def finish_kernel(
    message_ref, local_ref, decay_ref, scale_ref, taps_ref, ahead_ref, query_ref, kf_ref, vf_ref,
    *refs, taps,
):
    (
        *part_refs, _, gq_ref, gk_ref, gv_ref, projected_ref,
        total_ref, feat_ref, query_vmem, wide_ref, rows_ref, tail_ref, out_vmem, parts_vmem,
        sems, part_sems,
    ) = refs
    tokens = gk_ref.shape[0]
    tail = tail_ref.shape[0]
    rim = taps - 1
    inside = pl.ds(0, tokens * SUB)
    copies = start_all(
        [
            pltpu.make_async_copy(
                query_ref.at[pl.ds((tokens - tail) * SUB, tail * SUB), :],
                query_vmem.at[pl.ds(0, tail * SUB), :],
                sems.at[0],
            ),
            pltpu.make_async_copy(vf_ref, feat_ref.at[0], sems.at[1]),
            pltpu.make_async_copy(kf_ref, feat_ref.at[1], sems.at[2]),
        ]
    )
    parts = start_all(
        [
            pltpu.make_async_copy(ref, parts_vmem.at[number], part_sems.at[number])
            for number, ref in enumerate(part_refs)
        ]
    )
    states = read_messages(message_ref)
    carried(total_ref, states, decay_ref, scale_ref, True, local_ref)
    growth = fades(decay_ref, -1.0)
    scales = scales_of(scale_ref)
    for ahead in range(rim):
        rows = pl.ds((tokens + ahead) * SUB, SUB)
        theirs = pl.ds(ahead * SUB, SUB)
        grad_conv = tree_sum([scale * state for scale, state in zip(scales, states)])
        query_vmem[pl.ds((tail + ahead) * SUB, SUB), :] = ahead_ref[0, theirs, :]
        wide_ref[0, rows, :] = round16(grad_conv * ahead_ref[3, theirs, :])
        wide_ref[1, rows, :] = round16(grad_conv * ahead_ref[2, theirs, :])
        arrived = ahead_ref[1, theirs, :]
        states = [(state - arrived) * grow for state, grow in zip(states, growth)]
    copies[0].wait()
    spread_back(query_vmem, taps_ref, 0, taps, rows_ref, tail_ref)
    outs = [
        pltpu.make_async_copy(tail_ref, gq_ref.at[pl.ds(tokens - tail, tail), :], sems.at[0])
    ]
    wait_all(parts)
    out_vmem[2] = tree_sum(
        [parts_vmem[number].astype(F32) for number in range(len(part_refs))]
    ).astype(out_vmem.dtype)
    outs.append(pltpu.make_async_copy(out_vmem.at[2], projected_ref, sems.at[3]))
    start_all(outs)
    for stream, out_ref in enumerate((gk_ref, gv_ref)):
        copies[1 + stream].wait()
        wide_ref[stream, inside, :] = round16(total_ref[...] * feat_ref[stream])
        spread_back(
            wide_ref.at[stream], taps_ref, 1 + stream, taps, rows_ref, out_vmem.at[stream]
        )
        outs.append(pltpu.make_async_copy(out_vmem.at[stream], out_ref, sems.at[1 + stream]))
        outs[-1].start()
    wait_all(outs)


IN_VMEM = pl.BlockSpec(memory_space=pltpu.VMEM)
IN_SMEM = pl.BlockSpec(memory_space=pltpu.SMEM)
IN_HBM = pl.BlockSpec(memory_space=pltpu.HBM)
HBM_RATE = 3.5e6


def in_hbm(shape, kind):
    return pltpu.HBM(shape, kind)


def call(kernel, outs, args, specs, scratch, name, micros, mebibytes, aliases=None):
    args = [
        pltpu.with_memory_space_constraint(arg, pltpu.HBM) if spec is IN_HBM else arg
        for arg, spec in zip(args, specs)
    ]
    held = [isinstance(out, tuple) for out in outs]
    return pl.pallas_call(
        kernel,
        out_shape=[jax.ShapeDtypeStruct(*out) if own else out for own, out in zip(held, outs)],
        in_specs=specs,
        out_specs=[IN_VMEM if own else IN_HBM for own in held],
        scratch_shapes=scratch,
        compiler_params=pltpu.CompilerParams(vmem_limit_bytes=mebibytes * 1024 * 1024),
        cost_estimate=pl.CostEstimate(
            flops=0, bytes_accessed=int(micros * HBM_RATE), transcendentals=0
        ),
        name=name,
        input_output_aliases=aliases or {},
    )(*args)


def shift(value, axis, steps):
    count = lax.axis_size(axis)
    pairs = [(s, s + steps) for s in range(count) if 0 <= s + steps < count]
    return lax.ppermute(value, axis, pairs)


def exchange(value, axis, mask):
    count = lax.axis_size(axis)
    return lax.ppermute(value, axis, [(s, s ^ mask) for s in range(count)])


def shards(query_in, key_in, value_in, short_taps, residues, decays, out_weight, out_grad):
    tokens, channels = query_in.shape
    taps = short_taps.shape[0]
    rim = taps - 1
    modes = decays.shape[1]
    blocks = lax.axis_size("ctx")
    fans = lax.axis_size("ch")
    position = lax.axis_index("ctx")[None].astype(jnp.int32)
    tile_shape = (tokens * SUB, LANES)
    mode_shape = (modes * SUB, LANES)
    message_shape = (blocks,) + mode_shape
    streams = (query_in, key_in, value_in)
    rim_rows = 16

    tap_rows = jnp.transpose(short_taps, (1, 0, 2))
    halo, narrow, taps_vmem, residues_vmem, decays_vmem = call(
        rim_kernel,
        [
            ((3 * rim_rows, channels), BF16),
            ((3, tokens, channels), BF16),
            ((3, taps, channels), F32),
            ((modes, channels), F32),
            ((modes, channels), F32),
        ],
        streams + (tap_rows, residues.T, decays.T), [IN_HBM] * 6,
        [pltpu.SemaphoreType.DMA((9,))], "rim", 1.2, 2,
    )
    halo, out_grad = lax.optimization_barrier((halo, out_grad))
    halo = shift(halo, "ctx", 1)
    if fans == 4:
        order = lax.axis_index("ch") ^ jnp.arange(fans, dtype=jnp.int32)
        pieces = [out_grad] + [exchange(out_grad, "ch", mask) for mask in range(1, fans - 1)]
    else:
        order = jnp.arange(fans, dtype=jnp.int32)
        everyone = lax.all_gather(out_grad, "ch", axis=0, tiled=False)
        pieces = [everyone[number] for number in range(fans)]
    tile = pltpu.VMEM(tile_shape, F32)
    wide_rows = (tokens + rim) * SUB

    (
        query_feat, key_feat, value_feat, local, grad_copy, messages,
        tap_tiles, scale_tiles, decay_tiles,
    ) = call(
        featurize_kernel,
        [in_hbm(tile_shape, F32)] * 4
        + [in_hbm((tokens, channels), BF16), (message_shape, BF16)]
        + [((3 * taps * SUB, LANES), F32), (mode_shape, F32), (mode_shape, F32)],
        (position, narrow, taps_vmem, residues_vmem, decays_vmem, halo, out_grad),
        [IN_SMEM] + [IN_VMEM] * 5 + [IN_HBM],
        [
            pltpu.VMEM((3, wide_rows, LANES), F32),
            pltpu.VMEM((4,) + tile_shape, F32),
            pltpu.VMEM((tokens, channels), BF16),
            pltpu.SemaphoreType.DMA((5,)),
        ],
        "featurize", 6.0, 10,
    )
    if fans == 4:
        pieces.append(exchange(grad_copy, "ch", fans - 1))
    arrived = lax.all_to_all(messages, "ctx", split_axis=0, concat_axis=0, tiled=True)

    def weight_scratch(count):
        return [
            pltpu.VMEM((count, channels, channels), BF16),
            pltpu.SemaphoreType.DMA((count,)),
        ]

    early = fans - 1
    (base,) = call(
        middle_kernel,
        [((channels, tokens), F32)],
        (order, out_weight, *pieces[:early]),
        [IN_SMEM] + [IN_HBM] * (1 + early),
        [
            pltpu.VMEM((early, tokens, channels), BF16),
            pltpu.VMEM((early, channels, tokens), BF16),
        ]
        + weight_scratch(early)
        + [pltpu.SemaphoreType.DMA((early,))],
        "middle", 6.0, 11,
    )
    conv_out, *partial_sums = call(
        project_kernel,
        [in_hbm(tile_shape, F32)] + [in_hbm((tokens, channels), BF16)] * fans,
        (
            order, arrived, decay_tiles, scale_tiles, base, query_feat, local, out_weight,
            *pieces[1:early],
        ),
        [IN_SMEM] + [IN_VMEM] * 4 + [IN_HBM] * (2 + early),
        [
            tile,
            tile,
            tile,
            pltpu.VMEM((tokens, channels), BF16),
            pltpu.VMEM((fans, channels, channels), BF16),
            pltpu.VMEM((fans, tokens, channels), BF16),
            pltpu.SemaphoreType.DMA((fans + 2,)),
            pltpu.SemaphoreType.DMA((fans,)),
        ],
        "project", 7.0, 16,
    )
    if fans == 4:
        parts = [
            exchange(part, "ch", mask) if mask else part for mask, part in enumerate(partial_sums)
        ]
    else:
        parts = lax.all_to_all(
            jnp.stack(partial_sums), "ch", split_axis=0, concat_axis=0, tiled=True
        )
        parts = [parts[number] for number in range(fans)]
    back_query, grad_mixed, back_messages, ahead = call(
        functools.partial(back_last_kernel, rim=rim),
        [in_hbm(tile_shape, F32), (tile_shape, F32), (message_shape, BF16)]
        + [((4, rim * SUB, LANES), F32)],
        (
            order, position, base, decay_tiles, out_weight, query_feat, key_feat,
            value_feat, conv_out, *pieces[early:],
        ),
        [IN_SMEM] * 2 + [IN_VMEM] * 2 + [IN_HBM] * 5 + [IN_VMEM] * (fans - early),
        [
            pltpu.VMEM((fans - early, channels, tokens), BF16),
            pltpu.VMEM((channels, tokens), F32),
            tile,
            tile,
            tile,
        ]
        + weight_scratch(fans - early)
        + [pltpu.SemaphoreType.DMA((5,))],
        "back_last", 6.0, 9,
    )
    back_arrived = lax.all_to_all(back_messages, "ctx", split_axis=0, concat_axis=0, tiled=True)
    ahead = shift(ahead, "ctx", -1)
    back_local, grad_query = call(
        functools.partial(back_local_kernel, taps=taps),
        [(tile_shape, F32), in_hbm((tokens, channels), BF16)],
        (grad_mixed, decay_tiles, scale_tiles, tap_tiles, back_query),
        [IN_VMEM] * 4 + [IN_HBM],
        [
            pltpu.VMEM((wide_rows, LANES), F32),
            tile,
            pltpu.VMEM((tokens, channels), BF16),
            pltpu.SemaphoreType.DMA,
        ],
        "back_local", 4.5, 5,
    )
    tail = 16
    grad_query, grad_key, grad_value, projected = call(
        functools.partial(finish_kernel, taps=taps),
        [in_hbm((tokens, channels), BF16)] * 4,
        (
            back_arrived, back_local, decay_tiles, scale_tiles, tap_tiles, ahead, back_query,
            key_feat, value_feat, *parts, grad_query,
        ),
        [IN_VMEM] * 6 + [IN_HBM] * (4 + fans),
        [
            tile,
            pltpu.VMEM((2,) + tile_shape, F32),
            pltpu.VMEM(((tail + rim) * SUB, LANES), F32),
            pltpu.VMEM((2, wide_rows, LANES), F32),
            tile,
            pltpu.VMEM((tail, channels), BF16),
            pltpu.VMEM((3, tokens, channels), BF16),
            pltpu.VMEM((fans, tokens, channels), BF16),
            pltpu.SemaphoreType.DMA((4,)),
            pltpu.SemaphoreType.DMA((fans,)),
        ],
        "finish", 5.0, 12,
        {9 + fans: 0},
    )
    return (projected, grad_query, grad_key, grad_value)


def solution(mesh):
    in_specs = (
        P("ctx", "ch"),
        P("ctx", "ch"),
        P("ctx", "ch"),
        P(None, None, "ch"),
        P("ch", None),
        P("ch", None),
        P("ch", None),
        P("ctx", "ch"),
    )
    out_specs = (P("ctx", "ch"), P("ctx", "ch"), P("ctx", "ch"), P("ctx", "ch"))
    return jax.shard_map(shards, mesh=mesh, in_specs=in_specs, out_specs=out_specs, check_vma=False)
```

```python
import functools

import jax
import jax.numpy as jnp
from jax import lax
from jax.experimental import pallas as pl
from jax.experimental.pallas import tpu as pltpu
from jax.sharding import PartitionSpec as P

SUB = 8
LANES = 128
STEP = 8
F32 = jnp.float32
BF16 = jnp.bfloat16


def as_tiles(rows):
    return rows.reshape(rows.shape[0] // SUB, SUB, LANES)


def as_rows(tiles):
    return tiles.reshape(tiles.shape[0] * SUB, LANES)


def tile(ref, token):
    return ref[pl.ds(pl.multiple_of(token * SUB, SUB), SUB), :]


def tree_sum(terms):
    while len(terms) > 1:
        terms = [
            terms[i] + terms[i + 1] if i + 1 < len(terms) else terms[i]
            for i in range(0, len(terms), 2)
        ]
    return terms[0]


def round16(value):
    return value.astype(BF16).astype(F32)


def scatter_tokens(ref, value, first_token):
    tokens, channels = value.shape
    for group in range(channels // LANES):
        ref[pl.ds(first_token * SUB + group, tokens, stride=SUB), :] = value[
            :, group * LANES : (group + 1) * LANES
        ]


def gather_tokens(rows, out_ref):
    for group in range(out_ref.shape[1] // LANES):
        out_ref[:, group * LANES : (group + 1) * LANES] = rows(group).astype(out_ref.dtype)


def group_rows(ref, group, tokens):
    return ref[pl.ds(group, tokens, stride=SUB), :]


def start_all(copies):
    for copy in copies:
        copy.start()
    return copies


def wait_all(copies):
    for copy in copies:
        copy.wait()


def advance_states(signal_ref, factors, states, first, count, reverse):
    last = signal_ref.shape[0] // SUB - 1

    def body(step, states):
        for inner in range(STEP):
            token = first + step * STEP + inner
            u = tile(signal_ref, last - token if reverse else token)
            states = [factor * state + u for factor, state in zip(factors, states)]
        return states

    return lax.fori_loop(0, count // STEP, body, states)


def zero_states(modes):
    return [jnp.zeros((SUB, LANES), F32) for _ in range(modes)]


def mode_rows(n):
    return slice(n * SUB, (n + 1) * SUB)


def fades(decay_ref, tokens):
    return [
        jnp.exp(-decay_ref[mode_rows(n), :] * tokens) for n in range(decay_ref.shape[0] // SUB)
    ]


def write_messages(out_ref, states, decay_ref, position_ref, tokens, direction):
    count = out_ref.shape[0]
    out_ref[...] = jnp.zeros_like(out_ref)
    fade = fades(decay_ref, float(tokens))
    for gap in range(count - 1):
        other = position_ref[0] + direction * (gap + 1)
        value = jnp.concatenate(states, axis=0).astype(out_ref.dtype)

        @pl.when((other >= 0) & (other < count))
        def _():
            out_ref[jnp.clip(other, 0, count - 1)] = value

        states = [state * factor for state, factor in zip(states, fade)]


def read_messages(in_ref):
    total = in_ref[0].astype(F32)
    for other in range(1, in_ref.shape[0]):
        total = total + in_ref[other].astype(F32)
    return [total[mode_rows(n)] for n in range(total.shape[0] // SUB)]


def rim_kernel(
    q_ref, k_ref, v_ref, taps_ref, residue_ref, decay_ref,
    rim_ref, streams_ref, taps_vmem, residue_vmem, decay_vmem, sems,
):
    rows = rim_ref.shape[0] // 3
    streams = (q_ref, k_ref, v_ref)
    rims = [
        pltpu.make_async_copy(
            source.at[pl.ds(source.shape[0] - rows, rows), :],
            rim_ref.at[pl.ds(stream * rows, rows), :],
            sems.at[stream],
        )
        for stream, source in enumerate(streams)
    ]
    pairs = [(source, streams_ref.at[stream]) for stream, source in enumerate(streams)]
    pairs += [(taps_ref, taps_vmem), (residue_ref, residue_vmem), (decay_ref, decay_vmem)]
    others = [
        pltpu.make_async_copy(source, target, sems.at[3 + number])
        for number, (source, target) in enumerate(pairs)
    ]
    wait_all(start_all(rims + others))


def filtered(window, taps_ref, stream, taps, steps, forward):
    total = None
    for tap in range(taps):
        first = taps - 1 - tap if forward else tap
        term = taps_ref[pl.ds((stream * taps + tap) * SUB, SUB), :] * window[first : first + steps]
        total = term if total is None else total + term
    return total


def featurize_kernel(
    position_ref, streams_ref, taps_in_ref, residue_ref, decay_in_ref, halo_ref, grad_in_ref,
    qf_ref, kf_ref, vf_ref, local_ref, grad_copy_ref, message_ref, taps_ref, scale_ref, decay_ref,
    wide_ref, feat_ref, grad_vmem, sems,
):
    grad_in = pltpu.make_async_copy(grad_in_ref, grad_vmem, sems.at[4])
    grad_in.start()
    tokens = streams_ref.shape[1]
    _, taps, _ = taps_in_ref.shape
    rim = taps - 1
    modes = decay_in_ref.shape[0]
    held = halo_ref.shape[0] // 3
    decays = decay_in_ref[...]
    scatter_tokens(decay_ref, decays, 0)
    scatter_tokens(scale_ref, residue_ref[...] * jnp.sqrt(decays), 0)
    for stream in range(3):
        scatter_tokens(taps_ref, taps_in_ref[stream], stream * taps)
        behind = halo_ref[stream * held : (stream + 1) * held, :].astype(F32)
        scatter_tokens(wide_ref.at[stream], behind[held - rim :], 0)
        scatter_tokens(wide_ref.at[stream], streams_ref[stream].astype(F32), rim)

    def body(step, carry):
        begin = pl.multiple_of(step * STEP * SUB, SUB)
        rows = pl.ds(begin, STEP * SUB)
        feats = []
        for stream in range(3):
            window = as_tiles(wide_ref[stream, pl.ds(begin, (STEP + rim) * SUB), :])
            feats.append(filtered(window, taps_ref, stream, taps, STEP, True))
            feat_ref[stream, rows, :] = as_rows(feats[-1])
        feat_ref[3, rows, :] = as_rows(round16(feats[1] * feats[2]))
        return carry

    lax.fori_loop(0, tokens // STEP, body, 0)
    grad_in.wait()
    copies = start_all(
        [
            pltpu.make_async_copy(source, target, sems.at[number])
            for number, (source, target) in enumerate(
                (
                    (feat_ref.at[0], qf_ref),
                    (feat_ref.at[1], kf_ref),
                    (feat_ref.at[2], vf_ref),
                    (grad_vmem, grad_copy_ref),
                )
            )
        ]
    )
    local_vmem = wide_ref.at[0, pl.ds(0, tokens * SUB), :]
    states = local_conv(feat_ref.at[3], decay_ref, scale_ref, local_vmem, False)
    copies += start_all([pltpu.make_async_copy(local_vmem, local_ref, sems.at[4])])
    write_messages(message_ref, states, decay_ref, position_ref, tokens, 1)
    wait_all(copies)


def scales_of(scale_ref):
    return [scale_ref[mode_rows(n), :] for n in range(scale_ref.shape[0] // SUB)]


def local_conv(signal_ref, decay_ref, scale_ref, out_ref, reverse):
    tokens = signal_ref.shape[0] // SUB
    factors = fades(decay_ref, 1.0)
    scales = scales_of(scale_ref)

    def body(step, states):
        for inner in range(STEP):
            token = step * STEP + inner
            token = tokens - 1 - token if reverse else token
            u = tile(signal_ref, token)
            states = [factor * state + u for factor, state in zip(factors, states)]
            out_ref[pl.ds(pl.multiple_of(token * SUB, SUB), SUB), :] = tree_sum(
                [scale * state for scale, state in zip(scales, states)]
            )
        return states

    return lax.fori_loop(0, tokens // STEP, body, zero_states(len(factors)))


def carried(out_ref, states, decay_ref, scale_ref, reverse, local_ref=None):
    tokens = out_ref.shape[0] // SUB
    factors = fades(decay_ref, 1.0)
    scaled = [scale * state for scale, state in zip(scales_of(scale_ref), states)]

    def body(step, scaled):
        for inner in range(STEP):
            token = step * STEP + inner
            token = tokens - 1 - token if reverse else token
            scaled = [factor * state for factor, state in zip(factors, scaled)]
            rows = pl.ds(pl.multiple_of(token * SUB, SUB), SUB)
            total = tree_sum(list(scaled))
            out_ref[rows, :] = total if local_ref is None else local_ref[rows, :] + total
        return scaled

    lax.fori_loop(0, tokens // STEP, body, scaled)


def project_kernel(
    index_ref, message_ref, decay_ref, scale_ref, _, qf_ref, local_ref, weight_ref, *refs
):
    rows_ref, feat_ref, local_vmem, gated_ref, held_ref, sent_ref, sems, out_sems = refs[-8:]
    conv_ref, *out_refs = refs[-9 - sent_ref.shape[0] : -8]
    parts, tokens, width = sent_ref.shape
    order = list(reversed(range(parts)))
    copies = [
        pltpu.make_async_copy(
            weight_ref.at[:, pl.ds(pl.multiple_of(index_ref[part] * width, width), width)],
            held_ref.at[part],
            sems.at[part],
        )
        for part in range(parts)
    ]
    outs = [
        pltpu.make_async_copy(sent_ref.at[part], out_refs[part], out_sems.at[part])
        for part in range(parts)
    ]
    local_copy = pltpu.make_async_copy(local_ref, local_vmem, sems.at[parts + 1])
    feat_copy = pltpu.make_async_copy(qf_ref, feat_ref, sems.at[parts])
    start_all([local_copy, feat_copy])
    start_all([copies[part] for part in order])
    carried(rows_ref, read_messages(message_ref), decay_ref, scale_ref, False)
    local_copy.wait()
    rows_ref[...] += local_vmem[...]
    conv_copy = pltpu.make_async_copy(rows_ref, conv_ref, sems.at[parts + 1])
    conv_copy.start()
    feat_copy.wait()
    gather_tokens(
        lambda group: group_rows(rows_ref, group, tokens) * group_rows(feat_ref, group, tokens),
        gated_ref,
    )
    for part in order:
        copies[part].wait()
        sent_ref[part] = jnp.dot(
            gated_ref[...], held_ref[part], preferred_element_type=F32
        ).astype(sent_ref.dtype)
        outs[part].start()
    conv_copy.wait()
    wait_all(outs)


def start_weights(index_ref, first, weight_ref, held_ref, sems):
    count, _, width = held_ref.shape
    return start_all(
        [
            pltpu.make_async_copy(
                weight_ref.at[
                    :, pl.ds(pl.multiple_of(index_ref[first + number] * width, width), width)
                ],
                held_ref.at[number],
                sems.at[number],
            )
            for number in range(count)
        ]
    )


def back_products(weights, piece_refs, turned_ref, held_ref, total_ref, before_ref):
    for number, ref in enumerate(piece_refs):
        turned_ref[number] = ref[...].T
    for number in range(len(piece_refs)):
        weights[number].wait()
        product = jnp.dot(held_ref[number], turned_ref[number], preferred_element_type=F32)
        earlier = before_ref if number == 0 else total_ref
        total_ref[...] = product if earlier is None else earlier[...] + product


def middle_kernel(index_ref, weight_ref, *refs):
    *piece_refs, total_ref, piece_vmem, turned_ref, held_ref, sems, piece_sems = refs
    pieces = start_all(
        [
            pltpu.make_async_copy(ref, piece_vmem.at[number], piece_sems.at[number])
            for number, ref in enumerate(piece_refs)
        ]
    )
    weights = start_weights(index_ref, 0, weight_ref, held_ref, sems)
    wait_all(pieces)
    held = [piece_vmem.at[number] for number in range(len(piece_refs))]
    back_products(weights, held, turned_ref, held_ref, total_ref, None)


def back_last_kernel(
    index_ref, position_ref, base_ref, decay_ref, weight_ref, qf_ref, kf_ref, vf_ref, conv_ref,
    *refs, rim,
):
    (
        *piece_refs, back_query_ref, mixed_ref, message_ref, ahead_ref,
        turned_ref, total_ref, rows_ref, feat_ref, conv_vmem, held_ref, sems, own_sems,
    ) = refs
    piece_refs = piece_refs[-turned_ref.shape[0] :]
    tokens = total_ref.shape[1]
    heads = pl.ds(0, rim * SUB)
    weights = start_weights(
        index_ref, index_ref.shape[0] - len(piece_refs), weight_ref, held_ref, sems
    )
    copies = start_all(
        [
            pltpu.make_async_copy(qf_ref, feat_ref, own_sems.at[0]),
            pltpu.make_async_copy(conv_ref, conv_vmem, own_sems.at[1]),
            pltpu.make_async_copy(kf_ref.at[heads, :], ahead_ref.at[2], own_sems.at[2]),
            pltpu.make_async_copy(vf_ref.at[heads, :], ahead_ref.at[3], own_sems.at[3]),
        ]
    )
    back_products(weights, piece_refs, turned_ref, held_ref, total_ref, base_ref)
    scatter_tokens(rows_ref, total_ref[...].T, 0)
    wait_all(copies)
    mixed_ref[...] = round16(rows_ref[...] * feat_ref[...])
    rows_ref[...] = round16(rows_ref[...] * conv_vmem[...])
    out = pltpu.make_async_copy(rows_ref, back_query_ref, own_sems.at[4])
    out.start()
    ahead_ref[0] = rows_ref[: rim * SUB, :]
    ahead_ref[1] = mixed_ref[: rim * SUB, :]
    modes = decay_ref.shape[0] // SUB
    states = advance_states(
        mixed_ref, fades(decay_ref, 1.0), zero_states(modes), 0, tokens, True
    )
    write_messages(message_ref, states, decay_ref, position_ref, tokens, -1)
    out.wait()


def spread_back(wide_ref, taps_ref, stream, taps, rows_ref, out_ref):
    tokens = out_ref.shape[0]

    def body(step, carry):
        first = pl.multiple_of(step * STEP * SUB, SUB)
        window = as_tiles(wide_ref[pl.ds(first, (STEP + taps - 1) * SUB), :])
        rows_ref[pl.ds(first, STEP * SUB), :] = as_rows(
            filtered(window, taps_ref, stream, taps, STEP, False)
        )
        return carry

    lax.fori_loop(0, tokens // STEP, body, 0)
    gather_tokens(lambda group: group_rows(rows_ref, group, tokens), out_ref)


def back_local_kernel(
    signal_ref, decay_ref, scale_ref, taps_ref, query_ref, local_ref, gq_ref,
    wide_ref, rows_ref, out_vmem, sem, *, taps,
):
    inside = query_ref.shape[0]
    copy = pltpu.make_async_copy(query_ref, wide_ref.at[pl.ds(0, inside), :], sem)
    copy.start()
    local_conv(signal_ref, decay_ref, scale_ref, local_ref, True)
    copy.wait()
    rest = (taps - 1) * SUB
    wide_ref[pl.ds(inside, rest), :] = jnp.zeros((rest, LANES), F32)
    spread_back(wide_ref, taps_ref, 0, taps, rows_ref, out_vmem)
    out = pltpu.make_async_copy(out_vmem, gq_ref, sem)
    out.start()
    out.wait()


def finish_kernel(
    message_ref, local_ref, decay_ref, scale_ref, taps_ref, ahead_ref, query_ref, kf_ref, vf_ref,
    *refs, taps,
):
    (
        *part_refs, _, gq_ref, gk_ref, gv_ref, projected_ref,
        total_ref, feat_ref, query_vmem, wide_ref, rows_ref, tail_ref, out_vmem, parts_vmem,
        sems, part_sems,
    ) = refs
    tokens = gk_ref.shape[0]
    tail = tail_ref.shape[0]
    rim = taps - 1
    inside = pl.ds(0, tokens * SUB)
    copies = start_all(
        [
            pltpu.make_async_copy(
                query_ref.at[pl.ds((tokens - tail) * SUB, tail * SUB), :],
                query_vmem.at[pl.ds(0, tail * SUB), :],
                sems.at[0],
            ),
            pltpu.make_async_copy(vf_ref, feat_ref.at[0], sems.at[1]),
            pltpu.make_async_copy(kf_ref, feat_ref.at[1], sems.at[2]),
        ]
    )
    parts = start_all(
        [
            pltpu.make_async_copy(ref, parts_vmem.at[number], part_sems.at[number])
            for number, ref in enumerate(part_refs)
        ]
    )
    states = read_messages(message_ref)
    carried(total_ref, states, decay_ref, scale_ref, True, local_ref)
    growth = fades(decay_ref, -1.0)
    scales = scales_of(scale_ref)
    for ahead in range(rim):
        rows = pl.ds((tokens + ahead) * SUB, SUB)
        theirs = pl.ds(ahead * SUB, SUB)
        grad_conv = tree_sum([scale * state for scale, state in zip(scales, states)])
        query_vmem[pl.ds((tail + ahead) * SUB, SUB), :] = ahead_ref[0, theirs, :]
        wide_ref[0, rows, :] = round16(grad_conv * ahead_ref[3, theirs, :])
        wide_ref[1, rows, :] = round16(grad_conv * ahead_ref[2, theirs, :])
        arrived = ahead_ref[1, theirs, :]
        states = [(state - arrived) * grow for state, grow in zip(states, growth)]
    copies[0].wait()
    spread_back(query_vmem, taps_ref, 0, taps, rows_ref, tail_ref)
    outs = [
        pltpu.make_async_copy(tail_ref, gq_ref.at[pl.ds(tokens - tail, tail), :], sems.at[0])
    ]
    wait_all(parts)
    out_vmem[2] = tree_sum(
        [parts_vmem[number].astype(F32) for number in range(len(part_refs))]
    ).astype(out_vmem.dtype)
    outs.append(pltpu.make_async_copy(out_vmem.at[2], projected_ref, sems.at[3]))
    start_all(outs)
    for stream, out_ref in enumerate((gk_ref, gv_ref)):
        copies[1 + stream].wait()
        wide_ref[stream, inside, :] = round16(total_ref[...] * feat_ref[stream])
        spread_back(
            wide_ref.at[stream], taps_ref, 1 + stream, taps, rows_ref, out_vmem.at[stream]
        )
        outs.append(pltpu.make_async_copy(out_vmem.at[stream], out_ref, sems.at[1 + stream]))
        outs[-1].start()
    wait_all(outs)


IN_VMEM = pl.BlockSpec(memory_space=pltpu.VMEM)
IN_SMEM = pl.BlockSpec(memory_space=pltpu.SMEM)
IN_HBM = pl.BlockSpec(memory_space=pltpu.HBM)
HBM_RATE = 3.5e6


def in_hbm(shape, kind):
    return pltpu.HBM(shape, kind)


def call(kernel, outs, args, specs, scratch, name, micros, mebibytes, aliases=None):
    args = [
        pltpu.with_memory_space_constraint(arg, pltpu.HBM) if spec is IN_HBM else arg
        for arg, spec in zip(args, specs)
    ]
    held = [isinstance(out, tuple) for out in outs]
    return pl.pallas_call(
        kernel,
        out_shape=[jax.ShapeDtypeStruct(*out) if own else out for own, out in zip(held, outs)],
        in_specs=specs,
        out_specs=[IN_VMEM if own else IN_HBM for own in held],
        scratch_shapes=scratch,
        compiler_params=pltpu.CompilerParams(vmem_limit_bytes=mebibytes * 1024 * 1024),
        cost_estimate=pl.CostEstimate(
            flops=0, bytes_accessed=int(micros * HBM_RATE), transcendentals=0
        ),
        name=name,
        input_output_aliases=aliases or {},
    )(*args)


def shift(value, axis, steps):
    count = lax.axis_size(axis)
    pairs = [(s, s + steps) for s in range(count) if 0 <= s + steps < count]
    return lax.ppermute(value, axis, pairs)


def exchange(value, axis, mask):
    count = lax.axis_size(axis)
    return lax.ppermute(value, axis, [(s, s ^ mask) for s in range(count)])


def shards(query_in, key_in, value_in, short_taps, residues, decays, out_weight, out_grad):
    tokens, channels = query_in.shape
    taps = short_taps.shape[0]
    rim = taps - 1
    modes = decays.shape[1]
    blocks = lax.axis_size("ctx")
    fans = lax.axis_size("ch")
    position = lax.axis_index("ctx")[None].astype(jnp.int32)
    tile_shape = (tokens * SUB, LANES)
    mode_shape = (modes * SUB, LANES)
    message_shape = (blocks,) + mode_shape
    streams = (query_in, key_in, value_in)
    rim_rows = 16

    tap_rows = jnp.transpose(short_taps, (1, 0, 2))
    halo, narrow, taps_vmem, residues_vmem, decays_vmem = call(
        rim_kernel,
        [
            ((3 * rim_rows, channels), BF16),
            ((3, tokens, channels), BF16),
            ((3, taps, channels), F32),
            ((modes, channels), F32),
            ((modes, channels), F32),
        ],
        streams + (tap_rows, residues.T, decays.T), [IN_HBM] * 6,
        [pltpu.SemaphoreType.DMA((9,))], "rim", 1.2, 2,
    )
    halo, out_grad = lax.optimization_barrier((halo, out_grad))
    halo = shift(halo, "ctx", 1)
    if fans == 4:
        order = lax.axis_index("ch") ^ jnp.arange(fans, dtype=jnp.int32)
        pieces = [out_grad] + [exchange(out_grad, "ch", mask) for mask in range(1, fans - 1)]
    else:
        order = jnp.arange(fans, dtype=jnp.int32)
        everyone = lax.all_gather(out_grad, "ch", axis=0, tiled=False)
        pieces = [everyone[number] for number in range(fans)]
    tile = pltpu.VMEM(tile_shape, F32)
    wide_rows = (tokens + rim) * SUB

    (
        query_feat, key_feat, value_feat, local, grad_copy, messages,
        tap_tiles, scale_tiles, decay_tiles,
    ) = call(
        featurize_kernel,
        [in_hbm(tile_shape, F32)] * 4
        + [in_hbm((tokens, channels), BF16), (message_shape, BF16)]
        + [((3 * taps * SUB, LANES), F32), (mode_shape, F32), (mode_shape, F32)],
        (position, narrow, taps_vmem, residues_vmem, decays_vmem, halo, out_grad),
        [IN_SMEM] + [IN_VMEM] * 5 + [IN_HBM],
        [
            pltpu.VMEM((3, wide_rows, LANES), F32),
            pltpu.VMEM((4,) + tile_shape, F32),
            pltpu.VMEM((tokens, channels), BF16),
            pltpu.SemaphoreType.DMA((5,)),
        ],
        "featurize", 6.0, 10,
    )
    if fans == 4:
        pieces.append(exchange(grad_copy, "ch", fans - 1))
    arrived = lax.all_to_all(messages, "ctx", split_axis=0, concat_axis=0, tiled=True)

    def weight_scratch(count):
        return [
            pltpu.VMEM((count, channels, channels), BF16),
            pltpu.SemaphoreType.DMA((count,)),
        ]

    early = fans - 1
    (base,) = call(
        middle_kernel,
        [((channels, tokens), F32)],
        (order, out_weight, *pieces[:early]),
        [IN_SMEM] + [IN_HBM] * (1 + early),
        [
            pltpu.VMEM((early, tokens, channels), BF16),
            pltpu.VMEM((early, channels, tokens), BF16),
        ]
        + weight_scratch(early)
        + [pltpu.SemaphoreType.DMA((early,))],
        "middle", 6.0, 11,
    )
    conv_out, *partial_sums = call(
        project_kernel,
        [in_hbm(tile_shape, F32)] + [in_hbm((tokens, channels), BF16)] * fans,
        (
            order, arrived, decay_tiles, scale_tiles, base, query_feat, local, out_weight,
            *pieces[1:early],
        ),
        [IN_SMEM] + [IN_VMEM] * 4 + [IN_HBM] * (2 + early),
        [
            tile,
            tile,
            tile,
            pltpu.VMEM((tokens, channels), BF16),
            pltpu.VMEM((fans, channels, channels), BF16),
            pltpu.VMEM((fans, tokens, channels), BF16),
            pltpu.SemaphoreType.DMA((fans + 2,)),
            pltpu.SemaphoreType.DMA((fans,)),
        ],
        "project", 7.0, 16,
    )
    if fans == 4:
        parts = [exchange(partial_sums[mask], "ch", mask) for mask in reversed(range(1, fans))]
        parts.append(partial_sums[0])
    else:
        parts = lax.all_to_all(
            jnp.stack(partial_sums), "ch", split_axis=0, concat_axis=0, tiled=True
        )
        parts = [parts[number] for number in range(fans)]
    back_query, grad_mixed, back_messages, ahead = call(
        functools.partial(back_last_kernel, rim=rim),
        [in_hbm(tile_shape, F32), (tile_shape, F32), (message_shape, BF16)]
        + [((4, rim * SUB, LANES), F32)],
        (
            order, position, base, decay_tiles, out_weight, query_feat, key_feat,
            value_feat, conv_out, *pieces[1:early], *pieces[early:],
        ),
        [IN_SMEM] * 2 + [IN_VMEM] * 2 + [IN_HBM] * (4 + early) + [IN_VMEM] * (fans - early),
        [
            pltpu.VMEM((fans - early, channels, tokens), BF16),
            pltpu.VMEM((channels, tokens), F32),
            tile,
            tile,
            tile,
        ]
        + weight_scratch(fans - early)
        + [pltpu.SemaphoreType.DMA((5,))],
        "back_last", 6.0, 9,
    )
    back_arrived = lax.all_to_all(back_messages, "ctx", split_axis=0, concat_axis=0, tiled=True)
    ahead = shift(ahead, "ctx", -1)
    back_local, grad_query = call(
        functools.partial(back_local_kernel, taps=taps),
        [(tile_shape, F32), in_hbm((tokens, channels), BF16)],
        (grad_mixed, decay_tiles, scale_tiles, tap_tiles, back_query),
        [IN_VMEM] * 4 + [IN_HBM],
        [
            pltpu.VMEM((wide_rows, LANES), F32),
            tile,
            pltpu.VMEM((tokens, channels), BF16),
            pltpu.SemaphoreType.DMA,
        ],
        "back_local", 4.5, 5,
    )
    tail = 16
    grad_query, grad_key, grad_value, projected = call(
        functools.partial(finish_kernel, taps=taps),
        [in_hbm((tokens, channels), BF16)] * 4,
        (
            back_arrived, back_local, decay_tiles, scale_tiles, tap_tiles, ahead, back_query,
            key_feat, value_feat, *parts, grad_query,
        ),
        [IN_VMEM] * 6 + [IN_HBM] * (4 + fans),
        [
            tile,
            pltpu.VMEM((2,) + tile_shape, F32),
            pltpu.VMEM(((tail + rim) * SUB, LANES), F32),
            pltpu.VMEM((2, wide_rows, LANES), F32),
            tile,
            pltpu.VMEM((tail, channels), BF16),
            pltpu.VMEM((3, tokens, channels), BF16),
            pltpu.VMEM((fans, tokens, channels), BF16),
            pltpu.SemaphoreType.DMA((4,)),
            pltpu.SemaphoreType.DMA((fans,)),
        ],
        "finish", 5.0, 12,
        {9 + fans: 0},
    )
    return (projected, grad_query, grad_key, grad_value)


def solution(mesh):
    in_specs = (
        P("ctx", "ch"),
        P("ctx", "ch"),
        P("ctx", "ch"),
        P(None, None, "ch"),
        P("ch", None),
        P("ch", None),
        P("ch", None),
        P("ctx", "ch"),
    )
    out_specs = (P("ctx", "ch"), P("ctx", "ch"), P("ctx", "ch"), P("ctx", "ch"))
    return jax.shard_map(shards, mesh=mesh, in_specs=in_specs, out_specs=out_specs, check_vma=False)
```

```python
import functools

import jax
import jax.numpy as jnp
from jax import lax
from jax.experimental import pallas as pl
from jax.experimental.pallas import tpu as pltpu
from jax.sharding import PartitionSpec as P

SUB = 8
LANES = 128
STEP = 8
F32 = jnp.float32
BF16 = jnp.bfloat16


def as_tiles(rows):
    return rows.reshape(rows.shape[0] // SUB, SUB, LANES)


def as_rows(tiles):
    return tiles.reshape(tiles.shape[0] * SUB, LANES)


def tile(ref, token):
    return ref[pl.ds(pl.multiple_of(token * SUB, SUB), SUB), :]


def tree_sum(terms):
    while len(terms) > 1:
        terms = [
            terms[i] + terms[i + 1] if i + 1 < len(terms) else terms[i]
            for i in range(0, len(terms), 2)
        ]
    return terms[0]


def round16(value):
    return value.astype(BF16).astype(F32)


def scatter_tokens(ref, value, first_token):
    tokens, channels = value.shape
    for group in range(channels // LANES):
        ref[pl.ds(first_token * SUB + group, tokens, stride=SUB), :] = value[
            :, group * LANES : (group + 1) * LANES
        ]


def gather_tokens(rows, out_ref):
    for group in range(out_ref.shape[1] // LANES):
        out_ref[:, group * LANES : (group + 1) * LANES] = rows(group).astype(out_ref.dtype)


def group_rows(ref, group, tokens):
    return ref[pl.ds(group, tokens, stride=SUB), :]


def start_all(copies):
    for copy in copies:
        copy.start()
    return copies


def wait_all(copies):
    for copy in copies:
        copy.wait()


def advance_states(signal_ref, factors, states, first, count, reverse):
    last = signal_ref.shape[0] // SUB - 1

    def body(step, states):
        for inner in range(STEP):
            token = first + step * STEP + inner
            u = tile(signal_ref, last - token if reverse else token)
            states = [factor * state + u for factor, state in zip(factors, states)]
        return states

    return lax.fori_loop(0, count // STEP, body, states)


def zero_states(modes):
    return [jnp.zeros((SUB, LANES), F32) for _ in range(modes)]


def mode_rows(n):
    return slice(n * SUB, (n + 1) * SUB)


def fades(decay_ref, tokens):
    return [
        jnp.exp(-decay_ref[mode_rows(n), :] * tokens) for n in range(decay_ref.shape[0] // SUB)
    ]


def write_messages(out_ref, states, decay_ref, position_ref, tokens, direction):
    count = out_ref.shape[0]
    out_ref[...] = jnp.zeros_like(out_ref)
    fade = fades(decay_ref, float(tokens))
    for gap in range(count - 1):
        other = position_ref[0] + direction * (gap + 1)
        value = jnp.concatenate(states, axis=0).astype(out_ref.dtype)

        @pl.when((other >= 0) & (other < count))
        def _():
            out_ref[jnp.clip(other, 0, count - 1)] = value

        states = [state * factor for state, factor in zip(states, fade)]


def read_messages(in_ref):
    total = in_ref[0].astype(F32)
    for other in range(1, in_ref.shape[0]):
        total = total + in_ref[other].astype(F32)
    return [total[mode_rows(n)] for n in range(total.shape[0] // SUB)]


def rim_kernel(
    q_ref, k_ref, v_ref, taps_ref, residue_ref, decay_ref,
    rim_ref, streams_ref, taps_vmem, residue_vmem, decay_vmem, sems,
):
    rows = rim_ref.shape[0] // 3
    streams = (q_ref, k_ref, v_ref)
    rims = [
        pltpu.make_async_copy(
            source.at[pl.ds(source.shape[0] - rows, rows), :],
            rim_ref.at[pl.ds(stream * rows, rows), :],
            sems.at[stream],
        )
        for stream, source in enumerate(streams)
    ]
    pairs = [(source, streams_ref.at[stream]) for stream, source in enumerate(streams)]
    pairs += [(taps_ref, taps_vmem), (residue_ref, residue_vmem), (decay_ref, decay_vmem)]
    others = [
        pltpu.make_async_copy(source, target, sems.at[3 + number])
        for number, (source, target) in enumerate(pairs)
    ]
    wait_all(start_all(rims + others))


def filtered(window, taps_ref, stream, taps, steps, forward):
    total = None
    for tap in range(taps):
        first = taps - 1 - tap if forward else tap
        term = taps_ref[pl.ds((stream * taps + tap) * SUB, SUB), :] * window[first : first + steps]
        total = term if total is None else total + term
    return total


def featurize_kernel(
    position_ref, streams_ref, taps_in_ref, residue_ref, decay_in_ref, halo_ref, grad_in_ref,
    qf_ref, kf_ref, vf_ref, local_ref, grad_copy_ref, message_ref, taps_ref, scale_ref, decay_ref,
    wide_ref, feat_ref, grad_vmem, sems,
):
    grad_in = pltpu.make_async_copy(grad_in_ref, grad_vmem, sems.at[4])
    grad_in.start()
    tokens = streams_ref.shape[1]
    _, taps, _ = taps_in_ref.shape
    rim = taps - 1
    modes = decay_in_ref.shape[0]
    held = halo_ref.shape[0] // 3
    decays = decay_in_ref[...]
    scatter_tokens(decay_ref, decays, 0)
    scatter_tokens(scale_ref, residue_ref[...] * jnp.sqrt(decays), 0)
    for stream in range(3):
        scatter_tokens(taps_ref, taps_in_ref[stream], stream * taps)
        behind = halo_ref[stream * held : (stream + 1) * held, :].astype(F32)
        scatter_tokens(wide_ref.at[stream], behind[held - rim :], 0)
        scatter_tokens(wide_ref.at[stream], streams_ref[stream].astype(F32), rim)

    def body(step, carry):
        begin = pl.multiple_of(step * STEP * SUB, SUB)
        rows = pl.ds(begin, STEP * SUB)
        feats = []
        for stream in range(3):
            window = as_tiles(wide_ref[stream, pl.ds(begin, (STEP + rim) * SUB), :])
            feats.append(filtered(window, taps_ref, stream, taps, STEP, True))
            feat_ref[stream, rows, :] = as_rows(feats[-1])
        feat_ref[3, rows, :] = as_rows(round16(feats[1] * feats[2]))
        return carry

    lax.fori_loop(0, tokens // STEP, body, 0)
    grad_in.wait()
    copies = start_all(
        [
            pltpu.make_async_copy(source, target, sems.at[number])
            for number, (source, target) in enumerate(
                (
                    (feat_ref.at[0], qf_ref),
                    (feat_ref.at[1], kf_ref),
                    (feat_ref.at[2], vf_ref),
                    (grad_vmem, grad_copy_ref),
                )
            )
        ]
    )
    local_vmem = wide_ref.at[0, pl.ds(0, tokens * SUB), :]
    states = local_conv(feat_ref.at[3], decay_ref, scale_ref, local_vmem, False)
    copies += start_all([pltpu.make_async_copy(local_vmem, local_ref, sems.at[4])])
    write_messages(message_ref, states, decay_ref, position_ref, tokens, 1)
    wait_all(copies)


def scales_of(scale_ref):
    return [scale_ref[mode_rows(n), :] for n in range(scale_ref.shape[0] // SUB)]


def local_conv(signal_ref, decay_ref, scale_ref, out_ref, reverse):
    tokens = signal_ref.shape[0] // SUB
    factors = fades(decay_ref, 1.0)
    scales = scales_of(scale_ref)

    def body(step, states):
        for inner in range(STEP):
            token = step * STEP + inner
            token = tokens - 1 - token if reverse else token
            u = tile(signal_ref, token)
            states = [factor * state + u for factor, state in zip(factors, states)]
            out_ref[pl.ds(pl.multiple_of(token * SUB, SUB), SUB), :] = tree_sum(
                [scale * state for scale, state in zip(scales, states)]
            )
        return states

    return lax.fori_loop(0, tokens // STEP, body, zero_states(len(factors)))


def carried(out_ref, states, decay_ref, scale_ref, reverse, local_ref=None):
    tokens = out_ref.shape[0] // SUB
    factors = fades(decay_ref, 1.0)
    scaled = [scale * state for scale, state in zip(scales_of(scale_ref), states)]

    def body(step, scaled):
        for inner in range(STEP):
            token = step * STEP + inner
            token = tokens - 1 - token if reverse else token
            scaled = [factor * state for factor, state in zip(factors, scaled)]
            rows = pl.ds(pl.multiple_of(token * SUB, SUB), SUB)
            total = tree_sum(list(scaled))
            out_ref[rows, :] = total if local_ref is None else local_ref[rows, :] + total
        return scaled

    lax.fori_loop(0, tokens // STEP, body, scaled)


def project_kernel(
    index_ref, message_ref, decay_ref, scale_ref, _, qf_ref, local_ref, weight_ref, *refs
):
    rows_ref, feat_ref, local_vmem, gated_ref, held_ref, sent_ref, sems, out_sems = refs[-8:]
    conv_ref, *out_refs = refs[-9 - sent_ref.shape[0] : -8]
    parts, tokens, width = sent_ref.shape
    order = list(reversed(range(parts)))
    copies = [
        pltpu.make_async_copy(
            weight_ref.at[:, pl.ds(pl.multiple_of(index_ref[part] * width, width), width)],
            held_ref.at[part],
            sems.at[part],
        )
        for part in range(parts)
    ]
    outs = [
        pltpu.make_async_copy(sent_ref.at[part], out_refs[part], out_sems.at[part])
        for part in range(parts)
    ]
    local_copy = pltpu.make_async_copy(local_ref, local_vmem, sems.at[parts + 1])
    feat_copy = pltpu.make_async_copy(qf_ref, feat_ref, sems.at[parts])
    start_all([local_copy, feat_copy])
    start_all([copies[part] for part in order])
    carried(rows_ref, read_messages(message_ref), decay_ref, scale_ref, False)
    local_copy.wait()
    rows_ref[...] += local_vmem[...]
    conv_copy = pltpu.make_async_copy(rows_ref, conv_ref, sems.at[parts + 1])
    conv_copy.start()
    feat_copy.wait()
    gather_tokens(
        lambda group: group_rows(rows_ref, group, tokens) * group_rows(feat_ref, group, tokens),
        gated_ref,
    )
    for part in order:
        copies[part].wait()
        sent_ref[part] = jnp.dot(
            gated_ref[...], held_ref[part], preferred_element_type=F32
        ).astype(sent_ref.dtype)
        outs[part].start()
    conv_copy.wait()
    wait_all(outs)


def start_weights(index_ref, first, weight_ref, held_ref, sems):
    count, _, width = held_ref.shape
    return start_all(
        [
            pltpu.make_async_copy(
                weight_ref.at[
                    :, pl.ds(pl.multiple_of(index_ref[first + number] * width, width), width)
                ],
                held_ref.at[number],
                sems.at[number],
            )
            for number in range(count)
        ]
    )


def back_products(weights, piece_refs, turned_ref, held_ref, total_ref, before_ref):
    for number, ref in enumerate(piece_refs):
        turned_ref[number] = ref[...].T
    for number in range(len(piece_refs)):
        weights[number].wait()
        product = jnp.dot(held_ref[number], turned_ref[number], preferred_element_type=F32)
        earlier = before_ref if number == 0 else total_ref
        total_ref[...] = product if earlier is None else earlier[...] + product


def middle_kernel(index_ref, weight_ref, *refs):
    *piece_refs, total_ref, piece_vmem, turned_ref, held_ref, sems, piece_sems = refs
    pieces = start_all(
        [
            pltpu.make_async_copy(ref, piece_vmem.at[number], piece_sems.at[number])
            for number, ref in enumerate(piece_refs)
        ]
    )
    weights = start_weights(index_ref, 0, weight_ref, held_ref, sems)
    wait_all(pieces)
    held = [piece_vmem.at[number] for number in range(len(piece_refs))]
    back_products(weights, held, turned_ref, held_ref, total_ref, None)


def back_last_kernel(
    index_ref, position_ref, base_ref, decay_ref, weight_ref, qf_ref, kf_ref, vf_ref, conv_ref,
    *refs, rim,
):
    (
        *piece_refs, back_query_ref, mixed_ref, message_ref, ahead_ref, piece_vmem,
        turned_ref, total_ref, rows_ref, feat_ref, conv_vmem, held_ref, sems, piece_sems, own_sems,
    ) = refs
    piece_refs = piece_refs[-turned_ref.shape[0] :]
    pieces = start_all(
        [
            pltpu.make_async_copy(ref, piece_vmem.at[number], piece_sems.at[number])
            for number, ref in enumerate(piece_refs)
        ]
    )
    tokens = total_ref.shape[1]
    heads = pl.ds(0, rim * SUB)
    weights = start_weights(
        index_ref, index_ref.shape[0] - len(piece_refs), weight_ref, held_ref, sems
    )
    copies = start_all(
        [
            pltpu.make_async_copy(qf_ref, feat_ref, own_sems.at[0]),
            pltpu.make_async_copy(conv_ref, conv_vmem, own_sems.at[1]),
            pltpu.make_async_copy(kf_ref.at[heads, :], ahead_ref.at[2], own_sems.at[2]),
            pltpu.make_async_copy(vf_ref.at[heads, :], ahead_ref.at[3], own_sems.at[3]),
        ]
    )
    wait_all(pieces)
    held = [piece_vmem.at[number] for number in range(len(piece_refs))]
    back_products(weights, held, turned_ref, held_ref, total_ref, base_ref)
    scatter_tokens(rows_ref, total_ref[...].T, 0)
    wait_all(copies)
    mixed_ref[...] = round16(rows_ref[...] * feat_ref[...])
    rows_ref[...] = round16(rows_ref[...] * conv_vmem[...])
    out = pltpu.make_async_copy(rows_ref, back_query_ref, own_sems.at[4])
    out.start()
    ahead_ref[0] = rows_ref[: rim * SUB, :]
    ahead_ref[1] = mixed_ref[: rim * SUB, :]
    modes = decay_ref.shape[0] // SUB
    states = advance_states(
        mixed_ref, fades(decay_ref, 1.0), zero_states(modes), 0, tokens, True
    )
    write_messages(message_ref, states, decay_ref, position_ref, tokens, -1)
    out.wait()


def spread_back(wide_ref, taps_ref, stream, taps, rows_ref, out_ref):
    tokens = out_ref.shape[0]

    def body(step, carry):
        first = pl.multiple_of(step * STEP * SUB, SUB)
        window = as_tiles(wide_ref[pl.ds(first, (STEP + taps - 1) * SUB), :])
        rows_ref[pl.ds(first, STEP * SUB), :] = as_rows(
            filtered(window, taps_ref, stream, taps, STEP, False)
        )
        return carry

    lax.fori_loop(0, tokens // STEP, body, 0)
    gather_tokens(lambda group: group_rows(rows_ref, group, tokens), out_ref)


def back_local_kernel(
    signal_ref, decay_ref, scale_ref, taps_ref, query_ref, *refs, taps
):
    local_ref, gq_ref, wide_ref, rows_ref, out_vmem, sem = refs[-6:]
    inside = query_ref.shape[0]
    copy = pltpu.make_async_copy(query_ref, wide_ref.at[pl.ds(0, inside), :], sem)
    copy.start()
    local_conv(signal_ref, decay_ref, scale_ref, local_ref, True)
    copy.wait()
    rest = (taps - 1) * SUB
    wide_ref[pl.ds(inside, rest), :] = jnp.zeros((rest, LANES), F32)
    spread_back(wide_ref, taps_ref, 0, taps, rows_ref, out_vmem)
    out = pltpu.make_async_copy(out_vmem, gq_ref, sem)
    out.start()
    out.wait()


def finish_kernel(
    message_ref, local_ref, decay_ref, scale_ref, taps_ref, ahead_ref, query_ref, kf_ref, vf_ref,
    *refs, taps,
):
    (
        *part_refs, _, gq_ref, gk_ref, gv_ref, projected_ref,
        total_ref, feat_ref, query_vmem, wide_ref, rows_ref, tail_ref, out_vmem, parts_vmem,
        sems, part_sems,
    ) = refs
    tokens = gk_ref.shape[0]
    tail = tail_ref.shape[0]
    rim = taps - 1
    inside = pl.ds(0, tokens * SUB)
    copies = start_all(
        [
            pltpu.make_async_copy(
                query_ref.at[pl.ds((tokens - tail) * SUB, tail * SUB), :],
                query_vmem.at[pl.ds(0, tail * SUB), :],
                sems.at[0],
            ),
            pltpu.make_async_copy(vf_ref, feat_ref.at[0], sems.at[1]),
            pltpu.make_async_copy(kf_ref, feat_ref.at[1], sems.at[2]),
        ]
    )
    parts = start_all(
        [
            pltpu.make_async_copy(ref, parts_vmem.at[number], part_sems.at[number])
            for number, ref in enumerate(part_refs)
        ]
    )
    states = read_messages(message_ref)
    carried(total_ref, states, decay_ref, scale_ref, True, local_ref)
    growth = fades(decay_ref, -1.0)
    scales = scales_of(scale_ref)
    for ahead in range(rim):
        rows = pl.ds((tokens + ahead) * SUB, SUB)
        theirs = pl.ds(ahead * SUB, SUB)
        grad_conv = tree_sum([scale * state for scale, state in zip(scales, states)])
        query_vmem[pl.ds((tail + ahead) * SUB, SUB), :] = ahead_ref[0, theirs, :]
        wide_ref[0, rows, :] = round16(grad_conv * ahead_ref[3, theirs, :])
        wide_ref[1, rows, :] = round16(grad_conv * ahead_ref[2, theirs, :])
        arrived = ahead_ref[1, theirs, :]
        states = [(state - arrived) * grow for state, grow in zip(states, growth)]
    copies[0].wait()
    spread_back(query_vmem, taps_ref, 0, taps, rows_ref, tail_ref)
    outs = [
        pltpu.make_async_copy(tail_ref, gq_ref.at[pl.ds(tokens - tail, tail), :], sems.at[0])
    ]
    wait_all(parts)
    out_vmem[2] = tree_sum(
        [parts_vmem[number].astype(F32) for number in range(len(part_refs))]
    ).astype(out_vmem.dtype)
    outs.append(pltpu.make_async_copy(out_vmem.at[2], projected_ref, sems.at[3]))
    start_all(outs)
    for stream, out_ref in enumerate((gk_ref, gv_ref)):
        copies[1 + stream].wait()
        wide_ref[stream, inside, :] = round16(total_ref[...] * feat_ref[stream])
        spread_back(
            wide_ref.at[stream], taps_ref, 1 + stream, taps, rows_ref, out_vmem.at[stream]
        )
        outs.append(pltpu.make_async_copy(out_vmem.at[stream], out_ref, sems.at[1 + stream]))
        outs[-1].start()
    wait_all(outs)


IN_VMEM = pl.BlockSpec(memory_space=pltpu.VMEM)
IN_SMEM = pl.BlockSpec(memory_space=pltpu.SMEM)
IN_HBM = pl.BlockSpec(memory_space=pltpu.HBM)
HBM_RATE = 3.5e6


def in_hbm(shape, kind):
    return pltpu.HBM(shape, kind)


def call(kernel, outs, args, specs, scratch, name, micros, mebibytes, aliases=None):
    args = [
        pltpu.with_memory_space_constraint(arg, pltpu.HBM) if spec is IN_HBM else arg
        for arg, spec in zip(args, specs)
    ]
    held = [isinstance(out, tuple) for out in outs]
    return pl.pallas_call(
        kernel,
        out_shape=[jax.ShapeDtypeStruct(*out) if own else out for own, out in zip(held, outs)],
        in_specs=specs,
        out_specs=[IN_VMEM if own else IN_HBM for own in held],
        scratch_shapes=scratch,
        compiler_params=pltpu.CompilerParams(vmem_limit_bytes=mebibytes * 1024 * 1024),
        cost_estimate=pl.CostEstimate(
            flops=0, bytes_accessed=int(micros * HBM_RATE), transcendentals=0
        ),
        name=name,
        input_output_aliases=aliases or {},
    )(*args)


def shift(value, axis, steps):
    count = lax.axis_size(axis)
    pairs = [(s, s + steps) for s in range(count) if 0 <= s + steps < count]
    return lax.ppermute(value, axis, pairs)


def exchange(value, axis, mask):
    count = lax.axis_size(axis)
    return lax.ppermute(value, axis, [(s, s ^ mask) for s in range(count)])


def shards(query_in, key_in, value_in, short_taps, residues, decays, out_weight, out_grad):
    tokens, channels = query_in.shape
    taps = short_taps.shape[0]
    rim = taps - 1
    modes = decays.shape[1]
    blocks = lax.axis_size("ctx")
    fans = lax.axis_size("ch")
    position = lax.axis_index("ctx")[None].astype(jnp.int32)
    tile_shape = (tokens * SUB, LANES)
    mode_shape = (modes * SUB, LANES)
    message_shape = (blocks,) + mode_shape
    streams = (query_in, key_in, value_in)
    rim_rows = 16

    tap_rows = jnp.transpose(short_taps, (1, 0, 2))
    halo, narrow, taps_vmem, residues_vmem, decays_vmem = call(
        rim_kernel,
        [
            ((3 * rim_rows, channels), BF16),
            ((3, tokens, channels), BF16),
            ((3, taps, channels), F32),
            ((modes, channels), F32),
            ((modes, channels), F32),
        ],
        streams + (tap_rows, residues.T, decays.T), [IN_HBM] * 6,
        [pltpu.SemaphoreType.DMA((9,))], "rim", 1.2, 2,
    )
    halo, out_grad = lax.optimization_barrier((halo, out_grad))
    halo = shift(halo, "ctx", 1)
    if fans == 4:
        order = lax.axis_index("ch") ^ jnp.arange(fans, dtype=jnp.int32)
        pieces = [out_grad] + [exchange(out_grad, "ch", mask) for mask in range(1, fans - 1)]
    else:
        order = jnp.arange(fans, dtype=jnp.int32)
        everyone = lax.all_gather(out_grad, "ch", axis=0, tiled=False)
        pieces = [everyone[number] for number in range(fans)]
    tile = pltpu.VMEM(tile_shape, F32)
    wide_rows = (tokens + rim) * SUB

    (
        query_feat, key_feat, value_feat, local, grad_copy, messages,
        tap_tiles, scale_tiles, decay_tiles,
    ) = call(
        featurize_kernel,
        [in_hbm(tile_shape, F32)] * 4
        + [in_hbm((tokens, channels), BF16), (message_shape, BF16)]
        + [((3 * taps * SUB, LANES), F32), (mode_shape, F32), (mode_shape, F32)],
        (position, narrow, taps_vmem, residues_vmem, decays_vmem, halo, out_grad),
        [IN_SMEM] + [IN_VMEM] * 5 + [IN_HBM],
        [
            pltpu.VMEM((3, wide_rows, LANES), F32),
            pltpu.VMEM((4,) + tile_shape, F32),
            pltpu.VMEM((tokens, channels), BF16),
            pltpu.SemaphoreType.DMA((5,)),
        ],
        "featurize", 6.0, 10,
    )
    if fans == 4:
        pieces.append(exchange(grad_copy, "ch", fans - 1))
    arrived = lax.all_to_all(messages, "ctx", split_axis=0, concat_axis=0, tiled=True)

    def weight_scratch(count):
        return [
            pltpu.VMEM((count, channels, channels), BF16),
            pltpu.SemaphoreType.DMA((count,)),
        ]

    early = fans // 2
    (base,) = call(
        middle_kernel,
        [((channels, tokens), F32)],
        (order, out_weight, *pieces[:early]),
        [IN_SMEM] + [IN_HBM] * (1 + early),
        [
            pltpu.VMEM((early, tokens, channels), BF16),
            pltpu.VMEM((early, channels, tokens), BF16),
        ]
        + weight_scratch(early)
        + [pltpu.SemaphoreType.DMA((early,))],
        "middle", 6.0, 11,
    )
    conv_out, *partial_sums = call(
        project_kernel,
        [in_hbm(tile_shape, F32)] + [in_hbm((tokens, channels), BF16)] * fans,
        (
            order, arrived, decay_tiles, scale_tiles, base, query_feat, local, out_weight,
            *pieces[1:early],
        ),
        [IN_SMEM] + [IN_VMEM] * 4 + [IN_HBM] * (2 + early),
        [
            tile,
            tile,
            tile,
            pltpu.VMEM((tokens, channels), BF16),
            pltpu.VMEM((fans, channels, channels), BF16),
            pltpu.VMEM((fans, tokens, channels), BF16),
            pltpu.SemaphoreType.DMA((fans + 2,)),
            pltpu.SemaphoreType.DMA((fans,)),
        ],
        "project", 7.0, 16,
    )
    if fans == 4:
        parts = [
            exchange(part, "ch", mask) if mask else part for mask, part in enumerate(partial_sums)
        ]
    else:
        parts = lax.all_to_all(
            jnp.stack(partial_sums), "ch", split_axis=0, concat_axis=0, tiled=True
        )
        parts = [parts[number] for number in range(fans)]
    back_query, grad_mixed, back_messages, ahead = call(
        functools.partial(back_last_kernel, rim=rim),
        [in_hbm(tile_shape, F32), (tile_shape, F32), (message_shape, BF16)]
        + [((4, rim * SUB, LANES), F32)],
        (
            order, position, base, decay_tiles, out_weight, query_feat, key_feat,
            value_feat, conv_out, *pieces[1:early], *pieces[early:],
        ),
        [IN_SMEM] * 2 + [IN_VMEM] * 2 + [IN_HBM] * (4 + fans),
        [
            pltpu.VMEM((fans - early, tokens, channels), BF16),
            pltpu.VMEM((fans - early, channels, tokens), BF16),
            pltpu.VMEM((channels, tokens), F32),
            tile,
            tile,
            tile,
        ]
        + weight_scratch(fans - early)
        + [pltpu.SemaphoreType.DMA((fans - early,)), pltpu.SemaphoreType.DMA((5,))],
        "back_last", 7.0, 13,
    )
    back_arrived = lax.all_to_all(back_messages, "ctx", split_axis=0, concat_axis=0, tiled=True)
    ahead = shift(ahead, "ctx", -1)
    back_local, grad_query = call(
        functools.partial(back_local_kernel, taps=taps),
        [(tile_shape, F32), in_hbm((tokens, channels), BF16)],
        (grad_mixed, decay_tiles, scale_tiles, tap_tiles, back_query, *pieces[early:]),
        [IN_VMEM] * 4 + [IN_HBM] * (1 + fans - early),
        [
            pltpu.VMEM((wide_rows, LANES), F32),
            tile,
            pltpu.VMEM((tokens, channels), BF16),
            pltpu.SemaphoreType.DMA,
        ],
        "back_local", 4.5, 5,
    )
    tail = 16
    grad_query, grad_key, grad_value, projected = call(
        functools.partial(finish_kernel, taps=taps),
        [in_hbm((tokens, channels), BF16)] * 4,
        (
            back_arrived, back_local, decay_tiles, scale_tiles, tap_tiles, ahead, back_query,
            key_feat, value_feat, *parts, grad_query,
        ),
        [IN_VMEM] * 6 + [IN_HBM] * (4 + fans),
        [
            tile,
            pltpu.VMEM((2,) + tile_shape, F32),
            pltpu.VMEM(((tail + rim) * SUB, LANES), F32),
            pltpu.VMEM((2, wide_rows, LANES), F32),
            tile,
            pltpu.VMEM((tail, channels), BF16),
            pltpu.VMEM((3, tokens, channels), BF16),
            pltpu.VMEM((fans, tokens, channels), BF16),
            pltpu.SemaphoreType.DMA((4,)),
            pltpu.SemaphoreType.DMA((fans,)),
        ],
        "finish", 5.0, 12,
        {9 + fans: 0},
    )
    return (projected, grad_query, grad_key, grad_value)


def solution(mesh):
    in_specs = (
        P("ctx", "ch"),
        P("ctx", "ch"),
        P("ctx", "ch"),
        P(None, None, "ch"),
        P("ch", None),
        P("ch", None),
        P("ch", None),
        P("ctx", "ch"),
    )
    out_specs = (P("ctx", "ch"), P("ctx", "ch"), P("ctx", "ch"), P("ctx", "ch"))
    return jax.shard_map(shards, mesh=mesh, in_specs=in_specs, out_specs=out_specs, check_vma=False)
```

```python
import functools

import jax
import jax.numpy as jnp
from jax import lax
from jax.experimental import pallas as pl
from jax.experimental.pallas import tpu as pltpu
from jax.sharding import PartitionSpec as P

SUB = 8
LANES = 128
STEP = 8
F32 = jnp.float32
BF16 = jnp.bfloat16


def as_tiles(rows):
    return rows.reshape(rows.shape[0] // SUB, SUB, LANES)


def as_rows(tiles):
    return tiles.reshape(tiles.shape[0] * SUB, LANES)


def tile(ref, token):
    return ref[pl.ds(pl.multiple_of(token * SUB, SUB), SUB), :]


def tree_sum(terms):
    while len(terms) > 1:
        terms = [
            terms[i] + terms[i + 1] if i + 1 < len(terms) else terms[i]
            for i in range(0, len(terms), 2)
        ]
    return terms[0]


def round16(value):
    return value.astype(BF16).astype(F32)


def scatter_tokens(ref, value, first_token):
    tokens, channels = value.shape
    for group in range(channels // LANES):
        ref[pl.ds(first_token * SUB + group, tokens, stride=SUB), :] = value[
            :, group * LANES : (group + 1) * LANES
        ]


def gather_tokens(rows, out_ref):
    for group in range(out_ref.shape[1] // LANES):
        out_ref[:, group * LANES : (group + 1) * LANES] = rows(group).astype(out_ref.dtype)


def group_rows(ref, group, tokens):
    return ref[pl.ds(group, tokens, stride=SUB), :]


def start_all(copies):
    for copy in copies:
        copy.start()
    return copies


def wait_all(copies):
    for copy in copies:
        copy.wait()


def advance_states(signal_ref, factors, states, first, count, reverse):
    last = signal_ref.shape[0] // SUB - 1

    def body(step, states):
        for inner in range(STEP):
            token = first + step * STEP + inner
            u = tile(signal_ref, last - token if reverse else token)
            states = [factor * state + u for factor, state in zip(factors, states)]
        return states

    return lax.fori_loop(0, count // STEP, body, states)


def zero_states(modes):
    return [jnp.zeros((SUB, LANES), F32) for _ in range(modes)]


def mode_rows(n):
    return slice(n * SUB, (n + 1) * SUB)


def fades(decay_ref, tokens):
    return [
        jnp.exp(-decay_ref[mode_rows(n), :] * tokens) for n in range(decay_ref.shape[0] // SUB)
    ]


def write_state(out_ref, states):
    out_ref[...] = jnp.concatenate(states, axis=0)


def comes_first(position, direction):
    return (position % 2 == 0) == (direction > 0)


def incoming(position_ref, partner_ref, message_refs, decay_ref, tokens, direction):
    total = tree_sum([ref[...].astype(F32) for ref in message_refs])
    faded = total * jnp.exp(-decay_ref[...] * float(tokens)) + partner_ref[...]
    total = jnp.where(comes_first(position_ref[0], direction), total, faded)
    return [total[mode_rows(n)] for n in range(total.shape[0] // SUB)]


def rim_kernel(
    q_ref, k_ref, v_ref, taps_ref, residue_ref, decay_ref,
    rim_ref, streams_ref, taps_vmem, residue_vmem, decay_vmem, sems,
):
    rows = rim_ref.shape[0] // 3
    streams = (q_ref, k_ref, v_ref)
    rims = [
        pltpu.make_async_copy(
            source.at[pl.ds(source.shape[0] - rows, rows), :],
            rim_ref.at[pl.ds(stream * rows, rows), :],
            sems.at[stream],
        )
        for stream, source in enumerate(streams)
    ]
    pairs = [(source, streams_ref.at[stream]) for stream, source in enumerate(streams)]
    pairs += [(taps_ref, taps_vmem), (residue_ref, residue_vmem), (decay_ref, decay_vmem)]
    others = [
        pltpu.make_async_copy(source, target, sems.at[3 + number])
        for number, (source, target) in enumerate(pairs)
    ]
    wait_all(start_all(rims + others))


def filtered(window, taps_ref, stream, taps, steps, forward):
    total = None
    for tap in range(taps):
        first = taps - 1 - tap if forward else tap
        term = taps_ref[pl.ds((stream * taps + tap) * SUB, SUB), :] * window[first : first + steps]
        total = term if total is None else total + term
    return total


def featurize_kernel(
    streams_ref, taps_in_ref, residue_ref, decay_in_ref, halo_ref, grad_in_ref,
    qf_ref, kf_ref, vf_ref, local_ref, grad_copy_ref, state_ref, taps_ref, scale_ref, decay_ref,
    wide_ref, feat_ref, grad_vmem, sems,
):
    grad_in = pltpu.make_async_copy(grad_in_ref, grad_vmem, sems.at[4])
    grad_in.start()
    tokens = streams_ref.shape[1]
    _, taps, _ = taps_in_ref.shape
    rim = taps - 1
    modes = decay_in_ref.shape[0]
    held = halo_ref.shape[0] // 3
    decays = decay_in_ref[...]
    scatter_tokens(decay_ref, decays, 0)
    scatter_tokens(scale_ref, residue_ref[...] * jnp.sqrt(decays), 0)
    for stream in range(3):
        scatter_tokens(taps_ref, taps_in_ref[stream], stream * taps)
        behind = halo_ref[stream * held : (stream + 1) * held, :].astype(F32)
        scatter_tokens(wide_ref.at[stream], behind[held - rim :], 0)
        scatter_tokens(wide_ref.at[stream], streams_ref[stream].astype(F32), rim)

    def body(step, carry):
        begin = pl.multiple_of(step * STEP * SUB, SUB)
        rows = pl.ds(begin, STEP * SUB)
        feats = []
        for stream in range(3):
            window = as_tiles(wide_ref[stream, pl.ds(begin, (STEP + rim) * SUB), :])
            feats.append(filtered(window, taps_ref, stream, taps, STEP, True))
            feat_ref[stream, rows, :] = as_rows(feats[-1])
        feat_ref[3, rows, :] = as_rows(round16(feats[1] * feats[2]))
        return carry

    lax.fori_loop(0, tokens // STEP, body, 0)
    grad_in.wait()
    copies = start_all(
        [
            pltpu.make_async_copy(source, target, sems.at[number])
            for number, (source, target) in enumerate(
                (
                    (feat_ref.at[0], qf_ref),
                    (feat_ref.at[1], kf_ref),
                    (feat_ref.at[2], vf_ref),
                    (grad_vmem, grad_copy_ref),
                )
            )
        ]
    )
    local_vmem = wide_ref.at[0, pl.ds(0, tokens * SUB), :]
    states = local_conv(feat_ref.at[3], decay_ref, scale_ref, local_vmem, False)
    copies += start_all([pltpu.make_async_copy(local_vmem, local_ref, sems.at[4])])
    write_state(state_ref, states)
    wait_all(copies)


def scales_of(scale_ref):
    return [scale_ref[mode_rows(n), :] for n in range(scale_ref.shape[0] // SUB)]


def local_conv(signal_ref, decay_ref, scale_ref, out_ref, reverse):
    tokens = signal_ref.shape[0] // SUB
    factors = fades(decay_ref, 1.0)
    scales = scales_of(scale_ref)

    def body(step, states):
        for inner in range(STEP):
            token = step * STEP + inner
            token = tokens - 1 - token if reverse else token
            u = tile(signal_ref, token)
            states = [factor * state + u for factor, state in zip(factors, states)]
            out_ref[pl.ds(pl.multiple_of(token * SUB, SUB), SUB), :] = tree_sum(
                [scale * state for scale, state in zip(scales, states)]
            )
        return states

    return lax.fori_loop(0, tokens // STEP, body, zero_states(len(factors)))


def carried(out_ref, states, decay_ref, scale_ref, reverse, local_ref=None):
    tokens = out_ref.shape[0] // SUB
    factors = fades(decay_ref, 1.0)
    scaled = [scale * state for scale, state in zip(scales_of(scale_ref), states)]

    def body(step, scaled):
        for inner in range(STEP):
            token = step * STEP + inner
            token = tokens - 1 - token if reverse else token
            scaled = [factor * state for factor, state in zip(factors, scaled)]
            rows = pl.ds(pl.multiple_of(token * SUB, SUB), SUB)
            total = tree_sum(list(scaled))
            out_ref[rows, :] = total if local_ref is None else local_ref[rows, :] + total
        return scaled

    lax.fori_loop(0, tokens // STEP, body, scaled)


def project_kernel(
    index_ref, position_ref, decay_ref, scale_ref, qf_ref, local_ref, weight_ref, partner_ref, *refs
):
    rows_ref, feat_ref, local_vmem, gated_ref, held_ref, sent_ref, sems, out_sems = refs[-8:]
    outputs = 1 + sent_ref.shape[0]
    message_refs = refs[: -8 - outputs]
    conv_ref, *out_refs = refs[-8 - outputs : -8]
    parts, tokens, width = sent_ref.shape
    order = list(reversed(range(parts)))
    copies = [
        pltpu.make_async_copy(
            weight_ref.at[:, pl.ds(pl.multiple_of(index_ref[part] * width, width), width)],
            held_ref.at[part],
            sems.at[part],
        )
        for part in range(parts)
    ]
    outs = [
        pltpu.make_async_copy(sent_ref.at[part], out_refs[part], out_sems.at[part])
        for part in range(parts)
    ]
    local_copy = pltpu.make_async_copy(local_ref, local_vmem, sems.at[parts + 1])
    feat_copy = pltpu.make_async_copy(qf_ref, feat_ref, sems.at[parts])
    start_all([local_copy, feat_copy])
    start_all([copies[part] for part in order])
    states = incoming(position_ref, partner_ref, message_refs, decay_ref, tokens, 1)
    carried(rows_ref, states, decay_ref, scale_ref, False)
    local_copy.wait()
    rows_ref[...] += local_vmem[...]
    conv_copy = pltpu.make_async_copy(rows_ref, conv_ref, sems.at[parts + 1])
    conv_copy.start()
    feat_copy.wait()
    gather_tokens(
        lambda group: group_rows(rows_ref, group, tokens) * group_rows(feat_ref, group, tokens),
        gated_ref,
    )
    for part in order:
        copies[part].wait()
        sent_ref[part] = jnp.dot(
            gated_ref[...], held_ref[part], preferred_element_type=F32
        ).astype(sent_ref.dtype)
        outs[part].start()
    conv_copy.wait()
    wait_all(outs)


def start_weights(index_ref, weight_ref, held_ref, sems):
    count, _, width = held_ref.shape
    return start_all(
        [
            pltpu.make_async_copy(
                weight_ref.at[
                    :, pl.ds(pl.multiple_of(index_ref[number] * width, width), width)
                ],
                held_ref.at[number],
                sems.at[number],
            )
            for number in range(count)
        ]
    )


def back_products(weights, piece_refs, turned_ref, held_ref, total_ref):
    for number, ref in enumerate(piece_refs):
        turned_ref[number] = ref[...].T
    for number in range(len(piece_refs)):
        weights[number].wait()
        product = jnp.dot(held_ref[number], turned_ref[number], preferred_element_type=F32)
        total_ref[...] = product if number == 0 else total_ref[...] + product


def back_last_kernel(
    index_ref, decay_ref, weight_ref, qf_ref, kf_ref, vf_ref, conv_ref, *refs, rim
):
    (
        *piece_refs, back_query_ref, mixed_ref, state_ref, ahead_ref, piece_vmem,
        turned_ref, total_ref, rows_ref, feat_ref, conv_vmem, held_ref, sems, piece_sems, own_sems,
    ) = refs
    pieces = start_all(
        [
            pltpu.make_async_copy(ref, piece_vmem.at[number], piece_sems.at[number])
            for number, ref in enumerate(piece_refs)
        ]
    )
    tokens = total_ref.shape[1]
    heads = pl.ds(0, rim * SUB)
    weights = start_weights(index_ref, weight_ref, held_ref, sems)
    copies = start_all(
        [
            pltpu.make_async_copy(qf_ref, feat_ref, own_sems.at[0]),
            pltpu.make_async_copy(conv_ref, conv_vmem, own_sems.at[1]),
            pltpu.make_async_copy(kf_ref.at[heads, :], ahead_ref.at[2], own_sems.at[2]),
            pltpu.make_async_copy(vf_ref.at[heads, :], ahead_ref.at[3], own_sems.at[3]),
        ]
    )
    wait_all(pieces)
    held = [piece_vmem.at[number] for number in range(len(piece_refs))]
    back_products(weights, held, turned_ref, held_ref, total_ref)
    scatter_tokens(rows_ref, total_ref[...].T, 0)
    wait_all(copies)
    mixed_ref[...] = round16(rows_ref[...] * feat_ref[...])
    rows_ref[...] = round16(rows_ref[...] * conv_vmem[...])
    out = pltpu.make_async_copy(rows_ref, back_query_ref, own_sems.at[4])
    out.start()
    ahead_ref[0] = rows_ref[: rim * SUB, :]
    ahead_ref[1] = mixed_ref[: rim * SUB, :]
    modes = decay_ref.shape[0] // SUB
    states = advance_states(
        mixed_ref, fades(decay_ref, 1.0), zero_states(modes), 0, tokens, True
    )
    write_state(state_ref, states)
    out.wait()


def spread_back(wide_ref, taps_ref, stream, taps, rows_ref, out_ref):
    tokens = out_ref.shape[0]

    def body(step, carry):
        first = pl.multiple_of(step * STEP * SUB, SUB)
        window = as_tiles(wide_ref[pl.ds(first, (STEP + taps - 1) * SUB), :])
        rows_ref[pl.ds(first, STEP * SUB), :] = as_rows(
            filtered(window, taps_ref, stream, taps, STEP, False)
        )
        return carry

    lax.fori_loop(0, tokens // STEP, body, 0)
    gather_tokens(lambda group: group_rows(rows_ref, group, tokens), out_ref)


def back_local_kernel(
    signal_ref, decay_ref, scale_ref, taps_ref, query_ref, *refs, taps
):
    local_ref, gq_ref, wide_ref, rows_ref, out_vmem, sem = refs[-6:]
    inside = query_ref.shape[0]
    copy = pltpu.make_async_copy(query_ref, wide_ref.at[pl.ds(0, inside), :], sem)
    copy.start()
    local_conv(signal_ref, decay_ref, scale_ref, local_ref, True)
    copy.wait()
    rest = (taps - 1) * SUB
    wide_ref[pl.ds(inside, rest), :] = jnp.zeros((rest, LANES), F32)
    spread_back(wide_ref, taps_ref, 0, taps, rows_ref, out_vmem)
    out = pltpu.make_async_copy(out_vmem, gq_ref, sem)
    out.start()
    out.wait()


def finish_kernel(
    position_ref, local_ref, decay_ref, scale_ref, taps_ref, ahead_ref, query_ref, kf_ref, vf_ref,
    *refs, taps, pairs,
):
    partner_ref, *message_refs = refs[:pairs]
    (
        *part_refs, _, gq_ref, gk_ref, gv_ref, projected_ref,
        total_ref, feat_ref, query_vmem, wide_ref, rows_ref, tail_ref, out_vmem, parts_vmem,
        sems, part_sems,
    ) = refs[pairs:]
    tokens = gk_ref.shape[0]
    tail = tail_ref.shape[0]
    rim = taps - 1
    inside = pl.ds(0, tokens * SUB)
    copies = start_all(
        [
            pltpu.make_async_copy(
                query_ref.at[pl.ds((tokens - tail) * SUB, tail * SUB), :],
                query_vmem.at[pl.ds(0, tail * SUB), :],
                sems.at[0],
            ),
            pltpu.make_async_copy(vf_ref, feat_ref.at[0], sems.at[1]),
            pltpu.make_async_copy(kf_ref, feat_ref.at[1], sems.at[2]),
        ]
    )
    parts = start_all(
        [
            pltpu.make_async_copy(ref, parts_vmem.at[number], part_sems.at[number])
            for number, ref in enumerate(part_refs)
        ]
    )
    states = incoming(position_ref, partner_ref, message_refs, decay_ref, tokens, -1)
    carried(total_ref, states, decay_ref, scale_ref, True, local_ref)
    growth = fades(decay_ref, -1.0)
    scales = scales_of(scale_ref)
    for ahead in range(rim):
        rows = pl.ds((tokens + ahead) * SUB, SUB)
        theirs = pl.ds(ahead * SUB, SUB)
        grad_conv = tree_sum([scale * state for scale, state in zip(scales, states)])
        query_vmem[pl.ds((tail + ahead) * SUB, SUB), :] = ahead_ref[0, theirs, :]
        wide_ref[0, rows, :] = round16(grad_conv * ahead_ref[3, theirs, :])
        wide_ref[1, rows, :] = round16(grad_conv * ahead_ref[2, theirs, :])
        arrived = ahead_ref[1, theirs, :]
        states = [(state - arrived) * grow for state, grow in zip(states, growth)]
    copies[0].wait()
    spread_back(query_vmem, taps_ref, 0, taps, rows_ref, tail_ref)
    outs = [
        pltpu.make_async_copy(tail_ref, gq_ref.at[pl.ds(tokens - tail, tail), :], sems.at[0])
    ]
    wait_all(parts)
    out_vmem[2] = tree_sum(
        [parts_vmem[number].astype(F32) for number in range(len(part_refs))]
    ).astype(out_vmem.dtype)
    outs.append(pltpu.make_async_copy(out_vmem.at[2], projected_ref, sems.at[3]))
    start_all(outs)
    for stream, out_ref in enumerate((gk_ref, gv_ref)):
        copies[1 + stream].wait()
        wide_ref[stream, inside, :] = round16(total_ref[...] * feat_ref[stream])
        spread_back(
            wide_ref.at[stream], taps_ref, 1 + stream, taps, rows_ref, out_vmem.at[stream]
        )
        outs.append(pltpu.make_async_copy(out_vmem.at[stream], out_ref, sems.at[1 + stream]))
        outs[-1].start()
    wait_all(outs)


IN_VMEM = pl.BlockSpec(memory_space=pltpu.VMEM)
IN_SMEM = pl.BlockSpec(memory_space=pltpu.SMEM)
IN_HBM = pl.BlockSpec(memory_space=pltpu.HBM)
HBM_RATE = 3.5e6


def in_hbm(shape, kind):
    return pltpu.HBM(shape, kind)


def call(kernel, outs, args, specs, scratch, name, micros, mebibytes, aliases=None):
    args = [
        pltpu.with_memory_space_constraint(arg, pltpu.HBM) if spec is IN_HBM else arg
        for arg, spec in zip(args, specs)
    ]
    held = [isinstance(out, tuple) for out in outs]
    return pl.pallas_call(
        kernel,
        out_shape=[jax.ShapeDtypeStruct(*out) if own else out for own, out in zip(held, outs)],
        in_specs=specs,
        out_specs=[IN_VMEM if own else IN_HBM for own in held],
        scratch_shapes=scratch,
        compiler_params=pltpu.CompilerParams(vmem_limit_bytes=mebibytes * 1024 * 1024),
        cost_estimate=pl.CostEstimate(
            flops=0, bytes_accessed=int(micros * HBM_RATE), transcendentals=0
        ),
        name=name,
        input_output_aliases=aliases or {},
    )(*args)


def shift(value, axis, steps):
    count = lax.axis_size(axis)
    pairs = [(s, s + steps) for s in range(count) if 0 <= s + steps < count]
    return lax.ppermute(value, axis, pairs)


def exchange(value, axis, mask):
    count = lax.axis_size(axis)
    return lax.ppermute(value, axis, [(s, s ^ mask) for s in range(count)])


def exchange_states(state, decays, tokens, direction):
    blocks = lax.axis_size("ctx")
    first = comes_first(lax.axis_index("ctx"), direction)
    partner = exchange(state, "ctx", 1)
    lead, follow = jnp.where(first, state, partner), jnp.where(first, partner, state)
    total = lead * jnp.exp(-decays * float(tokens)) + follow
    messages = []
    for pair in range(1, blocks // 2):
        faded = total * jnp.exp(-decays * float(2 * tokens * (pair - 1)))
        messages.append(shift(faded.astype(BF16), "ctx", direction * 2 * pair))
    return [partner] + messages


def shards(query_in, key_in, value_in, short_taps, residues, decays, out_weight, out_grad):
    tokens, channels = query_in.shape
    taps = short_taps.shape[0]
    rim = taps - 1
    modes = decays.shape[1]
    blocks = lax.axis_size("ctx")
    fans = lax.axis_size("ch")
    position = lax.axis_index("ctx")[None].astype(jnp.int32)
    tile_shape = (tokens * SUB, LANES)
    mode_shape = (modes * SUB, LANES)
    streams = (query_in, key_in, value_in)
    rim_rows = 16

    tap_rows = jnp.transpose(short_taps, (1, 0, 2))
    halo, narrow, taps_vmem, residues_vmem, decays_vmem = call(
        rim_kernel,
        [
            ((3 * rim_rows, channels), BF16),
            ((3, tokens, channels), BF16),
            ((3, taps, channels), F32),
            ((modes, channels), F32),
            ((modes, channels), F32),
        ],
        streams + (tap_rows, residues.T, decays.T), [IN_HBM] * 6,
        [pltpu.SemaphoreType.DMA((9,))], "rim", 1.2, 2,
    )
    halo, out_grad = lax.optimization_barrier((halo, out_grad))
    halo = shift(halo, "ctx", 1)
    if fans == 4:
        order = lax.axis_index("ch") ^ jnp.arange(fans, dtype=jnp.int32)
        pieces = [out_grad] + [exchange(out_grad, "ch", mask) for mask in range(1, fans - 1)]
    else:
        order = jnp.arange(fans, dtype=jnp.int32)
        everyone = lax.all_gather(out_grad, "ch", axis=0, tiled=False)
        pieces = [everyone[number] for number in range(fans)]
    tile = pltpu.VMEM(tile_shape, F32)
    wide_rows = (tokens + rim) * SUB

    (
        query_feat, key_feat, value_feat, local, grad_copy, state,
        tap_tiles, scale_tiles, decay_tiles,
    ) = call(
        featurize_kernel,
        [in_hbm(tile_shape, F32)] * 4
        + [in_hbm((tokens, channels), BF16), (mode_shape, F32)]
        + [((3 * taps * SUB, LANES), F32), (mode_shape, F32), (mode_shape, F32)],
        (narrow, taps_vmem, residues_vmem, decays_vmem, halo, out_grad),
        [IN_VMEM] * 5 + [IN_HBM],
        [
            pltpu.VMEM((3, wide_rows, LANES), F32),
            pltpu.VMEM((4,) + tile_shape, F32),
            pltpu.VMEM((tokens, channels), BF16),
            pltpu.SemaphoreType.DMA((5,)),
        ],
        "featurize", 6.0, 10,
    )
    if fans == 4:
        pieces.append(exchange(grad_copy, "ch", fans - 1))
    arrived = exchange_states(state, decay_tiles, tokens, 1)

    def weight_scratch(count):
        return [
            pltpu.VMEM((count, channels, channels), BF16),
            pltpu.SemaphoreType.DMA((count,)),
        ]

    pairs = blocks // 2
    conv_out, *partial_sums = call(
        project_kernel,
        [in_hbm(tile_shape, F32)] + [in_hbm((tokens, channels), BF16)] * fans,
        (
            order, position, decay_tiles, scale_tiles, query_feat, local, out_weight, *arrived,
        ),
        [IN_SMEM] * 2 + [IN_VMEM] * 2 + [IN_HBM] * 3 + [IN_VMEM] * pairs,
        [
            tile,
            tile,
            tile,
            pltpu.VMEM((tokens, channels), BF16),
            pltpu.VMEM((fans, channels, channels), BF16),
            pltpu.VMEM((fans, tokens, channels), BF16),
            pltpu.SemaphoreType.DMA((fans + 2,)),
            pltpu.SemaphoreType.DMA((fans,)),
        ],
        "project", 7.0, 16,
    )
    if fans == 4:
        parts = [
            exchange(part, "ch", mask) if mask else part for mask, part in enumerate(partial_sums)
        ]
    else:
        parts = lax.all_to_all(
            jnp.stack(partial_sums), "ch", split_axis=0, concat_axis=0, tiled=True
        )
        parts = [parts[number] for number in range(fans)]
    back_query, grad_mixed, back_state, ahead = call(
        functools.partial(back_last_kernel, rim=rim),
        [in_hbm(tile_shape, F32), (tile_shape, F32), (mode_shape, F32)]
        + [((4, rim * SUB, LANES), F32)],
        (
            order, decay_tiles, out_weight, query_feat, key_feat, value_feat, conv_out, *pieces,
        ),
        [IN_SMEM, IN_VMEM] + [IN_HBM] * (5 + fans),
        [
            pltpu.VMEM((fans, tokens, channels), BF16),
            pltpu.VMEM((fans, channels, tokens), BF16),
            pltpu.VMEM((channels, tokens), F32),
            tile,
            tile,
            tile,
        ]
        + weight_scratch(fans)
        + [pltpu.SemaphoreType.DMA((fans,)), pltpu.SemaphoreType.DMA((5,))],
        "back_last", 9.0, 20,
    )
    back_arrived = exchange_states(back_state, decay_tiles, tokens, -1)
    ahead = shift(ahead, "ctx", -1)
    back_local, grad_query = call(
        functools.partial(back_local_kernel, taps=taps),
        [(tile_shape, F32), in_hbm((tokens, channels), BF16)],
        (grad_mixed, decay_tiles, scale_tiles, tap_tiles, back_query, *pieces[1:]),
        [IN_VMEM] * 4 + [IN_HBM] * fans,
        [
            pltpu.VMEM((wide_rows, LANES), F32),
            tile,
            pltpu.VMEM((tokens, channels), BF16),
            pltpu.SemaphoreType.DMA,
        ],
        "back_local", 4.5, 5,
    )
    tail = 16
    grad_query, grad_key, grad_value, projected = call(
        functools.partial(finish_kernel, taps=taps, pairs=pairs),
        [in_hbm((tokens, channels), BF16)] * 4,
        (
            position, back_local, decay_tiles, scale_tiles, tap_tiles, ahead, back_query,
            key_feat, value_feat, *back_arrived, *parts, grad_query,
        ),
        [IN_SMEM] + [IN_VMEM] * 5 + [IN_HBM] * 3 + [IN_VMEM] * pairs + [IN_HBM] * (1 + fans),
        [
            tile,
            pltpu.VMEM((2,) + tile_shape, F32),
            pltpu.VMEM(((tail + rim) * SUB, LANES), F32),
            pltpu.VMEM((2, wide_rows, LANES), F32),
            tile,
            pltpu.VMEM((tail, channels), BF16),
            pltpu.VMEM((3, tokens, channels), BF16),
            pltpu.VMEM((fans, tokens, channels), BF16),
            pltpu.SemaphoreType.DMA((4,)),
            pltpu.SemaphoreType.DMA((fans,)),
        ],
        "finish", 5.0, 12,
        {9 + pairs + fans: 0},
    )
    return (projected, grad_query, grad_key, grad_value)


def solution(mesh):
    in_specs = (
        P("ctx", "ch"),
        P("ctx", "ch"),
        P("ctx", "ch"),
        P(None, None, "ch"),
        P("ch", None),
        P("ch", None),
        P("ch", None),
        P("ctx", "ch"),
    )
    out_specs = (P("ctx", "ch"), P("ctx", "ch"), P("ctx", "ch"), P("ctx", "ch"))
    return jax.shard_map(shards, mesh=mesh, in_specs=in_specs, out_specs=out_specs, check_vma=False)
```

```python
import functools

import jax
import jax.numpy as jnp
from jax import lax
from jax.experimental import pallas as pl
from jax.experimental.pallas import tpu as pltpu
from jax.sharding import PartitionSpec as P

SUB = 8
LANES = 128
STEP = 8
F32 = jnp.float32
BF16 = jnp.bfloat16


def as_tiles(rows):
    return rows.reshape(rows.shape[0] // SUB, SUB, LANES)


def as_rows(tiles):
    return tiles.reshape(tiles.shape[0] * SUB, LANES)


def tile(ref, token):
    return ref[pl.ds(pl.multiple_of(token * SUB, SUB), SUB), :]


def tree_sum(terms):
    while len(terms) > 1:
        terms = [
            terms[i] + terms[i + 1] if i + 1 < len(terms) else terms[i]
            for i in range(0, len(terms), 2)
        ]
    return terms[0]


def round16(value):
    return value.astype(BF16).astype(F32)


def scatter_tokens(ref, value, first_token):
    tokens, channels = value.shape
    for group in range(channels // LANES):
        ref[pl.ds(first_token * SUB + group, tokens, stride=SUB), :] = value[
            :, group * LANES : (group + 1) * LANES
        ]


def gather_tokens(rows, out_ref):
    for group in range(out_ref.shape[1] // LANES):
        out_ref[:, group * LANES : (group + 1) * LANES] = rows(group).astype(out_ref.dtype)


def group_rows(ref, group, tokens):
    return ref[pl.ds(group, tokens, stride=SUB), :]


def start_all(copies):
    for copy in copies:
        copy.start()
    return copies


def wait_all(copies):
    for copy in copies:
        copy.wait()


def advance_states(signal_ref, factors, states, first, count, reverse):
    last = signal_ref.shape[0] // SUB - 1

    def body(step, states):
        for inner in range(STEP):
            token = first + step * STEP + inner
            u = tile(signal_ref, last - token if reverse else token)
            states = [factor * state + u for factor, state in zip(factors, states)]
        return states

    return lax.fori_loop(0, count // STEP, body, states)


def zero_states(modes):
    return [jnp.zeros((SUB, LANES), F32) for _ in range(modes)]


def mode_rows(n):
    return slice(n * SUB, (n + 1) * SUB)


def fades(decay_ref, tokens):
    return [
        jnp.exp(-decay_ref[mode_rows(n), :] * tokens) for n in range(decay_ref.shape[0] // SUB)
    ]


def write_messages(out_ref, states, decay_ref, position_ref, tokens, direction):
    count = out_ref.shape[0]
    out_ref[...] = jnp.zeros_like(out_ref)
    fade = fades(decay_ref, float(tokens))
    for gap in range(count - 1):
        other = position_ref[0] + direction * (gap + 1)
        value = jnp.concatenate(states, axis=0).astype(out_ref.dtype)

        @pl.when((other >= 0) & (other < count))
        def _():
            out_ref[jnp.clip(other, 0, count - 1)] = value

        states = [state * factor for state, factor in zip(states, fade)]


def read_messages(in_ref):
    total = in_ref[0].astype(F32)
    for other in range(1, in_ref.shape[0]):
        total = total + in_ref[other].astype(F32)
    return [total[mode_rows(n)] for n in range(total.shape[0] // SUB)]


def rim_kernel(
    q_ref, k_ref, v_ref, taps_ref, residue_ref, decay_ref,
    rim_ref, streams_ref, taps_vmem, residue_vmem, decay_vmem, sems,
):
    rows = rim_ref.shape[0] // 3
    streams = (q_ref, k_ref, v_ref)
    rims = [
        pltpu.make_async_copy(
            source.at[pl.ds(source.shape[0] - rows, rows), :],
            rim_ref.at[pl.ds(stream * rows, rows), :],
            sems.at[stream],
        )
        for stream, source in enumerate(streams)
    ]
    pairs = [(source, streams_ref.at[stream]) for stream, source in enumerate(streams)]
    pairs += [(taps_ref, taps_vmem), (residue_ref, residue_vmem), (decay_ref, decay_vmem)]
    others = [
        pltpu.make_async_copy(source, target, sems.at[3 + number])
        for number, (source, target) in enumerate(pairs)
    ]
    wait_all(start_all(rims + others))


def filtered(window, taps_ref, stream, taps, steps, forward):
    total = None
    for tap in range(taps):
        first = taps - 1 - tap if forward else tap
        term = taps_ref[pl.ds((stream * taps + tap) * SUB, SUB), :] * window[first : first + steps]
        total = term if total is None else total + term
    return total


def featurize_kernel(
    position_ref, streams_ref, taps_in_ref, residue_ref, decay_in_ref, halo_ref, grad_in_ref,
    qf_ref, kf_ref, vf_ref, local_ref, grad_copy_ref, message_ref, taps_ref, scale_ref, decay_ref,
    wide_ref, feat_ref, grad_vmem, sems,
):
    grad_in = pltpu.make_async_copy(grad_in_ref, grad_vmem, sems.at[4])
    grad_in.start()
    tokens = streams_ref.shape[1]
    _, taps, _ = taps_in_ref.shape
    rim = taps - 1
    modes = decay_in_ref.shape[0]
    held = halo_ref.shape[0] // 3
    decays = decay_in_ref[...]
    scatter_tokens(decay_ref, decays, 0)
    scatter_tokens(scale_ref, residue_ref[...] * jnp.sqrt(decays), 0)
    for stream in range(3):
        scatter_tokens(taps_ref, taps_in_ref[stream], stream * taps)
        behind = halo_ref[stream * held : (stream + 1) * held, :].astype(F32)
        scatter_tokens(wide_ref.at[stream], behind[held - rim :], 0)
        scatter_tokens(wide_ref.at[stream], streams_ref[stream].astype(F32), rim)

    def body(step, carry):
        begin = pl.multiple_of(step * STEP * SUB, SUB)
        rows = pl.ds(begin, STEP * SUB)
        feats = []
        for stream in range(3):
            window = as_tiles(wide_ref[stream, pl.ds(begin, (STEP + rim) * SUB), :])
            feats.append(filtered(window, taps_ref, stream, taps, STEP, True))
            feat_ref[stream, rows, :] = as_rows(feats[-1])
        feat_ref[3, rows, :] = as_rows(round16(feats[1] * feats[2]))
        return carry

    lax.fori_loop(0, tokens // STEP, body, 0)
    grad_in.wait()
    copies = start_all(
        [
            pltpu.make_async_copy(source, target, sems.at[number])
            for number, (source, target) in enumerate(
                (
                    (feat_ref.at[0], qf_ref),
                    (feat_ref.at[1], kf_ref),
                    (feat_ref.at[2], vf_ref),
                    (grad_vmem, grad_copy_ref),
                )
            )
        ]
    )
    local_vmem = wide_ref.at[0, pl.ds(0, tokens * SUB), :]
    states = local_conv(feat_ref.at[3], decay_ref, scale_ref, local_vmem, False)
    copies += start_all([pltpu.make_async_copy(local_vmem, local_ref, sems.at[4])])
    write_messages(message_ref, states, decay_ref, position_ref, tokens, 1)
    wait_all(copies)


def scales_of(scale_ref):
    return [scale_ref[mode_rows(n), :] for n in range(scale_ref.shape[0] // SUB)]


def local_conv(signal_ref, decay_ref, scale_ref, out_ref, reverse):
    tokens = signal_ref.shape[0] // SUB
    factors = fades(decay_ref, 1.0)
    scales = scales_of(scale_ref)

    def body(step, states):
        for inner in range(STEP):
            token = step * STEP + inner
            token = tokens - 1 - token if reverse else token
            u = tile(signal_ref, token)
            states = [factor * state + u for factor, state in zip(factors, states)]
            out_ref[pl.ds(pl.multiple_of(token * SUB, SUB), SUB), :] = tree_sum(
                [scale * state for scale, state in zip(scales, states)]
            )
        return states

    return lax.fori_loop(0, tokens // STEP, body, zero_states(len(factors)))


def carried(out_ref, states, decay_ref, scale_ref, reverse, local_ref=None):
    tokens = out_ref.shape[0] // SUB
    factors = fades(decay_ref, 1.0)
    scaled = [scale * state for scale, state in zip(scales_of(scale_ref), states)]

    def body(step, scaled):
        for inner in range(STEP):
            token = step * STEP + inner
            token = tokens - 1 - token if reverse else token
            scaled = [factor * state for factor, state in zip(factors, scaled)]
            rows = pl.ds(pl.multiple_of(token * SUB, SUB), SUB)
            total = tree_sum(list(scaled))
            out_ref[rows, :] = total if local_ref is None else local_ref[rows, :] + total
        return scaled

    lax.fori_loop(0, tokens // STEP, body, scaled)


def project_kernel(
    index_ref, message_ref, decay_ref, scale_ref, _, qf_ref, local_ref, weight_ref, *refs
):
    rows_ref, feat_ref, local_vmem, gated_ref, held_ref, sent_ref, sems, out_sems = refs[-8:]
    conv_ref, *out_refs = refs[-9 - sent_ref.shape[0] : -8]
    parts, tokens, width = sent_ref.shape
    order = list(reversed(range(parts)))
    copies = [
        pltpu.make_async_copy(
            weight_ref.at[:, pl.ds(pl.multiple_of(index_ref[part] * width, width), width)],
            held_ref.at[part],
            sems.at[part],
        )
        for part in range(parts)
    ]
    outs = [
        pltpu.make_async_copy(sent_ref.at[part], out_refs[part], out_sems.at[part])
        for part in range(parts)
    ]
    local_copy = pltpu.make_async_copy(local_ref, local_vmem, sems.at[parts + 1])
    feat_copy = pltpu.make_async_copy(qf_ref, feat_ref, sems.at[parts])
    start_all([local_copy, feat_copy])
    start_all([copies[part] for part in order])
    carried(rows_ref, read_messages(message_ref), decay_ref, scale_ref, False)
    local_copy.wait()
    rows_ref[...] += local_vmem[...]
    conv_copy = pltpu.make_async_copy(rows_ref, conv_ref, sems.at[parts + 1])
    conv_copy.start()
    feat_copy.wait()
    gather_tokens(
        lambda group: group_rows(rows_ref, group, tokens) * group_rows(feat_ref, group, tokens),
        gated_ref,
    )
    for part in order:
        copies[part].wait()
        sent_ref[part] = jnp.dot(
            gated_ref[...], held_ref[part], preferred_element_type=F32
        ).astype(sent_ref.dtype)
        outs[part].start()
    conv_copy.wait()
    wait_all(outs)


def start_weights(index_ref, first, weight_ref, held_ref, sems):
    count, _, width = held_ref.shape
    return start_all(
        [
            pltpu.make_async_copy(
                weight_ref.at[
                    :, pl.ds(pl.multiple_of(index_ref[first + number] * width, width), width)
                ],
                held_ref.at[number],
                sems.at[number],
            )
            for number in range(count)
        ]
    )


def back_products(weights, piece_refs, turned_ref, held_ref, total_ref, before_ref):
    for number, ref in enumerate(piece_refs):
        turned_ref[number] = ref[...].T
    for number in range(len(piece_refs)):
        weights[number].wait()
        product = jnp.dot(held_ref[number], turned_ref[number], preferred_element_type=F32)
        earlier = before_ref if number == 0 else total_ref
        total_ref[...] = product if earlier is None else earlier[...] + product


def middle_kernel(index_ref, weight_ref, *refs):
    *piece_refs, total_ref, piece_vmem, turned_ref, held_ref, sems, piece_sems = refs
    pieces = start_all(
        [
            pltpu.make_async_copy(ref, piece_vmem.at[number], piece_sems.at[number])
            for number, ref in enumerate(piece_refs)
        ]
    )
    weights = start_weights(index_ref, 0, weight_ref, held_ref, sems)
    wait_all(pieces)
    held = [piece_vmem.at[number] for number in range(len(piece_refs))]
    back_products(weights, held, turned_ref, held_ref, total_ref, None)


def back_last_kernel(
    index_ref, position_ref, base_ref, decay_ref, weight_ref, qf_ref, kf_ref, vf_ref, conv_ref,
    *refs, rim,
):
    (
        *piece_refs, back_query_ref, mixed_ref, message_ref, ahead_ref, piece_vmem,
        turned_ref, total_ref, rows_ref, feat_ref, conv_vmem, held_ref, sems, piece_sems, own_sems,
    ) = refs
    piece_refs = piece_refs[-turned_ref.shape[0] :]
    pieces = start_all(
        [
            pltpu.make_async_copy(ref, piece_vmem.at[number], piece_sems.at[number])
            for number, ref in enumerate(piece_refs)
        ]
    )
    tokens = total_ref.shape[1]
    heads = pl.ds(0, rim * SUB)
    weights = start_weights(
        index_ref, index_ref.shape[0] - len(piece_refs), weight_ref, held_ref, sems
    )
    copies = start_all(
        [
            pltpu.make_async_copy(qf_ref, feat_ref, own_sems.at[0]),
            pltpu.make_async_copy(conv_ref, conv_vmem, own_sems.at[1]),
            pltpu.make_async_copy(kf_ref.at[heads, :], ahead_ref.at[2], own_sems.at[2]),
            pltpu.make_async_copy(vf_ref.at[heads, :], ahead_ref.at[3], own_sems.at[3]),
        ]
    )
    wait_all(pieces)
    held = [piece_vmem.at[number] for number in range(len(piece_refs))]
    back_products(weights, held, turned_ref, held_ref, total_ref, base_ref)
    scatter_tokens(rows_ref, total_ref[...].T, 0)
    wait_all(copies)
    mixed_ref[...] = round16(rows_ref[...] * feat_ref[...])
    rows_ref[...] = round16(rows_ref[...] * conv_vmem[...])
    out = pltpu.make_async_copy(rows_ref, back_query_ref, own_sems.at[4])
    out.start()
    ahead_ref[0] = rows_ref[: rim * SUB, :]
    ahead_ref[1] = mixed_ref[: rim * SUB, :]
    modes = decay_ref.shape[0] // SUB
    states = advance_states(
        mixed_ref, fades(decay_ref, 1.0), zero_states(modes), 0, tokens, True
    )
    write_messages(message_ref, states, decay_ref, position_ref, tokens, -1)
    out.wait()


def spread_back(wide_ref, taps_ref, stream, taps, rows_ref, out_ref):
    tokens = out_ref.shape[0]

    def body(step, carry):
        first = pl.multiple_of(step * STEP * SUB, SUB)
        window = as_tiles(wide_ref[pl.ds(first, (STEP + taps - 1) * SUB), :])
        rows_ref[pl.ds(first, STEP * SUB), :] = as_rows(
            filtered(window, taps_ref, stream, taps, STEP, False)
        )
        return carry

    lax.fori_loop(0, tokens // STEP, body, 0)
    gather_tokens(lambda group: group_rows(rows_ref, group, tokens), out_ref)


def back_local_kernel(
    signal_ref, decay_ref, scale_ref, taps_ref, query_ref, *refs, taps
):
    local_ref, gq_ref, wide_ref, rows_ref, out_vmem, sem = refs[-6:]
    inside = query_ref.shape[0]
    copy = pltpu.make_async_copy(query_ref, wide_ref.at[pl.ds(0, inside), :], sem)
    copy.start()
    local_conv(signal_ref, decay_ref, scale_ref, local_ref, True)
    copy.wait()
    rest = (taps - 1) * SUB
    wide_ref[pl.ds(inside, rest), :] = jnp.zeros((rest, LANES), F32)
    spread_back(wide_ref, taps_ref, 0, taps, rows_ref, out_vmem)
    out = pltpu.make_async_copy(out_vmem, gq_ref, sem)
    out.start()
    out.wait()


def finish_kernel(
    message_ref, local_ref, decay_ref, scale_ref, taps_ref, ahead_ref, query_ref, kf_ref, vf_ref,
    *refs, taps,
):
    (
        *part_refs, _, gq_ref, gk_ref, gv_ref, projected_ref,
        total_ref, feat_ref, query_vmem, wide_ref, rows_ref, tail_ref, out_vmem, parts_vmem,
        sems, part_sems,
    ) = refs
    tokens = gk_ref.shape[0]
    tail = tail_ref.shape[0]
    rim = taps - 1
    inside = pl.ds(0, tokens * SUB)
    copies = start_all(
        [
            pltpu.make_async_copy(
                query_ref.at[pl.ds((tokens - tail) * SUB, tail * SUB), :],
                query_vmem.at[pl.ds(0, tail * SUB), :],
                sems.at[0],
            ),
            pltpu.make_async_copy(vf_ref, feat_ref.at[0], sems.at[1]),
            pltpu.make_async_copy(kf_ref, feat_ref.at[1], sems.at[2]),
        ]
    )
    parts = start_all(
        [
            pltpu.make_async_copy(ref, parts_vmem.at[number], part_sems.at[number])
            for number, ref in enumerate(part_refs)
        ]
    )
    states = read_messages(message_ref)
    carried(total_ref, states, decay_ref, scale_ref, True, local_ref)
    growth = fades(decay_ref, -1.0)
    scales = scales_of(scale_ref)
    for ahead in range(rim):
        rows = pl.ds((tokens + ahead) * SUB, SUB)
        theirs = pl.ds(ahead * SUB, SUB)
        grad_conv = tree_sum([scale * state for scale, state in zip(scales, states)])
        query_vmem[pl.ds((tail + ahead) * SUB, SUB), :] = ahead_ref[0, theirs, :]
        wide_ref[0, rows, :] = round16(grad_conv * ahead_ref[3, theirs, :])
        wide_ref[1, rows, :] = round16(grad_conv * ahead_ref[2, theirs, :])
        arrived = ahead_ref[1, theirs, :]
        states = [(state - arrived) * grow for state, grow in zip(states, growth)]
    copies[0].wait()
    spread_back(query_vmem, taps_ref, 0, taps, rows_ref, tail_ref)
    outs = [
        pltpu.make_async_copy(tail_ref, gq_ref.at[pl.ds(tokens - tail, tail), :], sems.at[0])
    ]
    wait_all(parts)
    out_vmem[2] = tree_sum(
        [parts_vmem[number].astype(F32) for number in range(len(part_refs))]
    ).astype(out_vmem.dtype)
    outs.append(pltpu.make_async_copy(out_vmem.at[2], projected_ref, sems.at[3]))
    start_all(outs)
    for stream, out_ref in enumerate((gk_ref, gv_ref)):
        copies[1 + stream].wait()
        wide_ref[stream, inside, :] = round16(total_ref[...] * feat_ref[stream])
        spread_back(
            wide_ref.at[stream], taps_ref, 1 + stream, taps, rows_ref, out_vmem.at[stream]
        )
        outs.append(pltpu.make_async_copy(out_vmem.at[stream], out_ref, sems.at[1 + stream]))
        outs[-1].start()
    wait_all(outs)


IN_VMEM = pl.BlockSpec(memory_space=pltpu.VMEM)
IN_SMEM = pl.BlockSpec(memory_space=pltpu.SMEM)
IN_HBM = pl.BlockSpec(memory_space=pltpu.HBM)
HBM_RATE = 3.5e6


def in_hbm(shape, kind):
    return pltpu.HBM(shape, kind)


def call(kernel, outs, args, specs, scratch, name, micros, mebibytes, aliases=None):
    args = [
        pltpu.with_memory_space_constraint(arg, pltpu.HBM) if spec is IN_HBM else arg
        for arg, spec in zip(args, specs)
    ]
    held = [isinstance(out, tuple) for out in outs]
    return pl.pallas_call(
        kernel,
        out_shape=[jax.ShapeDtypeStruct(*out) if own else out for own, out in zip(held, outs)],
        in_specs=specs,
        out_specs=[IN_VMEM if own else IN_HBM for own in held],
        scratch_shapes=scratch,
        compiler_params=pltpu.CompilerParams(vmem_limit_bytes=mebibytes * 1024 * 1024),
        cost_estimate=pl.CostEstimate(
            flops=0, bytes_accessed=int(micros * HBM_RATE), transcendentals=0
        ),
        name=name,
        input_output_aliases=aliases or {},
    )(*args)


def shift(value, axis, steps):
    count = lax.axis_size(axis)
    pairs = [(s, s + steps) for s in range(count) if 0 <= s + steps < count]
    return lax.ppermute(value, axis, pairs)


def exchange(value, axis, mask):
    count = lax.axis_size(axis)
    return lax.ppermute(value, axis, [(s, s ^ mask) for s in range(count)])


def shards(query_in, key_in, value_in, short_taps, residues, decays, out_weight, out_grad):
    tokens, channels = query_in.shape
    taps = short_taps.shape[0]
    rim = taps - 1
    modes = decays.shape[1]
    blocks = lax.axis_size("ctx")
    fans = lax.axis_size("ch")
    position = lax.axis_index("ctx")[None].astype(jnp.int32)
    tile_shape = (tokens * SUB, LANES)
    mode_shape = (modes * SUB, LANES)
    message_shape = (blocks,) + mode_shape
    streams = (query_in, key_in, value_in)
    rim_rows = 16

    tap_rows = jnp.transpose(short_taps, (1, 0, 2))
    halo, narrow, taps_vmem, residues_vmem, decays_vmem = call(
        rim_kernel,
        [
            ((3 * rim_rows, channels), BF16),
            ((3, tokens, channels), BF16),
            ((3, taps, channels), F32),
            ((modes, channels), F32),
            ((modes, channels), F32),
        ],
        streams + (tap_rows, residues.T, decays.T), [IN_HBM] * 6,
        [pltpu.SemaphoreType.DMA((9,))], "rim", 1.2, 2,
    )
    halo, out_grad = lax.optimization_barrier((halo, out_grad))
    halo = shift(halo, "ctx", 1)
    if fans == 4:
        masks = (0, 2, 1, 3)
        order = lax.axis_index("ch") ^ jnp.asarray(masks, dtype=jnp.int32)
        pieces = [out_grad, exchange(out_grad, "ch", masks[1])]
    else:
        order = jnp.arange(fans, dtype=jnp.int32)
        everyone = lax.all_gather(out_grad, "ch", axis=0, tiled=False)
        pieces = [everyone[number] for number in range(fans)]
    tile = pltpu.VMEM(tile_shape, F32)
    wide_rows = (tokens + rim) * SUB

    (
        query_feat, key_feat, value_feat, local, grad_copy, messages,
        tap_tiles, scale_tiles, decay_tiles,
    ) = call(
        featurize_kernel,
        [in_hbm(tile_shape, F32)] * 4
        + [in_hbm((tokens, channels), BF16), (message_shape, BF16)]
        + [((3 * taps * SUB, LANES), F32), (mode_shape, F32), (mode_shape, F32)],
        (position, narrow, taps_vmem, residues_vmem, decays_vmem, halo, out_grad),
        [IN_SMEM] + [IN_VMEM] * 5 + [IN_HBM],
        [
            pltpu.VMEM((3, wide_rows, LANES), F32),
            pltpu.VMEM((4,) + tile_shape, F32),
            pltpu.VMEM((tokens, channels), BF16),
            pltpu.SemaphoreType.DMA((5,)),
        ],
        "featurize", 6.0, 10,
    )
    if fans == 4:
        pieces += [exchange(grad_copy, "ch", mask) for mask in masks[2:]]
    arrived = lax.all_to_all(messages, "ctx", split_axis=0, concat_axis=0, tiled=True)

    def weight_scratch(count):
        return [
            pltpu.VMEM((count, channels, channels), BF16),
            pltpu.SemaphoreType.DMA((count,)),
        ]

    early = fans // 2
    (base,) = call(
        middle_kernel,
        [((channels, tokens), F32)],
        (order, out_weight, *pieces[:early]),
        [IN_SMEM] + [IN_HBM] * (1 + early),
        [
            pltpu.VMEM((early, tokens, channels), BF16),
            pltpu.VMEM((early, channels, tokens), BF16),
        ]
        + weight_scratch(early)
        + [pltpu.SemaphoreType.DMA((early,))],
        "middle", 6.0, 11,
    )
    conv_out, *partial_sums = call(
        project_kernel,
        [in_hbm(tile_shape, F32)] + [in_hbm((tokens, channels), BF16)] * fans,
        (
            order, arrived, decay_tiles, scale_tiles, base, query_feat, local, out_weight,
            *pieces[1:early],
        ),
        [IN_SMEM] + [IN_VMEM] * 4 + [IN_HBM] * (2 + early),
        [
            tile,
            tile,
            tile,
            pltpu.VMEM((tokens, channels), BF16),
            pltpu.VMEM((fans, channels, channels), BF16),
            pltpu.VMEM((fans, tokens, channels), BF16),
            pltpu.SemaphoreType.DMA((fans + 2,)),
            pltpu.SemaphoreType.DMA((fans,)),
        ],
        "project", 7.0, 16,
    )
    if fans == 4:
        parts = [
            exchange(part, "ch", mask) if mask else part
            for mask, part in zip(masks, partial_sums)
        ]
    else:
        parts = lax.all_to_all(
            jnp.stack(partial_sums), "ch", split_axis=0, concat_axis=0, tiled=True
        )
        parts = [parts[number] for number in range(fans)]
    back_query, grad_mixed, back_messages, ahead = call(
        functools.partial(back_last_kernel, rim=rim),
        [in_hbm(tile_shape, F32), (tile_shape, F32), (message_shape, BF16)]
        + [((4, rim * SUB, LANES), F32)],
        (
            order, position, base, decay_tiles, out_weight, query_feat, key_feat,
            value_feat, conv_out, *pieces[1:early], *pieces[early:],
        ),
        [IN_SMEM] * 2 + [IN_VMEM] * 2 + [IN_HBM] * (4 + fans),
        [
            pltpu.VMEM((fans - early, tokens, channels), BF16),
            pltpu.VMEM((fans - early, channels, tokens), BF16),
            pltpu.VMEM((channels, tokens), F32),
            tile,
            tile,
            tile,
        ]
        + weight_scratch(fans - early)
        + [pltpu.SemaphoreType.DMA((fans - early,)), pltpu.SemaphoreType.DMA((5,))],
        "back_last", 7.0, 13,
    )
    back_arrived = lax.all_to_all(back_messages, "ctx", split_axis=0, concat_axis=0, tiled=True)
    ahead = shift(ahead, "ctx", -1)
    back_local, grad_query = call(
        functools.partial(back_local_kernel, taps=taps),
        [(tile_shape, F32), in_hbm((tokens, channels), BF16)],
        (grad_mixed, decay_tiles, scale_tiles, tap_tiles, back_query, *pieces[early:]),
        [IN_VMEM] * 4 + [IN_HBM] * (1 + fans - early),
        [
            pltpu.VMEM((wide_rows, LANES), F32),
            tile,
            pltpu.VMEM((tokens, channels), BF16),
            pltpu.SemaphoreType.DMA,
        ],
        "back_local", 4.5, 5,
    )
    tail = 16
    grad_query, grad_key, grad_value, projected = call(
        functools.partial(finish_kernel, taps=taps),
        [in_hbm((tokens, channels), BF16)] * 4,
        (
            back_arrived, back_local, decay_tiles, scale_tiles, tap_tiles, ahead, back_query,
            key_feat, value_feat, *parts, grad_query,
        ),
        [IN_VMEM] * 6 + [IN_HBM] * (4 + fans),
        [
            tile,
            pltpu.VMEM((2,) + tile_shape, F32),
            pltpu.VMEM(((tail + rim) * SUB, LANES), F32),
            pltpu.VMEM((2, wide_rows, LANES), F32),
            tile,
            pltpu.VMEM((tail, channels), BF16),
            pltpu.VMEM((3, tokens, channels), BF16),
            pltpu.VMEM((fans, tokens, channels), BF16),
            pltpu.SemaphoreType.DMA((4,)),
            pltpu.SemaphoreType.DMA((fans,)),
        ],
        "finish", 5.0, 12,
        {9 + fans: 0},
    )
    return (projected, grad_query, grad_key, grad_value)


def solution(mesh):
    in_specs = (
        P("ctx", "ch"),
        P("ctx", "ch"),
        P("ctx", "ch"),
        P(None, None, "ch"),
        P("ch", None),
        P("ch", None),
        P("ch", None),
        P("ctx", "ch"),
    )
    out_specs = (P("ctx", "ch"), P("ctx", "ch"), P("ctx", "ch"), P("ctx", "ch"))
    return jax.shard_map(shards, mesh=mesh, in_specs=in_specs, out_specs=out_specs, check_vma=False)
```

```python
import functools

import jax
import jax.numpy as jnp
from jax import lax
from jax.experimental import pallas as pl
from jax.experimental.pallas import tpu as pltpu
from jax.sharding import PartitionSpec as P

SUB = 8
LANES = 128
STEP = 8
F32 = jnp.float32
BF16 = jnp.bfloat16


def as_tiles(rows):
    return rows.reshape(rows.shape[0] // SUB, SUB, LANES)


def as_rows(tiles):
    return tiles.reshape(tiles.shape[0] * SUB, LANES)


def tile(ref, token):
    return ref[pl.ds(pl.multiple_of(token * SUB, SUB), SUB), :]


def tree_sum(terms):
    while len(terms) > 1:
        terms = [
            terms[i] + terms[i + 1] if i + 1 < len(terms) else terms[i]
            for i in range(0, len(terms), 2)
        ]
    return terms[0]


def round16(value):
    return value.astype(BF16).astype(F32)


def scatter_tokens(ref, value, first_token):
    tokens, channels = value.shape
    for group in range(channels // LANES):
        ref[pl.ds(first_token * SUB + group, tokens, stride=SUB), :] = value[
            :, group * LANES : (group + 1) * LANES
        ]


def gather_tokens(rows, out_ref):
    for group in range(out_ref.shape[1] // LANES):
        out_ref[:, group * LANES : (group + 1) * LANES] = rows(group).astype(out_ref.dtype)


def group_rows(ref, group, tokens):
    return ref[pl.ds(group, tokens, stride=SUB), :]


def start_all(copies):
    for copy in copies:
        copy.start()
    return copies


def wait_all(copies):
    for copy in copies:
        copy.wait()


def advance_states(signal_ref, factors, states, first, count, reverse):
    last = signal_ref.shape[0] // SUB - 1

    def body(step, states):
        for inner in range(STEP):
            token = first + step * STEP + inner
            u = tile(signal_ref, last - token if reverse else token)
            states = [factor * state + u for factor, state in zip(factors, states)]
        return states

    return lax.fori_loop(0, count // STEP, body, states)


def zero_states(modes):
    return [jnp.zeros((SUB, LANES), F32) for _ in range(modes)]


def mode_rows(n):
    return slice(n * SUB, (n + 1) * SUB)


def fades(decay_ref, tokens):
    return [
        jnp.exp(-decay_ref[mode_rows(n), :] * tokens) for n in range(decay_ref.shape[0] // SUB)
    ]


def write_messages(out_ref, states, decay_ref, position_ref, tokens, direction):
    count = out_ref.shape[0]
    out_ref[...] = jnp.zeros_like(out_ref)
    fade = fades(decay_ref, float(tokens))
    for gap in range(count - 1):
        other = position_ref[0] + direction * (gap + 1)
        value = jnp.concatenate(states, axis=0).astype(out_ref.dtype)

        @pl.when((other >= 0) & (other < count))
        def _():
            out_ref[jnp.clip(other, 0, count - 1)] = value

        states = [state * factor for state, factor in zip(states, fade)]


def read_messages(in_ref):
    total = in_ref[0].astype(F32)
    for other in range(1, in_ref.shape[0]):
        total = total + in_ref[other].astype(F32)
    return [total[mode_rows(n)] for n in range(total.shape[0] // SUB)]


def rim_kernel(
    q_ref, k_ref, v_ref, taps_ref, residue_ref, decay_ref,
    rim_ref, streams_ref, taps_vmem, residue_vmem, decay_vmem, sems,
):
    rows = rim_ref.shape[0] // 3
    streams = (q_ref, k_ref, v_ref)
    rims = [
        pltpu.make_async_copy(
            source.at[pl.ds(source.shape[0] - rows, rows), :],
            rim_ref.at[pl.ds(stream * rows, rows), :],
            sems.at[stream],
        )
        for stream, source in enumerate(streams)
    ]
    pairs = [(source, streams_ref.at[stream]) for stream, source in enumerate(streams)]
    pairs += [(taps_ref, taps_vmem), (residue_ref, residue_vmem), (decay_ref, decay_vmem)]
    others = [
        pltpu.make_async_copy(source, target, sems.at[3 + number])
        for number, (source, target) in enumerate(pairs)
    ]
    wait_all(start_all(rims + others))


def filtered(window, taps_ref, stream, taps, steps, forward):
    total = None
    for tap in range(taps):
        first = taps - 1 - tap if forward else tap
        term = taps_ref[pl.ds((stream * taps + tap) * SUB, SUB), :] * window[first : first + steps]
        total = term if total is None else total + term
    return total


def featurize_kernel(
    position_ref, streams_ref, taps_in_ref, residue_ref, decay_in_ref, halo_ref, grad_in_ref,
    qf_ref, kf_ref, vf_ref, local_ref, grad_copy_ref, message_ref, taps_ref, scale_ref, decay_ref,
    wide_ref, feat_ref, grad_vmem, sems,
):
    grad_in = pltpu.make_async_copy(grad_in_ref, grad_vmem, sems.at[4])
    grad_in.start()
    tokens = streams_ref.shape[1]
    _, taps, _ = taps_in_ref.shape
    rim = taps - 1
    modes = decay_in_ref.shape[0]
    held = halo_ref.shape[0] // 3
    decays = decay_in_ref[...]
    scatter_tokens(decay_ref, decays, 0)
    scatter_tokens(scale_ref, residue_ref[...] * jnp.sqrt(decays), 0)
    for stream in range(3):
        scatter_tokens(taps_ref, taps_in_ref[stream], stream * taps)
        behind = halo_ref[stream * held : (stream + 1) * held, :].astype(F32)
        scatter_tokens(wide_ref.at[stream], behind[held - rim :], 0)
        scatter_tokens(wide_ref.at[stream], streams_ref[stream].astype(F32), rim)

    def body(step, carry):
        begin = pl.multiple_of(step * STEP * SUB, SUB)
        rows = pl.ds(begin, STEP * SUB)
        feats = []
        for stream in range(3):
            window = as_tiles(wide_ref[stream, pl.ds(begin, (STEP + rim) * SUB), :])
            feats.append(filtered(window, taps_ref, stream, taps, STEP, True))
            feat_ref[stream, rows, :] = as_rows(feats[-1])
        feat_ref[3, rows, :] = as_rows(round16(feats[1] * feats[2]))
        return carry

    lax.fori_loop(0, tokens // STEP, body, 0)
    grad_in.wait()
    copies = start_all(
        [
            pltpu.make_async_copy(source, target, sems.at[number])
            for number, (source, target) in enumerate(
                (
                    (feat_ref.at[0], qf_ref),
                    (feat_ref.at[1], kf_ref),
                    (feat_ref.at[2], vf_ref),
                    (grad_vmem, grad_copy_ref),
                )
            )
        ]
    )
    local_vmem = wide_ref.at[0, pl.ds(0, tokens * SUB), :]
    states = local_conv(feat_ref.at[3], decay_ref, scale_ref, local_vmem, False)
    copies += start_all([pltpu.make_async_copy(local_vmem, local_ref, sems.at[4])])
    write_messages(message_ref, states, decay_ref, position_ref, tokens, 1)
    wait_all(copies)


def scales_of(scale_ref):
    return [scale_ref[mode_rows(n), :] for n in range(scale_ref.shape[0] // SUB)]


def local_conv(signal_ref, decay_ref, scale_ref, out_ref, reverse):
    tokens = signal_ref.shape[0] // SUB
    factors = fades(decay_ref, 1.0)
    scales = scales_of(scale_ref)

    def body(step, states):
        for inner in range(STEP):
            token = step * STEP + inner
            token = tokens - 1 - token if reverse else token
            u = tile(signal_ref, token)
            states = [factor * state + u for factor, state in zip(factors, states)]
            out_ref[pl.ds(pl.multiple_of(token * SUB, SUB), SUB), :] = tree_sum(
                [scale * state for scale, state in zip(scales, states)]
            )
        return states

    return lax.fori_loop(0, tokens // STEP, body, zero_states(len(factors)))


def carried(out_ref, states, decay_ref, scale_ref, reverse, local_ref=None):
    tokens = out_ref.shape[0] // SUB
    factors = fades(decay_ref, 1.0)
    scaled = [scale * state for scale, state in zip(scales_of(scale_ref), states)]

    def body(step, scaled):
        for inner in range(STEP):
            token = step * STEP + inner
            token = tokens - 1 - token if reverse else token
            scaled = [factor * state for factor, state in zip(factors, scaled)]
            rows = pl.ds(pl.multiple_of(token * SUB, SUB), SUB)
            total = tree_sum(list(scaled))
            out_ref[rows, :] = total if local_ref is None else local_ref[rows, :] + total
        return scaled

    lax.fori_loop(0, tokens // STEP, body, scaled)


def project_kernel(
    index_ref, message_ref, decay_ref, scale_ref, _, qf_ref, local_ref, weight_ref, *refs
):
    rows_ref, feat_ref, local_vmem, gated_ref, held_ref, sent_ref, sems, out_sems = refs[-8:]
    conv_ref, gated_out_ref, *out_refs = refs[-10 - sent_ref.shape[0] : -8]
    parts, tokens, width = sent_ref.shape
    offset = index_ref.shape[0] - parts
    order = list(reversed(range(parts)))
    copies = [
        pltpu.make_async_copy(
            weight_ref.at[
                :, pl.ds(pl.multiple_of(index_ref[offset + part] * width, width), width)
            ],
            held_ref.at[part],
            sems.at[part],
        )
        for part in range(parts)
    ]
    outs = [
        pltpu.make_async_copy(sent_ref.at[part], out_refs[part], out_sems.at[part])
        for part in range(parts)
    ]
    local_copy = pltpu.make_async_copy(local_ref, local_vmem, sems.at[parts + 1])
    feat_copy = pltpu.make_async_copy(qf_ref, feat_ref, sems.at[parts])
    start_all([local_copy, feat_copy])
    start_all([copies[part] for part in order])
    carried(rows_ref, read_messages(message_ref), decay_ref, scale_ref, False)
    local_copy.wait()
    rows_ref[...] += local_vmem[...]
    conv_copy = pltpu.make_async_copy(rows_ref, conv_ref, sems.at[parts + 1])
    conv_copy.start()
    feat_copy.wait()
    gather_tokens(
        lambda group: group_rows(rows_ref, group, tokens) * group_rows(feat_ref, group, tokens),
        gated_ref,
    )
    gated_copy = pltpu.make_async_copy(gated_ref, gated_out_ref, out_sems.at[parts])
    gated_copy.start()
    for part in order:
        copies[part].wait()
        sent_ref[part] = jnp.dot(
            gated_ref[...], held_ref[part], preferred_element_type=F32
        ).astype(sent_ref.dtype)
        outs[part].start()
    wait_all([conv_copy, gated_copy] + outs)


def start_weights(index_ref, first, weight_ref, held_ref, sems):
    count, _, width = held_ref.shape
    return start_all(
        [
            pltpu.make_async_copy(
                weight_ref.at[
                    :, pl.ds(pl.multiple_of(index_ref[first + number] * width, width), width)
                ],
                held_ref.at[number],
                sems.at[number],
            )
            for number in range(count)
        ]
    )


def back_products(weights, piece_refs, turned_ref, held_ref, total_ref, before_ref):
    for number, ref in enumerate(piece_refs):
        turned_ref[number] = ref[...].T
    for number in range(len(piece_refs)):
        weights[number].wait()
        product = jnp.dot(held_ref[number], turned_ref[number], preferred_element_type=F32)
        earlier = before_ref if number == 0 else total_ref
        total_ref[...] = product if earlier is None else earlier[...] + product


def middle_kernel(index_ref, weight_ref, *refs):
    *piece_refs, total_ref, piece_vmem, turned_ref, held_ref, sems, piece_sems = refs
    pieces = start_all(
        [
            pltpu.make_async_copy(ref, piece_vmem.at[number], piece_sems.at[number])
            for number, ref in enumerate(piece_refs)
        ]
    )
    weights = start_weights(index_ref, 0, weight_ref, held_ref, sems)
    wait_all(pieces)
    held = [piece_vmem.at[number] for number in range(len(piece_refs))]
    back_products(weights, held, turned_ref, held_ref, total_ref, None)


def back_last_kernel(
    index_ref, position_ref, base_ref, decay_ref, weight_ref, qf_ref, kf_ref, vf_ref, conv_ref,
    *refs, rim,
):
    (
        *piece_refs, back_query_ref, mixed_ref, message_ref, ahead_ref,
        turned_ref, total_ref, rows_ref, feat_ref, conv_vmem, held_ref, sems, own_sems,
    ) = refs
    tokens = total_ref.shape[1]
    heads = pl.ds(0, rim * SUB)
    weights = start_weights(
        index_ref, index_ref.shape[0] - len(piece_refs), weight_ref, held_ref, sems
    )
    copies = start_all(
        [
            pltpu.make_async_copy(qf_ref, feat_ref, own_sems.at[0]),
            pltpu.make_async_copy(conv_ref, conv_vmem, own_sems.at[1]),
            pltpu.make_async_copy(kf_ref.at[heads, :], ahead_ref.at[2], own_sems.at[2]),
            pltpu.make_async_copy(vf_ref.at[heads, :], ahead_ref.at[3], own_sems.at[3]),
        ]
    )
    back_products(weights, piece_refs, turned_ref, held_ref, total_ref, base_ref)
    scatter_tokens(rows_ref, total_ref[...].T, 0)
    wait_all(copies)
    mixed_ref[...] = round16(rows_ref[...] * feat_ref[...])
    rows_ref[...] = round16(rows_ref[...] * conv_vmem[...])
    out = pltpu.make_async_copy(rows_ref, back_query_ref, own_sems.at[4])
    out.start()
    ahead_ref[0] = rows_ref[: rim * SUB, :]
    ahead_ref[1] = mixed_ref[: rim * SUB, :]
    modes = decay_ref.shape[0] // SUB
    states = advance_states(
        mixed_ref, fades(decay_ref, 1.0), zero_states(modes), 0, tokens, True
    )
    write_messages(message_ref, states, decay_ref, position_ref, tokens, -1)
    out.wait()


def spread_back(wide_ref, taps_ref, stream, taps, rows_ref, out_ref):
    tokens = out_ref.shape[0]

    def body(step, carry):
        first = pl.multiple_of(step * STEP * SUB, SUB)
        window = as_tiles(wide_ref[pl.ds(first, (STEP + taps - 1) * SUB), :])
        rows_ref[pl.ds(first, STEP * SUB), :] = as_rows(
            filtered(window, taps_ref, stream, taps, STEP, False)
        )
        return carry

    lax.fori_loop(0, tokens // STEP, body, 0)
    gather_tokens(lambda group: group_rows(rows_ref, group, tokens), out_ref)


def back_local_kernel(
    index_ref, signal_ref, decay_ref, scale_ref, taps_ref, query_ref, gated_ref, weight_ref,
    local_ref, gq_ref, own_ref,
    wide_ref, rows_ref, out_vmem, gated_vmem, held_ref, own_vmem, sem, sems, *, taps,
):
    gated = pltpu.make_async_copy(gated_ref, gated_vmem, sems.at[1])
    gated.start()
    weights = start_weights(index_ref, 0, weight_ref, held_ref, sems)
    inside = query_ref.shape[0]
    copy = pltpu.make_async_copy(query_ref, wide_ref.at[pl.ds(0, inside), :], sem)
    copy.start()
    local_conv(signal_ref, decay_ref, scale_ref, local_ref, True)
    copy.wait()
    rest = (taps - 1) * SUB
    wide_ref[pl.ds(inside, rest), :] = jnp.zeros((rest, LANES), F32)
    spread_back(wide_ref, taps_ref, 0, taps, rows_ref, out_vmem)
    out = pltpu.make_async_copy(out_vmem, gq_ref, sem)
    out.start()
    wait_all([gated, *weights])
    own_vmem[...] = jnp.dot(
        gated_vmem[...], held_ref[0], preferred_element_type=F32
    ).astype(own_vmem.dtype)
    own = pltpu.make_async_copy(own_vmem, own_ref, sems.at[0])
    own.start()
    wait_all([out, own])


def finish_kernel(
    message_ref, local_ref, decay_ref, scale_ref, taps_ref, ahead_ref, query_ref, kf_ref, vf_ref,
    *refs, taps,
):
    (
        *part_refs, _, gq_ref, gk_ref, gv_ref, projected_ref,
        total_ref, feat_ref, query_vmem, wide_ref, rows_ref, tail_ref, out_vmem, parts_vmem,
        sems, part_sems,
    ) = refs
    tokens = gk_ref.shape[0]
    tail = tail_ref.shape[0]
    rim = taps - 1
    inside = pl.ds(0, tokens * SUB)
    copies = start_all(
        [
            pltpu.make_async_copy(
                query_ref.at[pl.ds((tokens - tail) * SUB, tail * SUB), :],
                query_vmem.at[pl.ds(0, tail * SUB), :],
                sems.at[0],
            ),
            pltpu.make_async_copy(vf_ref, feat_ref.at[0], sems.at[1]),
            pltpu.make_async_copy(kf_ref, feat_ref.at[1], sems.at[2]),
        ]
    )
    parts = start_all(
        [
            pltpu.make_async_copy(ref, parts_vmem.at[number], part_sems.at[number])
            for number, ref in enumerate(part_refs)
        ]
    )
    states = read_messages(message_ref)
    carried(total_ref, states, decay_ref, scale_ref, True, local_ref)
    growth = fades(decay_ref, -1.0)
    scales = scales_of(scale_ref)
    for ahead in range(rim):
        rows = pl.ds((tokens + ahead) * SUB, SUB)
        theirs = pl.ds(ahead * SUB, SUB)
        grad_conv = tree_sum([scale * state for scale, state in zip(scales, states)])
        query_vmem[pl.ds((tail + ahead) * SUB, SUB), :] = ahead_ref[0, theirs, :]
        wide_ref[0, rows, :] = round16(grad_conv * ahead_ref[3, theirs, :])
        wide_ref[1, rows, :] = round16(grad_conv * ahead_ref[2, theirs, :])
        arrived = ahead_ref[1, theirs, :]
        states = [(state - arrived) * grow for state, grow in zip(states, growth)]
    copies[0].wait()
    spread_back(query_vmem, taps_ref, 0, taps, rows_ref, tail_ref)
    outs = [
        pltpu.make_async_copy(tail_ref, gq_ref.at[pl.ds(tokens - tail, tail), :], sems.at[0])
    ]
    wait_all(parts)
    out_vmem[2] = tree_sum(
        [parts_vmem[number].astype(F32) for number in range(len(part_refs))]
    ).astype(out_vmem.dtype)
    outs.append(pltpu.make_async_copy(out_vmem.at[2], projected_ref, sems.at[3]))
    start_all(outs)
    for stream, out_ref in enumerate((gk_ref, gv_ref)):
        copies[1 + stream].wait()
        wide_ref[stream, inside, :] = round16(total_ref[...] * feat_ref[stream])
        spread_back(
            wide_ref.at[stream], taps_ref, 1 + stream, taps, rows_ref, out_vmem.at[stream]
        )
        outs.append(pltpu.make_async_copy(out_vmem.at[stream], out_ref, sems.at[1 + stream]))
        outs[-1].start()
    wait_all(outs)


IN_VMEM = pl.BlockSpec(memory_space=pltpu.VMEM)
IN_SMEM = pl.BlockSpec(memory_space=pltpu.SMEM)
IN_HBM = pl.BlockSpec(memory_space=pltpu.HBM)
HBM_RATE = 3.5e6


def in_hbm(shape, kind):
    return pltpu.HBM(shape, kind)


def call(kernel, outs, args, specs, scratch, name, micros, mebibytes, aliases=None):
    args = [
        pltpu.with_memory_space_constraint(arg, pltpu.HBM) if spec is IN_HBM else arg
        for arg, spec in zip(args, specs)
    ]
    held = [isinstance(out, tuple) for out in outs]
    return pl.pallas_call(
        kernel,
        out_shape=[jax.ShapeDtypeStruct(*out) if own else out for own, out in zip(held, outs)],
        in_specs=specs,
        out_specs=[IN_VMEM if own else IN_HBM for own in held],
        scratch_shapes=scratch,
        compiler_params=pltpu.CompilerParams(vmem_limit_bytes=mebibytes * 1024 * 1024),
        cost_estimate=pl.CostEstimate(
            flops=0, bytes_accessed=int(micros * HBM_RATE), transcendentals=0
        ),
        name=name,
        input_output_aliases=aliases or {},
    )(*args)


def shift(value, axis, steps):
    count = lax.axis_size(axis)
    pairs = [(s, s + steps) for s in range(count) if 0 <= s + steps < count]
    return lax.ppermute(value, axis, pairs)


def exchange(value, axis, mask):
    count = lax.axis_size(axis)
    return lax.ppermute(value, axis, [(s, s ^ mask) for s in range(count)])


def shards(query_in, key_in, value_in, short_taps, residues, decays, out_weight, out_grad):
    tokens, channels = query_in.shape
    taps = short_taps.shape[0]
    rim = taps - 1
    modes = decays.shape[1]
    blocks = lax.axis_size("ctx")
    fans = lax.axis_size("ch")
    position = lax.axis_index("ctx")[None].astype(jnp.int32)
    tile_shape = (tokens * SUB, LANES)
    mode_shape = (modes * SUB, LANES)
    message_shape = (blocks,) + mode_shape
    streams = (query_in, key_in, value_in)
    rim_rows = 16

    tap_rows = jnp.transpose(short_taps, (1, 0, 2))
    halo, narrow, taps_vmem, residues_vmem, decays_vmem = call(
        rim_kernel,
        [
            ((3 * rim_rows, channels), BF16),
            ((3, tokens, channels), BF16),
            ((3, taps, channels), F32),
            ((modes, channels), F32),
            ((modes, channels), F32),
        ],
        streams + (tap_rows, residues.T, decays.T), [IN_HBM] * 6,
        [pltpu.SemaphoreType.DMA((9,))], "rim", 1.2, 2,
    )
    halo, out_grad = lax.optimization_barrier((halo, out_grad))
    halo = shift(halo, "ctx", 1)
    if fans == 4:
        order = lax.axis_index("ch") ^ jnp.arange(fans, dtype=jnp.int32)
        pieces = [out_grad] + [exchange(out_grad, "ch", mask) for mask in range(1, fans - 1)]
    else:
        order = jnp.arange(fans, dtype=jnp.int32)
        everyone = lax.all_gather(out_grad, "ch", axis=0, tiled=False)
        pieces = [everyone[number] for number in range(fans)]
    tile = pltpu.VMEM(tile_shape, F32)
    wide_rows = (tokens + rim) * SUB

    (
        query_feat, key_feat, value_feat, local, grad_copy, messages,
        tap_tiles, scale_tiles, decay_tiles,
    ) = call(
        featurize_kernel,
        [in_hbm(tile_shape, F32)] * 4
        + [in_hbm((tokens, channels), BF16), (message_shape, BF16)]
        + [((3 * taps * SUB, LANES), F32), (mode_shape, F32), (mode_shape, F32)],
        (position, narrow, taps_vmem, residues_vmem, decays_vmem, halo, out_grad),
        [IN_SMEM] + [IN_VMEM] * 5 + [IN_HBM],
        [
            pltpu.VMEM((3, wide_rows, LANES), F32),
            pltpu.VMEM((4,) + tile_shape, F32),
            pltpu.VMEM((tokens, channels), BF16),
            pltpu.SemaphoreType.DMA((5,)),
        ],
        "featurize", 6.0, 10,
    )
    if fans == 4:
        pieces.append(exchange(grad_copy, "ch", fans - 1))
    arrived = lax.all_to_all(messages, "ctx", split_axis=0, concat_axis=0, tiled=True)

    def weight_scratch(count):
        return [
            pltpu.VMEM((count, channels, channels), BF16),
            pltpu.SemaphoreType.DMA((count,)),
        ]

    early = fans - 1
    (base,) = call(
        middle_kernel,
        [((channels, tokens), F32)],
        (order, out_weight, *pieces[:early]),
        [IN_SMEM] + [IN_HBM] * (1 + early),
        [
            pltpu.VMEM((early, tokens, channels), BF16),
            pltpu.VMEM((early, channels, tokens), BF16),
        ]
        + weight_scratch(early)
        + [pltpu.SemaphoreType.DMA((early,))],
        "middle", 6.0, 11,
    )
    sent = fans - 1 if fans == 4 else fans
    conv_out, gated, *partial_sums = call(
        project_kernel,
        [in_hbm(tile_shape, F32)] + [in_hbm((tokens, channels), BF16)] * (1 + sent),
        (
            order, arrived, decay_tiles, scale_tiles, base, query_feat, local, out_weight,
            *pieces[1:early],
        ),
        [IN_SMEM] + [IN_VMEM] * 4 + [IN_HBM] * (2 + early),
        [
            tile,
            tile,
            tile,
            pltpu.VMEM((tokens, channels), BF16),
            pltpu.VMEM((sent, channels, channels), BF16),
            pltpu.VMEM((sent, tokens, channels), BF16),
            pltpu.SemaphoreType.DMA((sent + 2,)),
            pltpu.SemaphoreType.DMA((sent + 1,)),
        ],
        "project", 7.0, 16,
    )
    if fans == 4:
        parts = [exchange(part, "ch", 1 + number) for number, part in enumerate(partial_sums)]
    else:
        parts = lax.all_to_all(
            jnp.stack(partial_sums), "ch", split_axis=0, concat_axis=0, tiled=True
        )
        parts = [parts[number] for number in range(fans)]
    back_query, grad_mixed, back_messages, ahead = call(
        functools.partial(back_last_kernel, rim=rim),
        [in_hbm(tile_shape, F32), (tile_shape, F32), (message_shape, BF16)]
        + [((4, rim * SUB, LANES), F32)],
        (
            order, position, base, decay_tiles, out_weight, query_feat, key_feat,
            value_feat, conv_out, *pieces[early:],
        ),
        [IN_SMEM] * 2 + [IN_VMEM] * 2 + [IN_HBM] * 5 + [IN_VMEM] * (fans - early),
        [
            pltpu.VMEM((fans - early, channels, tokens), BF16),
            pltpu.VMEM((channels, tokens), F32),
            tile,
            tile,
            tile,
        ]
        + weight_scratch(fans - early)
        + [pltpu.SemaphoreType.DMA((5,))],
        "back_last", 6.0, 9,
    )
    back_arrived = lax.all_to_all(back_messages, "ctx", split_axis=0, concat_axis=0, tiled=True)
    ahead = shift(ahead, "ctx", -1)
    back_local, grad_query, own_part = call(
        functools.partial(back_local_kernel, taps=taps),
        [(tile_shape, F32)] + [in_hbm((tokens, channels), BF16)] * 2,
        (order, grad_mixed, decay_tiles, scale_tiles, tap_tiles, back_query, gated, out_weight),
        [IN_SMEM] + [IN_VMEM] * 4 + [IN_HBM] * 3,
        [
            pltpu.VMEM((wide_rows, LANES), F32),
            tile,
            pltpu.VMEM((tokens, channels), BF16),
            pltpu.VMEM((tokens, channels), BF16),
            pltpu.VMEM((1, channels, channels), BF16),
            pltpu.VMEM((tokens, channels), BF16),
            pltpu.SemaphoreType.DMA,
            pltpu.SemaphoreType.DMA((2,)),
        ],
        "back_local", 5.0, 9,
    )
    if fans == 4:
        parts = [own_part] + parts
    tail = 16
    grad_query, grad_key, grad_value, projected = call(
        functools.partial(finish_kernel, taps=taps),
        [in_hbm((tokens, channels), BF16)] * 4,
        (
            back_arrived, back_local, decay_tiles, scale_tiles, tap_tiles, ahead, back_query,
            key_feat, value_feat, *parts, grad_query,
        ),
        [IN_VMEM] * 6 + [IN_HBM] * (4 + fans),
        [
            tile,
            pltpu.VMEM((2,) + tile_shape, F32),
            pltpu.VMEM(((tail + rim) * SUB, LANES), F32),
            pltpu.VMEM((2, wide_rows, LANES), F32),
            tile,
            pltpu.VMEM((tail, channels), BF16),
            pltpu.VMEM((3, tokens, channels), BF16),
            pltpu.VMEM((fans, tokens, channels), BF16),
            pltpu.SemaphoreType.DMA((4,)),
            pltpu.SemaphoreType.DMA((fans,)),
        ],
        "finish", 5.0, 12,
        {9 + fans: 0},
    )
    return (projected, grad_query, grad_key, grad_value)


def solution(mesh):
    in_specs = (
        P("ctx", "ch"),
        P("ctx", "ch"),
        P("ctx", "ch"),
        P(None, None, "ch"),
        P("ch", None),
        P("ch", None),
        P("ch", None),
        P("ctx", "ch"),
    )
    out_specs = (P("ctx", "ch"), P("ctx", "ch"), P("ctx", "ch"), P("ctx", "ch"))
    return jax.shard_map(shards, mesh=mesh, in_specs=in_specs, out_specs=out_specs, check_vma=False)
```

```python
import functools

import jax
import jax.numpy as jnp
from jax import lax
from jax.experimental import pallas as pl
from jax.experimental.pallas import tpu as pltpu
from jax.sharding import PartitionSpec as P

SUB = 8
LANES = 128
STEP = 8
F32 = jnp.float32
BF16 = jnp.bfloat16


def as_tiles(rows):
    return rows.reshape(rows.shape[0] // SUB, SUB, LANES)


def as_rows(tiles):
    return tiles.reshape(tiles.shape[0] * SUB, LANES)


def tile(ref, token):
    return ref[pl.ds(pl.multiple_of(token * SUB, SUB), SUB), :]


def tree_sum(terms):
    while len(terms) > 1:
        terms = [
            terms[i] + terms[i + 1] if i + 1 < len(terms) else terms[i]
            for i in range(0, len(terms), 2)
        ]
    return terms[0]


def round16(value):
    return value.astype(BF16).astype(F32)


def scatter_tokens(ref, value, first_token):
    tokens, channels = value.shape
    for group in range(channels // LANES):
        ref[pl.ds(first_token * SUB + group, tokens, stride=SUB), :] = value[
            :, group * LANES : (group + 1) * LANES
        ]


def gather_tokens(rows, out_ref):
    for group in range(out_ref.shape[1] // LANES):
        out_ref[:, group * LANES : (group + 1) * LANES] = rows(group).astype(out_ref.dtype)


def group_rows(ref, group, tokens):
    return ref[pl.ds(group, tokens, stride=SUB), :]


def start_all(copies):
    for copy in copies:
        copy.start()
    return copies


def wait_all(copies):
    for copy in copies:
        copy.wait()


def advance_states(signal_ref, factors, states, first, count, reverse):
    last = signal_ref.shape[0] // SUB - 1

    def body(step, states):
        for inner in range(STEP):
            token = first + step * STEP + inner
            u = tile(signal_ref, last - token if reverse else token)
            states = [factor * state + u for factor, state in zip(factors, states)]
        return states

    return lax.fori_loop(0, count // STEP, body, states)


def zero_states(modes):
    return [jnp.zeros((SUB, LANES), F32) for _ in range(modes)]


def mode_rows(n):
    return slice(n * SUB, (n + 1) * SUB)


def fades(decay_ref, tokens):
    return [
        jnp.exp(-decay_ref[mode_rows(n), :] * tokens) for n in range(decay_ref.shape[0] // SUB)
    ]


def write_messages(out_ref, states, decay_ref, position_ref, tokens, direction):
    count = out_ref.shape[0]
    out_ref[...] = jnp.zeros_like(out_ref)
    fade = fades(decay_ref, float(tokens))
    for gap in range(count - 1):
        other = position_ref[0] + direction * (gap + 1)
        value = jnp.concatenate(states, axis=0).astype(out_ref.dtype)

        @pl.when((other >= 0) & (other < count))
        def _():
            out_ref[jnp.clip(other, 0, count - 1)] = value

        states = [state * factor for state, factor in zip(states, fade)]


def read_messages(in_ref):
    total = in_ref[0].astype(F32)
    for other in range(1, in_ref.shape[0]):
        total = total + in_ref[other].astype(F32)
    return [total[mode_rows(n)] for n in range(total.shape[0] // SUB)]


def rim_kernel(
    q_ref, k_ref, v_ref, taps_ref, residue_ref, decay_ref,
    rim_ref, streams_ref, taps_vmem, residue_vmem, decay_vmem, sems,
):
    rows = rim_ref.shape[0] // 3
    streams = (q_ref, k_ref, v_ref)
    rims = [
        pltpu.make_async_copy(
            source.at[pl.ds(source.shape[0] - rows, rows), :],
            rim_ref.at[pl.ds(stream * rows, rows), :],
            sems.at[stream],
        )
        for stream, source in enumerate(streams)
    ]
    pairs = [(source, streams_ref.at[stream]) for stream, source in enumerate(streams)]
    pairs += [(taps_ref, taps_vmem), (residue_ref, residue_vmem), (decay_ref, decay_vmem)]
    others = [
        pltpu.make_async_copy(source, target, sems.at[3 + number])
        for number, (source, target) in enumerate(pairs)
    ]
    wait_all(start_all(rims + others))


def filtered(window, taps_ref, stream, taps, steps, forward):
    total = None
    for tap in range(taps):
        first = taps - 1 - tap if forward else tap
        term = taps_ref[pl.ds((stream * taps + tap) * SUB, SUB), :] * window[first : first + steps]
        total = term if total is None else total + term
    return total


def featurize_kernel(
    position_ref, streams_ref, taps_in_ref, residue_ref, decay_in_ref, halo_ref, grad_in_ref,
    qf_ref, kf_ref, vf_ref, local_ref, grad_copy_ref, message_ref, taps_ref, scale_ref, decay_ref,
    wide_ref, feat_ref, grad_vmem, sems,
):
    grad_in = pltpu.make_async_copy(grad_in_ref, grad_vmem, sems.at[4])
    grad_in.start()
    tokens = streams_ref.shape[1]
    _, taps, _ = taps_in_ref.shape
    rim = taps - 1
    modes = decay_in_ref.shape[0]
    held = halo_ref.shape[0] // 3
    decays = decay_in_ref[...]
    scatter_tokens(decay_ref, decays, 0)
    scatter_tokens(scale_ref, residue_ref[...] * jnp.sqrt(decays), 0)
    for stream in range(3):
        scatter_tokens(taps_ref, taps_in_ref[stream], stream * taps)
        behind = halo_ref[stream * held : (stream + 1) * held, :].astype(F32)
        scatter_tokens(wide_ref.at[stream], behind[held - rim :], 0)
    batch = 2 * STEP

    def place(number):
        first = pl.multiple_of(number * batch, batch)
        for stream in range(3):
            value = streams_ref[stream, pl.ds(first, batch), :].astype(F32)
            scatter_tokens(wide_ref.at[stream], value, rim + first)

    place(0)

    def body(number, carry):
        windows = [
            as_tiles(
                wide_ref[
                    stream,
                    pl.ds(pl.multiple_of(number * batch * SUB, SUB), (batch + rim) * SUB),
                    :,
                ]
            )
            for stream in range(3)
        ]
        place(jnp.minimum(number + 1, tokens // batch - 1))
        for half in range(2):
            rows = pl.ds(pl.multiple_of((number * 2 + half) * STEP * SUB, SUB), STEP * SUB)
            feats = []
            for stream in range(3):
                window = windows[stream][half * STEP : half * STEP + STEP + rim]
                feats.append(filtered(window, taps_ref, stream, taps, STEP, True))
                feat_ref[stream, rows, :] = as_rows(feats[-1])
            feat_ref[3, rows, :] = as_rows(round16(feats[1] * feats[2]))
        return carry

    lax.fori_loop(0, tokens // batch, body, 0)
    grad_in.wait()
    copies = start_all(
        [
            pltpu.make_async_copy(source, target, sems.at[number])
            for number, (source, target) in enumerate(
                (
                    (feat_ref.at[0], qf_ref),
                    (feat_ref.at[1], kf_ref),
                    (feat_ref.at[2], vf_ref),
                    (grad_vmem, grad_copy_ref),
                )
            )
        ]
    )
    local_vmem = wide_ref.at[0, pl.ds(0, tokens * SUB), :]
    states = local_conv(feat_ref.at[3], decay_ref, scale_ref, local_vmem, False)
    copies += start_all([pltpu.make_async_copy(local_vmem, local_ref, sems.at[4])])
    write_messages(message_ref, states, decay_ref, position_ref, tokens, 1)
    wait_all(copies)


def scales_of(scale_ref):
    return [scale_ref[mode_rows(n), :] for n in range(scale_ref.shape[0] // SUB)]


def local_conv(signal_ref, decay_ref, scale_ref, out_ref, reverse):
    tokens = signal_ref.shape[0] // SUB
    factors = fades(decay_ref, 1.0)
    scales = scales_of(scale_ref)

    def body(step, states):
        for inner in range(STEP):
            token = step * STEP + inner
            token = tokens - 1 - token if reverse else token
            u = tile(signal_ref, token)
            states = [factor * state + u for factor, state in zip(factors, states)]
            out_ref[pl.ds(pl.multiple_of(token * SUB, SUB), SUB), :] = tree_sum(
                [scale * state for scale, state in zip(scales, states)]
            )
        return states

    return lax.fori_loop(0, tokens // STEP, body, zero_states(len(factors)))


def carried(out_ref, states, decay_ref, scale_ref, reverse, local_ref=None):
    tokens = out_ref.shape[0] // SUB
    factors = fades(decay_ref, 1.0)
    scaled = [scale * state for scale, state in zip(scales_of(scale_ref), states)]

    def body(step, scaled):
        for inner in range(STEP):
            token = step * STEP + inner
            token = tokens - 1 - token if reverse else token
            scaled = [factor * state for factor, state in zip(factors, scaled)]
            rows = pl.ds(pl.multiple_of(token * SUB, SUB), SUB)
            total = tree_sum(list(scaled))
            out_ref[rows, :] = total if local_ref is None else local_ref[rows, :] + total
        return scaled

    lax.fori_loop(0, tokens // STEP, body, scaled)


def project_kernel(
    index_ref, message_ref, decay_ref, scale_ref, _, qf_ref, local_ref, weight_ref, *refs
):
    rows_ref, feat_ref, local_vmem, gated_ref, held_ref, sent_ref, sems, out_sems = refs[-8:]
    conv_ref, gated_out_ref, *out_refs = refs[-10 - sent_ref.shape[0] : -8]
    parts, tokens, width = sent_ref.shape
    offset = index_ref.shape[0] - parts
    order = list(reversed(range(parts)))
    copies = [
        pltpu.make_async_copy(
            weight_ref.at[
                :, pl.ds(pl.multiple_of(index_ref[offset + part] * width, width), width)
            ],
            held_ref.at[part],
            sems.at[part],
        )
        for part in range(parts)
    ]
    outs = [
        pltpu.make_async_copy(sent_ref.at[part], out_refs[part], out_sems.at[part])
        for part in range(parts)
    ]
    local_copy = pltpu.make_async_copy(local_ref, local_vmem, sems.at[parts + 1])
    feat_copy = pltpu.make_async_copy(qf_ref, feat_ref, sems.at[parts])
    start_all([local_copy, feat_copy])
    start_all([copies[part] for part in order])
    carried(rows_ref, read_messages(message_ref), decay_ref, scale_ref, False)
    local_copy.wait()
    rows_ref[...] += local_vmem[...]
    conv_copy = pltpu.make_async_copy(rows_ref, conv_ref, sems.at[parts + 1])
    conv_copy.start()
    feat_copy.wait()
    gather_tokens(
        lambda group: group_rows(rows_ref, group, tokens) * group_rows(feat_ref, group, tokens),
        gated_ref,
    )
    gated_copy = pltpu.make_async_copy(gated_ref, gated_out_ref, out_sems.at[parts])
    gated_copy.start()
    for part in order:
        copies[part].wait()
        sent_ref[part] = jnp.dot(
            gated_ref[...], held_ref[part], preferred_element_type=F32
        ).astype(sent_ref.dtype)
        outs[part].start()
    wait_all([conv_copy, gated_copy] + outs)


def start_weights(index_ref, first, weight_ref, held_ref, sems):
    count, _, width = held_ref.shape
    return start_all(
        [
            pltpu.make_async_copy(
                weight_ref.at[
                    :, pl.ds(pl.multiple_of(index_ref[first + number] * width, width), width)
                ],
                held_ref.at[number],
                sems.at[number],
            )
            for number in range(count)
        ]
    )


def back_products(weights, piece_refs, turned_ref, held_ref, total_ref, before_ref):
    for number, ref in enumerate(piece_refs):
        turned_ref[number] = ref[...].T
    for number in range(len(piece_refs)):
        weights[number].wait()
        product = jnp.dot(held_ref[number], turned_ref[number], preferred_element_type=F32)
        earlier = before_ref if number == 0 else total_ref
        total_ref[...] = product if earlier is None else earlier[...] + product


def middle_kernel(index_ref, weight_ref, *refs):
    *piece_refs, total_ref, piece_vmem, turned_ref, held_ref, sems, piece_sems = refs
    pieces = start_all(
        [
            pltpu.make_async_copy(ref, piece_vmem.at[number], piece_sems.at[number])
            for number, ref in enumerate(piece_refs)
        ]
    )
    weights = start_weights(index_ref, 0, weight_ref, held_ref, sems)
    wait_all(pieces)
    held = [piece_vmem.at[number] for number in range(len(piece_refs))]
    back_products(weights, held, turned_ref, held_ref, total_ref, None)


def back_last_kernel(
    index_ref, position_ref, base_ref, decay_ref, weight_ref, qf_ref, kf_ref, vf_ref, conv_ref,
    *refs, rim,
):
    (
        *piece_refs, back_query_ref, mixed_ref, message_ref, ahead_ref,
        turned_ref, total_ref, rows_ref, feat_ref, conv_vmem, held_ref, sems, own_sems,
    ) = refs
    tokens = total_ref.shape[1]
    heads = pl.ds(0, rim * SUB)
    weights = start_weights(
        index_ref, index_ref.shape[0] - len(piece_refs), weight_ref, held_ref, sems
    )
    copies = start_all(
        [
            pltpu.make_async_copy(qf_ref, feat_ref, own_sems.at[0]),
            pltpu.make_async_copy(conv_ref, conv_vmem, own_sems.at[1]),
            pltpu.make_async_copy(kf_ref.at[heads, :], ahead_ref.at[2], own_sems.at[2]),
            pltpu.make_async_copy(vf_ref.at[heads, :], ahead_ref.at[3], own_sems.at[3]),
        ]
    )
    back_products(weights, piece_refs, turned_ref, held_ref, total_ref, base_ref)
    scatter_tokens(rows_ref, total_ref[...].T, 0)
    wait_all(copies)
    mixed_ref[...] = round16(rows_ref[...] * feat_ref[...])
    rows_ref[...] = round16(rows_ref[...] * conv_vmem[...])
    out = pltpu.make_async_copy(rows_ref, back_query_ref, own_sems.at[4])
    out.start()
    ahead_ref[0] = rows_ref[: rim * SUB, :]
    ahead_ref[1] = mixed_ref[: rim * SUB, :]
    modes = decay_ref.shape[0] // SUB
    states = advance_states(
        mixed_ref, fades(decay_ref, 1.0), zero_states(modes), 0, tokens, True
    )
    write_messages(message_ref, states, decay_ref, position_ref, tokens, -1)
    out.wait()


def spread_back(wide_ref, taps_ref, stream, taps, rows_ref, out_ref):
    tokens = out_ref.shape[0]

    def body(step, carry):
        first = pl.multiple_of(step * STEP * SUB, SUB)
        window = as_tiles(wide_ref[pl.ds(first, (STEP + taps - 1) * SUB), :])
        rows_ref[pl.ds(first, STEP * SUB), :] = as_rows(
            filtered(window, taps_ref, stream, taps, STEP, False)
        )
        return carry

    lax.fori_loop(0, tokens // STEP, body, 0)
    gather_tokens(lambda group: group_rows(rows_ref, group, tokens), out_ref)


def back_local_kernel(
    index_ref, signal_ref, decay_ref, scale_ref, taps_ref, query_ref, gated_ref, weight_ref,
    local_ref, gq_ref, own_ref,
    wide_ref, rows_ref, out_vmem, gated_vmem, held_ref, own_vmem, sem, sems, *, taps,
):
    gated = pltpu.make_async_copy(gated_ref, gated_vmem, sems.at[1])
    gated.start()
    weights = start_weights(index_ref, 0, weight_ref, held_ref, sems)
    inside = query_ref.shape[0]
    copy = pltpu.make_async_copy(query_ref, wide_ref.at[pl.ds(0, inside), :], sem)
    copy.start()
    local_conv(signal_ref, decay_ref, scale_ref, local_ref, True)
    copy.wait()
    rest = (taps - 1) * SUB
    wide_ref[pl.ds(inside, rest), :] = jnp.zeros((rest, LANES), F32)
    spread_back(wide_ref, taps_ref, 0, taps, rows_ref, out_vmem)
    out = pltpu.make_async_copy(out_vmem, gq_ref, sem)
    out.start()
    wait_all([gated, *weights])
    own_vmem[...] = jnp.dot(
        gated_vmem[...], held_ref[0], preferred_element_type=F32
    ).astype(own_vmem.dtype)
    own = pltpu.make_async_copy(own_vmem, own_ref, sems.at[0])
    own.start()
    wait_all([out, own])


def finish_kernel(
    message_ref, local_ref, decay_ref, scale_ref, taps_ref, ahead_ref, query_ref, kf_ref, vf_ref,
    *refs, taps,
):
    (
        *part_refs, _, gq_ref, gk_ref, gv_ref, projected_ref,
        total_ref, feat_ref, query_vmem, wide_ref, rows_ref, tail_ref, out_vmem, parts_vmem,
        sems, part_sems,
    ) = refs
    tokens = gk_ref.shape[0]
    tail = tail_ref.shape[0]
    rim = taps - 1
    inside = pl.ds(0, tokens * SUB)
    copies = start_all(
        [
            pltpu.make_async_copy(
                query_ref.at[pl.ds((tokens - tail) * SUB, tail * SUB), :],
                query_vmem.at[pl.ds(0, tail * SUB), :],
                sems.at[0],
            ),
            pltpu.make_async_copy(vf_ref, feat_ref.at[0], sems.at[1]),
            pltpu.make_async_copy(kf_ref, feat_ref.at[1], sems.at[2]),
        ]
    )
    parts = start_all(
        [
            pltpu.make_async_copy(ref, parts_vmem.at[number], part_sems.at[number])
            for number, ref in enumerate(part_refs)
        ]
    )
    states = read_messages(message_ref)
    carried(total_ref, states, decay_ref, scale_ref, True, local_ref)
    growth = fades(decay_ref, -1.0)
    scales = scales_of(scale_ref)
    for ahead in range(rim):
        rows = pl.ds((tokens + ahead) * SUB, SUB)
        theirs = pl.ds(ahead * SUB, SUB)
        grad_conv = tree_sum([scale * state for scale, state in zip(scales, states)])
        query_vmem[pl.ds((tail + ahead) * SUB, SUB), :] = ahead_ref[0, theirs, :]
        wide_ref[0, rows, :] = round16(grad_conv * ahead_ref[3, theirs, :])
        wide_ref[1, rows, :] = round16(grad_conv * ahead_ref[2, theirs, :])
        arrived = ahead_ref[1, theirs, :]
        states = [(state - arrived) * grow for state, grow in zip(states, growth)]
    copies[0].wait()
    spread_back(query_vmem, taps_ref, 0, taps, rows_ref, tail_ref)
    outs = [
        pltpu.make_async_copy(tail_ref, gq_ref.at[pl.ds(tokens - tail, tail), :], sems.at[0])
    ]
    wait_all(parts)
    out_vmem[2] = tree_sum(
        [parts_vmem[number].astype(F32) for number in range(len(part_refs))]
    ).astype(out_vmem.dtype)
    outs.append(pltpu.make_async_copy(out_vmem.at[2], projected_ref, sems.at[3]))
    start_all(outs)
    for stream, out_ref in enumerate((gk_ref, gv_ref)):
        copies[1 + stream].wait()
        wide_ref[stream, inside, :] = round16(total_ref[...] * feat_ref[stream])
        spread_back(
            wide_ref.at[stream], taps_ref, 1 + stream, taps, rows_ref, out_vmem.at[stream]
        )
        outs.append(pltpu.make_async_copy(out_vmem.at[stream], out_ref, sems.at[1 + stream]))
        outs[-1].start()
    wait_all(outs)


IN_VMEM = pl.BlockSpec(memory_space=pltpu.VMEM)
IN_SMEM = pl.BlockSpec(memory_space=pltpu.SMEM)
IN_HBM = pl.BlockSpec(memory_space=pltpu.HBM)
HBM_RATE = 3.5e6


def in_hbm(shape, kind):
    return pltpu.HBM(shape, kind)


def call(kernel, outs, args, specs, scratch, name, micros, mebibytes, aliases=None):
    args = [
        pltpu.with_memory_space_constraint(arg, pltpu.HBM) if spec is IN_HBM else arg
        for arg, spec in zip(args, specs)
    ]
    held = [isinstance(out, tuple) for out in outs]
    return pl.pallas_call(
        kernel,
        out_shape=[jax.ShapeDtypeStruct(*out) if own else out for own, out in zip(held, outs)],
        in_specs=specs,
        out_specs=[IN_VMEM if own else IN_HBM for own in held],
        scratch_shapes=scratch,
        compiler_params=pltpu.CompilerParams(vmem_limit_bytes=mebibytes * 1024 * 1024),
        cost_estimate=pl.CostEstimate(
            flops=0, bytes_accessed=int(micros * HBM_RATE), transcendentals=0
        ),
        name=name,
        input_output_aliases=aliases or {},
    )(*args)


def shift(value, axis, steps):
    count = lax.axis_size(axis)
    pairs = [(s, s + steps) for s in range(count) if 0 <= s + steps < count]
    return lax.ppermute(value, axis, pairs)


def exchange(value, axis, mask):
    count = lax.axis_size(axis)
    return lax.ppermute(value, axis, [(s, s ^ mask) for s in range(count)])


def shards(query_in, key_in, value_in, short_taps, residues, decays, out_weight, out_grad):
    tokens, channels = query_in.shape
    taps = short_taps.shape[0]
    rim = taps - 1
    modes = decays.shape[1]
    blocks = lax.axis_size("ctx")
    fans = lax.axis_size("ch")
    position = lax.axis_index("ctx")[None].astype(jnp.int32)
    tile_shape = (tokens * SUB, LANES)
    mode_shape = (modes * SUB, LANES)
    message_shape = (blocks,) + mode_shape
    streams = (query_in, key_in, value_in)
    rim_rows = 16

    tap_rows = jnp.transpose(short_taps, (1, 0, 2))
    halo, narrow, taps_vmem, residues_vmem, decays_vmem = call(
        rim_kernel,
        [
            ((3 * rim_rows, channels), BF16),
            ((3, tokens, channels), BF16),
            ((3, taps, channels), F32),
            ((modes, channels), F32),
            ((modes, channels), F32),
        ],
        streams + (tap_rows, residues.T, decays.T), [IN_HBM] * 6,
        [pltpu.SemaphoreType.DMA((9,))], "rim", 1.2, 2,
    )
    halo, out_grad = lax.optimization_barrier((halo, out_grad))
    halo = shift(halo, "ctx", 1)
    if fans == 4:
        order = lax.axis_index("ch") ^ jnp.arange(fans, dtype=jnp.int32)
        pieces = [out_grad] + [exchange(out_grad, "ch", mask) for mask in range(1, fans - 1)]
    else:
        order = jnp.arange(fans, dtype=jnp.int32)
        everyone = lax.all_gather(out_grad, "ch", axis=0, tiled=False)
        pieces = [everyone[number] for number in range(fans)]
    tile = pltpu.VMEM(tile_shape, F32)
    wide_rows = (tokens + rim) * SUB

    (
        query_feat, key_feat, value_feat, local, grad_copy, messages,
        tap_tiles, scale_tiles, decay_tiles,
    ) = call(
        featurize_kernel,
        [in_hbm(tile_shape, F32)] * 4
        + [in_hbm((tokens, channels), BF16), (message_shape, BF16)]
        + [((3 * taps * SUB, LANES), F32), (mode_shape, F32), (mode_shape, F32)],
        (position, narrow, taps_vmem, residues_vmem, decays_vmem, halo, out_grad),
        [IN_SMEM] + [IN_VMEM] * 5 + [IN_HBM],
        [
            pltpu.VMEM((3, wide_rows, LANES), F32),
            pltpu.VMEM((4,) + tile_shape, F32),
            pltpu.VMEM((tokens, channels), BF16),
            pltpu.SemaphoreType.DMA((5,)),
        ],
        "featurize", 6.0, 10,
    )
    if fans == 4:
        pieces.append(exchange(grad_copy, "ch", fans - 1))
    arrived = lax.all_to_all(messages, "ctx", split_axis=0, concat_axis=0, tiled=True)

    def weight_scratch(count):
        return [
            pltpu.VMEM((count, channels, channels), BF16),
            pltpu.SemaphoreType.DMA((count,)),
        ]

    early = fans - 1
    (base,) = call(
        middle_kernel,
        [((channels, tokens), F32)],
        (order, out_weight, *pieces[:early]),
        [IN_SMEM] + [IN_HBM] * (1 + early),
        [
            pltpu.VMEM((early, tokens, channels), BF16),
            pltpu.VMEM((early, channels, tokens), BF16),
        ]
        + weight_scratch(early)
        + [pltpu.SemaphoreType.DMA((early,))],
        "middle", 6.0, 11,
    )
    sent = fans - 1 if fans == 4 else fans
    conv_out, gated, *partial_sums = call(
        project_kernel,
        [in_hbm(tile_shape, F32)] + [in_hbm((tokens, channels), BF16)] * (1 + sent),
        (
            order, arrived, decay_tiles, scale_tiles, base, query_feat, local, out_weight,
            *pieces[1:early],
        ),
        [IN_SMEM] + [IN_VMEM] * 4 + [IN_HBM] * (2 + early),
        [
            tile,
            tile,
            tile,
            pltpu.VMEM((tokens, channels), BF16),
            pltpu.VMEM((sent, channels, channels), BF16),
            pltpu.VMEM((sent, tokens, channels), BF16),
            pltpu.SemaphoreType.DMA((sent + 2,)),
            pltpu.SemaphoreType.DMA((sent + 1,)),
        ],
        "project", 7.0, 16,
    )
    if fans == 4:
        parts = [exchange(part, "ch", 1 + number) for number, part in enumerate(partial_sums)]
    else:
        parts = lax.all_to_all(
            jnp.stack(partial_sums), "ch", split_axis=0, concat_axis=0, tiled=True
        )
        parts = [parts[number] for number in range(fans)]
    back_query, grad_mixed, back_messages, ahead = call(
        functools.partial(back_last_kernel, rim=rim),
        [in_hbm(tile_shape, F32), (tile_shape, F32), (message_shape, BF16)]
        + [((4, rim * SUB, LANES), F32)],
        (
            order, position, base, decay_tiles, out_weight, query_feat, key_feat,
            value_feat, conv_out, *pieces[early:],
        ),
        [IN_SMEM] * 2 + [IN_VMEM] * 2 + [IN_HBM] * 5 + [IN_VMEM] * (fans - early),
        [
            pltpu.VMEM((fans - early, channels, tokens), BF16),
            pltpu.VMEM((channels, tokens), F32),
            tile,
            tile,
            tile,
        ]
        + weight_scratch(fans - early)
        + [pltpu.SemaphoreType.DMA((5,))],
        "back_last", 6.0, 9,
    )
    back_arrived = lax.all_to_all(back_messages, "ctx", split_axis=0, concat_axis=0, tiled=True)
    ahead = shift(ahead, "ctx", -1)
    back_local, grad_query, own_part = call(
        functools.partial(back_local_kernel, taps=taps),
        [(tile_shape, F32)] + [in_hbm((tokens, channels), BF16)] * 2,
        (order, grad_mixed, decay_tiles, scale_tiles, tap_tiles, back_query, gated, out_weight),
        [IN_SMEM] + [IN_VMEM] * 4 + [IN_HBM] * 3,
        [
            pltpu.VMEM((wide_rows, LANES), F32),
            tile,
            pltpu.VMEM((tokens, channels), BF16),
            pltpu.VMEM((tokens, channels), BF16),
            pltpu.VMEM((1, channels, channels), BF16),
            pltpu.VMEM((tokens, channels), BF16),
            pltpu.SemaphoreType.DMA,
            pltpu.SemaphoreType.DMA((2,)),
        ],
        "back_local", 5.0, 9,
    )
    if fans == 4:
        parts = [own_part] + parts
    tail = 16
    grad_query, grad_key, grad_value, projected = call(
        functools.partial(finish_kernel, taps=taps),
        [in_hbm((tokens, channels), BF16)] * 4,
        (
            back_arrived, back_local, decay_tiles, scale_tiles, tap_tiles, ahead, back_query,
            key_feat, value_feat, *parts, grad_query,
        ),
        [IN_VMEM] * 6 + [IN_HBM] * (4 + fans),
        [
            tile,
            pltpu.VMEM((2,) + tile_shape, F32),
            pltpu.VMEM(((tail + rim) * SUB, LANES), F32),
            pltpu.VMEM((2, wide_rows, LANES), F32),
            tile,
            pltpu.VMEM((tail, channels), BF16),
            pltpu.VMEM((3, tokens, channels), BF16),
            pltpu.VMEM((fans, tokens, channels), BF16),
            pltpu.SemaphoreType.DMA((4,)),
            pltpu.SemaphoreType.DMA((fans,)),
        ],
        "finish", 5.0, 12,
        {9 + fans: 0},
    )
    return (projected, grad_query, grad_key, grad_value)


def solution(mesh):
    in_specs = (
        P("ctx", "ch"),
        P("ctx", "ch"),
        P("ctx", "ch"),
        P(None, None, "ch"),
        P("ch", None),
        P("ch", None),
        P("ch", None),
        P("ctx", "ch"),
    )
    out_specs = (P("ctx", "ch"), P("ctx", "ch"), P("ctx", "ch"), P("ctx", "ch"))
    return jax.shard_map(shards, mesh=mesh, in_specs=in_specs, out_specs=out_specs, check_vma=False)
```

```python
import functools

import jax
import jax.numpy as jnp
from jax import lax
from jax.experimental import pallas as pl
from jax.experimental.pallas import tpu as pltpu
from jax.sharding import PartitionSpec as P

SUB = 8
LANES = 128
STEP = 8
F32 = jnp.float32
BF16 = jnp.bfloat16


def as_tiles(rows):
    return rows.reshape(rows.shape[0] // SUB, SUB, LANES)


def as_rows(tiles):
    return tiles.reshape(tiles.shape[0] * SUB, LANES)


def tile(ref, token):
    return ref[pl.ds(pl.multiple_of(token * SUB, SUB), SUB), :]


def tree_sum(terms):
    while len(terms) > 1:
        terms = [
            terms[i] + terms[i + 1] if i + 1 < len(terms) else terms[i]
            for i in range(0, len(terms), 2)
        ]
    return terms[0]


def round16(value):
    return value.astype(BF16).astype(F32)


def scatter_tokens(ref, value, first_token):
    tokens, channels = value.shape
    for group in range(channels // LANES):
        ref[pl.ds(first_token * SUB + group, tokens, stride=SUB), :] = value[
            :, group * LANES : (group + 1) * LANES
        ]


def gather_tokens(rows, out_ref):
    for group in range(out_ref.shape[1] // LANES):
        out_ref[:, group * LANES : (group + 1) * LANES] = rows(group).astype(out_ref.dtype)


def group_rows(ref, group, tokens):
    return ref[pl.ds(group, tokens, stride=SUB), :]


def start_all(copies):
    for copy in copies:
        copy.start()
    return copies


def wait_all(copies):
    for copy in copies:
        copy.wait()


def advance_states(signal_ref, factors, states, first, count, reverse):
    last = signal_ref.shape[0] // SUB - 1

    def body(step, states):
        for inner in range(STEP):
            token = first + step * STEP + inner
            u = tile(signal_ref, last - token if reverse else token)
            states = [factor * state + u for factor, state in zip(factors, states)]
        return states

    return lax.fori_loop(0, count // STEP, body, states)


def zero_states(modes):
    return [jnp.zeros((SUB, LANES), F32) for _ in range(modes)]


def mode_rows(n):
    return slice(n * SUB, (n + 1) * SUB)


def fades(decay_ref, tokens):
    return [
        jnp.exp(-decay_ref[mode_rows(n), :] * tokens) for n in range(decay_ref.shape[0] // SUB)
    ]


def write_messages(out_ref, states, decay_ref, position_ref, tokens, direction):
    count = out_ref.shape[0]
    out_ref[...] = jnp.zeros_like(out_ref)
    fade = fades(decay_ref, float(tokens))
    for gap in range(count - 1):
        other = position_ref[0] + direction * (gap + 1)
        value = jnp.concatenate(states, axis=0).astype(out_ref.dtype)

        @pl.when((other >= 0) & (other < count))
        def _():
            out_ref[jnp.clip(other, 0, count - 1)] = value

        states = [state * factor for state, factor in zip(states, fade)]


def read_messages(in_ref):
    total = in_ref[0].astype(F32)
    for other in range(1, in_ref.shape[0]):
        total = total + in_ref[other].astype(F32)
    return [total[mode_rows(n)] for n in range(total.shape[0] // SUB)]


def rim_kernel(
    q_ref, k_ref, v_ref, taps_ref, residue_ref, decay_ref,
    rim_ref, streams_ref, taps_vmem, residue_vmem, decay_vmem, sems,
):
    rows = rim_ref.shape[0] // 3
    streams = (q_ref, k_ref, v_ref)
    rims = [
        pltpu.make_async_copy(
            source.at[pl.ds(source.shape[0] - rows, rows), :],
            rim_ref.at[pl.ds(stream * rows, rows), :],
            sems.at[stream],
        )
        for stream, source in enumerate(streams)
    ]
    pairs = [(source, streams_ref.at[stream]) for stream, source in enumerate(streams)]
    pairs += [(taps_ref, taps_vmem), (residue_ref, residue_vmem), (decay_ref, decay_vmem)]
    others = [
        pltpu.make_async_copy(source, target, sems.at[3 + number])
        for number, (source, target) in enumerate(pairs)
    ]
    wait_all(start_all(rims + others))


def filtered(window, taps_ref, stream, taps, steps, forward):
    total = None
    for tap in range(taps):
        first = taps - 1 - tap if forward else tap
        term = taps_ref[pl.ds((stream * taps + tap) * SUB, SUB), :] * window[first : first + steps]
        total = term if total is None else total + term
    return total


def featurize_kernel(
    position_ref, streams_ref, taps_in_ref, residue_ref, decay_in_ref, halo_ref, grad_in_ref,
    qf_ref, kf_ref, vf_ref, local_ref, grad_copy_ref, message_ref, taps_ref, scale_ref, decay_ref,
    wide_ref, feat_ref, grad_vmem, sems,
):
    grad_in = pltpu.make_async_copy(grad_in_ref, grad_vmem, sems.at[4])
    grad_in.start()
    tokens = streams_ref.shape[1]
    _, taps, _ = taps_in_ref.shape
    rim = taps - 1
    modes = decay_in_ref.shape[0]
    held = halo_ref.shape[0] // 3
    decays = decay_in_ref[...]
    scatter_tokens(decay_ref, decays, 0)
    scatter_tokens(scale_ref, residue_ref[...] * jnp.sqrt(decays), 0)
    for stream in range(3):
        scatter_tokens(taps_ref, taps_in_ref[stream], stream * taps)
        behind = halo_ref[stream * held : (stream + 1) * held, :].astype(F32)
        scatter_tokens(wide_ref.at[stream], behind[held - rim :], 0)
    batch = 2 * STEP

    def place(number):
        first = pl.multiple_of(number * batch, batch)
        for stream in range(3):
            value = streams_ref[stream, pl.ds(first, batch), :].astype(F32)
            scatter_tokens(wide_ref.at[stream], value, rim + first)

    place(0)

    def body(number, carry):
        windows = [
            as_tiles(
                wide_ref[
                    stream,
                    pl.ds(pl.multiple_of(number * batch * SUB, SUB), (batch + rim) * SUB),
                    :,
                ]
            )
            for stream in range(3)
        ]
        place(jnp.minimum(number + 1, tokens // batch - 1))
        for half in range(2):
            rows = pl.ds(pl.multiple_of((number * 2 + half) * STEP * SUB, SUB), STEP * SUB)
            feats = []
            for stream in range(3):
                window = windows[stream][half * STEP : half * STEP + STEP + rim]
                feats.append(filtered(window, taps_ref, stream, taps, STEP, True))
                feat_ref[stream, rows, :] = as_rows(feats[-1])
            feat_ref[3, rows, :] = as_rows(round16(feats[1] * feats[2]))
        return carry

    lax.fori_loop(0, tokens // batch, body, 0)
    grad_in.wait()
    copies = start_all(
        [
            pltpu.make_async_copy(source, target, sems.at[number])
            for number, (source, target) in enumerate(
                (
                    (feat_ref.at[0], qf_ref),
                    (feat_ref.at[1], kf_ref),
                    (feat_ref.at[2], vf_ref),
                    (grad_vmem, grad_copy_ref),
                )
            )
        ]
    )
    local_vmem = wide_ref.at[0, pl.ds(0, tokens * SUB), :]
    states = local_conv(feat_ref.at[3], decay_ref, scale_ref, local_vmem, False)
    copies += start_all([pltpu.make_async_copy(local_vmem, local_ref, sems.at[4])])
    write_messages(message_ref, states, decay_ref, position_ref, tokens, 1)
    wait_all(copies)


def scales_of(scale_ref):
    return [scale_ref[mode_rows(n), :] for n in range(scale_ref.shape[0] // SUB)]


def local_conv(signal_ref, decay_ref, scale_ref, out_ref, reverse):
    tokens = signal_ref.shape[0] // SUB
    factors = fades(decay_ref, 1.0)
    scales = scales_of(scale_ref)

    def body(step, states):
        for inner in range(STEP):
            token = step * STEP + inner
            token = tokens - 1 - token if reverse else token
            u = tile(signal_ref, token)
            states = [factor * state + u for factor, state in zip(factors, states)]
            out_ref[pl.ds(pl.multiple_of(token * SUB, SUB), SUB), :] = tree_sum(
                [scale * state for scale, state in zip(scales, states)]
            )
        return states

    return lax.fori_loop(0, tokens // STEP, body, zero_states(len(factors)))


def carried(out_ref, states, decay_ref, scale_ref, reverse, local_ref=None):
    tokens = out_ref.shape[0] // SUB
    factors = fades(decay_ref, 1.0)
    scaled = [scale * state for scale, state in zip(scales_of(scale_ref), states)]

    def body(step, scaled):
        for inner in range(STEP):
            token = step * STEP + inner
            token = tokens - 1 - token if reverse else token
            scaled = [factor * state for factor, state in zip(factors, scaled)]
            rows = pl.ds(pl.multiple_of(token * SUB, SUB), SUB)
            total = tree_sum(list(scaled))
            out_ref[rows, :] = total if local_ref is None else local_ref[rows, :] + total
        return scaled

    lax.fori_loop(0, tokens // STEP, body, scaled)


def project_kernel(
    index_ref, message_ref, decay_ref, scale_ref, _, qf_ref, local_ref, weight_ref, *refs
):
    rows_ref, feat_ref, local_vmem, gated_ref, held_ref, sent_ref, sems, out_sems = refs[-8:]
    conv_ref, gated_out_ref, *out_refs = refs[-10 - sent_ref.shape[0] : -8]
    parts, tokens, width = sent_ref.shape
    offset = index_ref.shape[0] - parts
    order = list(reversed(range(parts)))
    copies = [
        pltpu.make_async_copy(
            weight_ref.at[
                :, pl.ds(pl.multiple_of(index_ref[offset + part] * width, width), width)
            ],
            held_ref.at[part],
            sems.at[part],
        )
        for part in range(parts)
    ]
    outs = [
        pltpu.make_async_copy(sent_ref.at[part], out_refs[part], out_sems.at[part])
        for part in range(parts)
    ]
    local_copy = pltpu.make_async_copy(local_ref, local_vmem, sems.at[parts + 1])
    feat_copy = pltpu.make_async_copy(qf_ref, feat_ref, sems.at[parts])
    start_all([local_copy, feat_copy])
    start_all([copies[part] for part in order])
    carried(rows_ref, read_messages(message_ref), decay_ref, scale_ref, False)
    local_copy.wait()
    rows_ref[...] += local_vmem[...]
    conv_copy = pltpu.make_async_copy(rows_ref, conv_ref, sems.at[parts + 1])
    conv_copy.start()
    feat_copy.wait()
    gather_tokens(
        lambda group: group_rows(rows_ref, group, tokens) * group_rows(feat_ref, group, tokens),
        gated_ref,
    )
    gated_copy = pltpu.make_async_copy(gated_ref, gated_out_ref, out_sems.at[parts])
    gated_copy.start()
    for part in order:
        copies[part].wait()
        sent_ref[part] = jnp.dot(
            gated_ref[...], held_ref[part], preferred_element_type=F32
        ).astype(sent_ref.dtype)
        outs[part].start()
    wait_all([conv_copy, gated_copy] + outs)


def start_weights(index_ref, first, weight_ref, held_ref, sems):
    count, _, width = held_ref.shape
    return start_all(
        [
            pltpu.make_async_copy(
                weight_ref.at[
                    :, pl.ds(pl.multiple_of(index_ref[first + number] * width, width), width)
                ],
                held_ref.at[number],
                sems.at[number],
            )
            for number in range(count)
        ]
    )


def back_products(weights, piece_refs, turned_ref, held_ref, total_ref, before_ref):
    for number, ref in enumerate(piece_refs):
        turned_ref[number] = ref[...].T
    for number in range(len(piece_refs)):
        weights[number].wait()
        product = jnp.dot(held_ref[number], turned_ref[number], preferred_element_type=F32)
        earlier = before_ref if number == 0 else total_ref
        total_ref[...] = product if earlier is None else earlier[...] + product


def middle_kernel(index_ref, weight_ref, *refs):
    *piece_refs, total_ref, piece_vmem, turned_ref, held_ref, sems, piece_sems = refs
    pieces = start_all(
        [
            pltpu.make_async_copy(ref, piece_vmem.at[number], piece_sems.at[number])
            for number, ref in enumerate(piece_refs)
        ]
    )
    weights = start_weights(index_ref, 0, weight_ref, held_ref, sems)
    wait_all(pieces)
    held = [piece_vmem.at[number] for number in range(len(piece_refs))]
    back_products(weights, held, turned_ref, held_ref, total_ref, None)


def back_last_kernel(
    index_ref, position_ref, base_ref, decay_ref, weight_ref, qf_ref, kf_ref, vf_ref, conv_ref,
    *refs, rim,
):
    (
        *piece_refs, back_query_ref, mixed_ref, message_ref, ahead_ref,
        turned_ref, total_ref, rows_ref, feat_ref, conv_vmem, held_ref, sems, own_sems,
    ) = refs
    tokens = total_ref.shape[1]
    heads = pl.ds(0, rim * SUB)
    weights = start_weights(
        index_ref, index_ref.shape[0] - len(piece_refs), weight_ref, held_ref, sems
    )
    copies = start_all(
        [
            pltpu.make_async_copy(qf_ref, feat_ref, own_sems.at[0]),
            pltpu.make_async_copy(conv_ref, conv_vmem, own_sems.at[1]),
            pltpu.make_async_copy(kf_ref.at[heads, :], ahead_ref.at[2], own_sems.at[2]),
            pltpu.make_async_copy(vf_ref.at[heads, :], ahead_ref.at[3], own_sems.at[3]),
        ]
    )
    back_products(weights, piece_refs, turned_ref, held_ref, total_ref, base_ref)
    scatter_tokens(rows_ref, total_ref[...].T, 0)
    wait_all(copies)
    mixed_ref[...] = round16(rows_ref[...] * feat_ref[...])
    rows_ref[...] = round16(rows_ref[...] * conv_vmem[...])
    out = pltpu.make_async_copy(rows_ref, back_query_ref, own_sems.at[4])
    out.start()
    ahead_ref[0] = rows_ref[: rim * SUB, :]
    ahead_ref[1] = mixed_ref[: rim * SUB, :]
    modes = decay_ref.shape[0] // SUB
    states = advance_states(
        mixed_ref, fades(decay_ref, 1.0), zero_states(modes), 0, tokens, True
    )
    write_messages(message_ref, states, decay_ref, position_ref, tokens, -1)
    out.wait()


def spread_back(wide_ref, taps_ref, stream, taps, rows_ref, out_ref):
    batch = 2 * STEP
    batches = out_ref.shape[0] // batch

    def bring(number):
        first = pl.multiple_of(number * batch, batch)
        for group in range(out_ref.shape[1] // LANES):
            out_ref[pl.ds(first, batch), group * LANES : (group + 1) * LANES] = rows_ref[
                pl.ds(first * SUB + group, batch, stride=SUB), :
            ].astype(out_ref.dtype)

    def filter_batch(number):
        first = pl.multiple_of(number * batch * SUB, SUB)
        window = as_tiles(wide_ref[pl.ds(first, (batch + taps - 1) * SUB), :])
        rows_ref[pl.ds(first, batch * SUB), :] = as_rows(
            filtered(window, taps_ref, stream, taps, batch, False)
        )

    filter_batch(0)

    def body(number, carry):
        bring(number - 1)
        filter_batch(number)
        return carry

    lax.fori_loop(1, batches, body, 0)
    bring(batches - 1)


def back_local_kernel(
    index_ref, signal_ref, decay_ref, scale_ref, taps_ref, query_ref, gated_ref, weight_ref,
    local_ref, gq_ref, own_ref,
    wide_ref, rows_ref, out_vmem, gated_vmem, held_ref, own_vmem, sem, sems, *, taps,
):
    gated = pltpu.make_async_copy(gated_ref, gated_vmem, sems.at[1])
    gated.start()
    weights = start_weights(index_ref, 0, weight_ref, held_ref, sems)
    inside = query_ref.shape[0]
    copy = pltpu.make_async_copy(query_ref, wide_ref.at[pl.ds(0, inside), :], sem)
    copy.start()
    local_conv(signal_ref, decay_ref, scale_ref, local_ref, True)
    copy.wait()
    rest = (taps - 1) * SUB
    wide_ref[pl.ds(inside, rest), :] = jnp.zeros((rest, LANES), F32)
    spread_back(wide_ref, taps_ref, 0, taps, rows_ref, out_vmem)
    out = pltpu.make_async_copy(out_vmem, gq_ref, sem)
    out.start()
    wait_all([gated, *weights])
    own_vmem[...] = jnp.dot(
        gated_vmem[...], held_ref[0], preferred_element_type=F32
    ).astype(own_vmem.dtype)
    own = pltpu.make_async_copy(own_vmem, own_ref, sems.at[0])
    own.start()
    wait_all([out, own])


def finish_kernel(
    message_ref, local_ref, decay_ref, scale_ref, taps_ref, ahead_ref, query_ref, kf_ref, vf_ref,
    *refs, taps,
):
    (
        *part_refs, _, gq_ref, gk_ref, gv_ref, projected_ref,
        total_ref, feat_ref, query_vmem, wide_ref, rows_ref, tail_ref, out_vmem, parts_vmem,
        sems, part_sems,
    ) = refs
    tokens = gk_ref.shape[0]
    tail = tail_ref.shape[0]
    rim = taps - 1
    inside = pl.ds(0, tokens * SUB)
    copies = start_all(
        [
            pltpu.make_async_copy(
                query_ref.at[pl.ds((tokens - tail) * SUB, tail * SUB), :],
                query_vmem.at[pl.ds(0, tail * SUB), :],
                sems.at[0],
            ),
            pltpu.make_async_copy(vf_ref, feat_ref.at[0], sems.at[1]),
            pltpu.make_async_copy(kf_ref, feat_ref.at[1], sems.at[2]),
        ]
    )
    parts = start_all(
        [
            pltpu.make_async_copy(ref, parts_vmem.at[number], part_sems.at[number])
            for number, ref in enumerate(part_refs)
        ]
    )
    states = read_messages(message_ref)
    carried(total_ref, states, decay_ref, scale_ref, True, local_ref)
    growth = fades(decay_ref, -1.0)
    scales = scales_of(scale_ref)
    for ahead in range(rim):
        rows = pl.ds((tokens + ahead) * SUB, SUB)
        theirs = pl.ds(ahead * SUB, SUB)
        grad_conv = tree_sum([scale * state for scale, state in zip(scales, states)])
        query_vmem[pl.ds((tail + ahead) * SUB, SUB), :] = ahead_ref[0, theirs, :]
        wide_ref[0, rows, :] = round16(grad_conv * ahead_ref[3, theirs, :])
        wide_ref[1, rows, :] = round16(grad_conv * ahead_ref[2, theirs, :])
        arrived = ahead_ref[1, theirs, :]
        states = [(state - arrived) * grow for state, grow in zip(states, growth)]
    copies[0].wait()
    spread_back(query_vmem, taps_ref, 0, taps, rows_ref, tail_ref)
    outs = [
        pltpu.make_async_copy(tail_ref, gq_ref.at[pl.ds(tokens - tail, tail), :], sems.at[0])
    ]
    wait_all(parts)
    out_vmem[2] = tree_sum(
        [parts_vmem[number].astype(F32) for number in range(len(part_refs))]
    ).astype(out_vmem.dtype)
    outs.append(pltpu.make_async_copy(out_vmem.at[2], projected_ref, sems.at[3]))
    start_all(outs)
    for stream, out_ref in enumerate((gk_ref, gv_ref)):
        copies[1 + stream].wait()
        wide_ref[stream, inside, :] = round16(total_ref[...] * feat_ref[stream])
        spread_back(
            wide_ref.at[stream], taps_ref, 1 + stream, taps, rows_ref, out_vmem.at[stream]
        )
        outs.append(pltpu.make_async_copy(out_vmem.at[stream], out_ref, sems.at[1 + stream]))
        outs[-1].start()
    wait_all(outs)


IN_VMEM = pl.BlockSpec(memory_space=pltpu.VMEM)
IN_SMEM = pl.BlockSpec(memory_space=pltpu.SMEM)
IN_HBM = pl.BlockSpec(memory_space=pltpu.HBM)
HBM_RATE = 3.5e6


def in_hbm(shape, kind):
    return pltpu.HBM(shape, kind)


def call(kernel, outs, args, specs, scratch, name, micros, mebibytes, aliases=None):
    args = [
        pltpu.with_memory_space_constraint(arg, pltpu.HBM) if spec is IN_HBM else arg
        for arg, spec in zip(args, specs)
    ]
    held = [isinstance(out, tuple) for out in outs]
    return pl.pallas_call(
        kernel,
        out_shape=[jax.ShapeDtypeStruct(*out) if own else out for own, out in zip(held, outs)],
        in_specs=specs,
        out_specs=[IN_VMEM if own else IN_HBM for own in held],
        scratch_shapes=scratch,
        compiler_params=pltpu.CompilerParams(vmem_limit_bytes=mebibytes * 1024 * 1024),
        cost_estimate=pl.CostEstimate(
            flops=0, bytes_accessed=int(micros * HBM_RATE), transcendentals=0
        ),
        name=name,
        input_output_aliases=aliases or {},
    )(*args)


def shift(value, axis, steps):
    count = lax.axis_size(axis)
    pairs = [(s, s + steps) for s in range(count) if 0 <= s + steps < count]
    return lax.ppermute(value, axis, pairs)


def exchange(value, axis, mask):
    count = lax.axis_size(axis)
    return lax.ppermute(value, axis, [(s, s ^ mask) for s in range(count)])


def shards(query_in, key_in, value_in, short_taps, residues, decays, out_weight, out_grad):
    tokens, channels = query_in.shape
    taps = short_taps.shape[0]
    rim = taps - 1
    modes = decays.shape[1]
    blocks = lax.axis_size("ctx")
    fans = lax.axis_size("ch")
    position = lax.axis_index("ctx")[None].astype(jnp.int32)
    tile_shape = (tokens * SUB, LANES)
    mode_shape = (modes * SUB, LANES)
    message_shape = (blocks,) + mode_shape
    streams = (query_in, key_in, value_in)
    rim_rows = 16

    tap_rows = jnp.transpose(short_taps, (1, 0, 2))
    halo, narrow, taps_vmem, residues_vmem, decays_vmem = call(
        rim_kernel,
        [
            ((3 * rim_rows, channels), BF16),
            ((3, tokens, channels), BF16),
            ((3, taps, channels), F32),
            ((modes, channels), F32),
            ((modes, channels), F32),
        ],
        streams + (tap_rows, residues.T, decays.T), [IN_HBM] * 6,
        [pltpu.SemaphoreType.DMA((9,))], "rim", 1.2, 2,
    )
    halo, out_grad = lax.optimization_barrier((halo, out_grad))
    halo = shift(halo, "ctx", 1)
    if fans == 4:
        order = lax.axis_index("ch") ^ jnp.arange(fans, dtype=jnp.int32)
        pieces = [out_grad] + [exchange(out_grad, "ch", mask) for mask in range(1, fans - 1)]
    else:
        order = jnp.arange(fans, dtype=jnp.int32)
        everyone = lax.all_gather(out_grad, "ch", axis=0, tiled=False)
        pieces = [everyone[number] for number in range(fans)]
    tile = pltpu.VMEM(tile_shape, F32)
    wide_rows = (tokens + rim) * SUB

    (
        query_feat, key_feat, value_feat, local, grad_copy, messages,
        tap_tiles, scale_tiles, decay_tiles,
    ) = call(
        featurize_kernel,
        [in_hbm(tile_shape, F32)] * 4
        + [in_hbm((tokens, channels), BF16), (message_shape, BF16)]
        + [((3 * taps * SUB, LANES), F32), (mode_shape, F32), (mode_shape, F32)],
        (position, narrow, taps_vmem, residues_vmem, decays_vmem, halo, out_grad),
        [IN_SMEM] + [IN_VMEM] * 5 + [IN_HBM],
        [
            pltpu.VMEM((3, wide_rows, LANES), F32),
            pltpu.VMEM((4,) + tile_shape, F32),
            pltpu.VMEM((tokens, channels), BF16),
            pltpu.SemaphoreType.DMA((5,)),
        ],
        "featurize", 6.0, 10,
    )
    if fans == 4:
        pieces.append(exchange(grad_copy, "ch", fans - 1))
    arrived = lax.all_to_all(messages, "ctx", split_axis=0, concat_axis=0, tiled=True)

    def weight_scratch(count):
        return [
            pltpu.VMEM((count, channels, channels), BF16),
            pltpu.SemaphoreType.DMA((count,)),
        ]

    early = fans - 1
    (base,) = call(
        middle_kernel,
        [((channels, tokens), F32)],
        (order, out_weight, *pieces[:early]),
        [IN_SMEM] + [IN_HBM] * (1 + early),
        [
            pltpu.VMEM((early, tokens, channels), BF16),
            pltpu.VMEM((early, channels, tokens), BF16),
        ]
        + weight_scratch(early)
        + [pltpu.SemaphoreType.DMA((early,))],
        "middle", 6.0, 11,
    )
    sent = fans - 1 if fans == 4 else fans
    conv_out, gated, *partial_sums = call(
        project_kernel,
        [in_hbm(tile_shape, F32)] + [in_hbm((tokens, channels), BF16)] * (1 + sent),
        (
            order, arrived, decay_tiles, scale_tiles, base, query_feat, local, out_weight,
            *pieces[1:early],
        ),
        [IN_SMEM] + [IN_VMEM] * 4 + [IN_HBM] * (2 + early),
        [
            tile,
            tile,
            tile,
            pltpu.VMEM((tokens, channels), BF16),
            pltpu.VMEM((sent, channels, channels), BF16),
            pltpu.VMEM((sent, tokens, channels), BF16),
            pltpu.SemaphoreType.DMA((sent + 2,)),
            pltpu.SemaphoreType.DMA((sent + 1,)),
        ],
        "project", 7.0, 16,
    )
    if fans == 4:
        parts = [exchange(part, "ch", 1 + number) for number, part in enumerate(partial_sums)]
    else:
        parts = lax.all_to_all(
            jnp.stack(partial_sums), "ch", split_axis=0, concat_axis=0, tiled=True
        )
        parts = [parts[number] for number in range(fans)]
    back_query, grad_mixed, back_messages, ahead = call(
        functools.partial(back_last_kernel, rim=rim),
        [in_hbm(tile_shape, F32), (tile_shape, F32), (message_shape, BF16)]
        + [((4, rim * SUB, LANES), F32)],
        (
            order, position, base, decay_tiles, out_weight, query_feat, key_feat,
            value_feat, conv_out, *pieces[early:],
        ),
        [IN_SMEM] * 2 + [IN_VMEM] * 2 + [IN_HBM] * 5 + [IN_VMEM] * (fans - early),
        [
            pltpu.VMEM((fans - early, channels, tokens), BF16),
            pltpu.VMEM((channels, tokens), F32),
            tile,
            tile,
            tile,
        ]
        + weight_scratch(fans - early)
        + [pltpu.SemaphoreType.DMA((5,))],
        "back_last", 6.0, 9,
    )
    back_arrived = lax.all_to_all(back_messages, "ctx", split_axis=0, concat_axis=0, tiled=True)
    ahead = shift(ahead, "ctx", -1)
    back_local, grad_query, own_part = call(
        functools.partial(back_local_kernel, taps=taps),
        [(tile_shape, F32)] + [in_hbm((tokens, channels), BF16)] * 2,
        (order, grad_mixed, decay_tiles, scale_tiles, tap_tiles, back_query, gated, out_weight),
        [IN_SMEM] + [IN_VMEM] * 4 + [IN_HBM] * 3,
        [
            pltpu.VMEM((wide_rows, LANES), F32),
            tile,
            pltpu.VMEM((tokens, channels), BF16),
            pltpu.VMEM((tokens, channels), BF16),
            pltpu.VMEM((1, channels, channels), BF16),
            pltpu.VMEM((tokens, channels), BF16),
            pltpu.SemaphoreType.DMA,
            pltpu.SemaphoreType.DMA((2,)),
        ],
        "back_local", 5.0, 9,
    )
    if fans == 4:
        parts = [own_part] + parts
    tail = 16
    grad_query, grad_key, grad_value, projected = call(
        functools.partial(finish_kernel, taps=taps),
        [in_hbm((tokens, channels), BF16)] * 4,
        (
            back_arrived, back_local, decay_tiles, scale_tiles, tap_tiles, ahead, back_query,
            key_feat, value_feat, *parts, grad_query,
        ),
        [IN_VMEM] * 6 + [IN_HBM] * (4 + fans),
        [
            tile,
            pltpu.VMEM((2,) + tile_shape, F32),
            pltpu.VMEM(((tail + rim) * SUB, LANES), F32),
            pltpu.VMEM((2, wide_rows, LANES), F32),
            tile,
            pltpu.VMEM((tail, channels), BF16),
            pltpu.VMEM((3, tokens, channels), BF16),
            pltpu.VMEM((fans, tokens, channels), BF16),
            pltpu.SemaphoreType.DMA((4,)),
            pltpu.SemaphoreType.DMA((fans,)),
        ],
        "finish", 5.0, 12,
        {9 + fans: 0},
    )
    return (projected, grad_query, grad_key, grad_value)


def solution(mesh):
    in_specs = (
        P("ctx", "ch"),
        P("ctx", "ch"),
        P("ctx", "ch"),
        P(None, None, "ch"),
        P("ch", None),
        P("ch", None),
        P("ch", None),
        P("ctx", "ch"),
    )
    out_specs = (P("ctx", "ch"), P("ctx", "ch"), P("ctx", "ch"), P("ctx", "ch"))
    return jax.shard_map(shards, mesh=mesh, in_specs=in_specs, out_specs=out_specs, check_vma=False)
```
